32 devices in a mesh: space: 8 (over z, y), depth: 4 (over x, core).
Axes of the slice: x: 2, y: 2, z: 4, core: 2. Of those that a mesh axis runs over, the one named last changes fastest.
Arguments:
- features: bfloat16 [8, 4, 512, 128], P('space', 'depth'), may hold values from -6 to 6
- cotangent: bfloat16 [8, 4, 512, 128], P('space', 'depth'), may hold values from -6 to 6
- first_kernel: bfloat16 [27, 128, 128], replicated, may hold values from -0.109375 to 0.109375
- second_kernel: bfloat16 [27, 128, 128], replicated, may hold values from -0.109375 to 0.109375
- slot_tile: int32 [8, 4], P('space'), may hold values from 0 to 3, as said below
- slot_used: int32 [8, 4], P('space'), may hold values from 0 to 1, as said below
Outputs:
- input_grad: bfloat16 [8, 4, 512, 128], P('space', 'depth')
- first_kernel_grad: float32 [442368], P(('space', 'depth'))
- second_kernel_grad: float32 [442368], P(('space', 'depth'))
The draws below stay inside these ranges and needn't reach their ends.
Inputs may be any that keep to these rules, and one draw needn't show every extreme that they name: `slot_tile`: in each column the used slots hold distinct z positions that form one unbroken run; in some column every slot is used. `slot_used`: every column has at least one used slot.
All inputs are finite; a program needn't handle non-finite values.
Results may differ from the reference program's by a relative error of at most 0.006.
Values may be sent and summed in bfloat16 or wider, within the bound.
No kernel may reach another device: no remote copies, remote signals or barrier semaphores. Data moves between devices by JAX's collectives and lax.ppermute only.
A program may use at most 64 MiB of HBM per device.

```python
import jax
import jax.numpy as jnp
from jax import lax

C = 128
TE = 8
GY = 8
VOX = 512
ZT = 4
COLUMNS = 8
GX = 1


def column_layout(key):
    base_key = jax.random.fold_in(key, 7)
    sub_keys = jax.random.split(base_key, 4)
    lengths = jax.random.randint(sub_keys[0], (COLUMNS,), 1, ZT + 1)
    forced = jax.random.randint(sub_keys[1], (), 0, COLUMNS)
    lengths = jnp.where(jnp.arange(COLUMNS) == forced, ZT, lengths)
    starts = jax.random.randint(sub_keys[2], (COLUMNS,), 0, ZT + 1 - lengths)

    def column_order(column_key):
        return jax.random.permutation(column_key, ZT)
    ranking = jax.vmap(column_order)(jax.random.split(sub_keys[3], COLUMNS))
    in_use = (ranking < lengths[:, None]).astype(jnp.int32)
    tile_spots = ((starts[:, None] + ranking) % ZT).astype(jnp.int32)
    return (tile_spots, in_use)


def draw_slot_tile(key, part):
    return column_layout(key)[0]


def draw_slot_used(key, part):
    return column_layout(key)[1]


def shard_levels(stream_key, shape, pieces, low, high):
    def one(axis_at, shards_of):
        heights = jax.random.uniform(jax.random.fold_in(jax.random.fold_in(stream_key, 6), axis_at), (shards_of,), jnp.float32, low / len(pieces), high / len(pieces))
        return jnp.repeat(jnp.exp(heights), shape[axis_at] // shards_of).reshape((-1,) + (1,) * (len(shape) - axis_at - 1))

    factor_of = one(*pieces[0])
    for cut in pieces[1:]:
        factor_of = factor_of * one(*cut)
    return factor_of


def normal_values(rng, shape, scale, bound, cuts=(), kind=jnp.bfloat16):
    drawn = scale * jax.random.normal(rng, shape, jnp.float32)
    if cuts:
        drawn = drawn * shard_levels(rng, shape, cuts, -0.22, 0.18)
    return jnp.clip(drawn, -bound, bound).astype(kind)


def setup_inputs(seed: int = 0) -> dict:
    streams_of = jax.random.split(jax.random.key(seed), 7)
    return {
        "features": normal_values(streams_of[0], (COLUMNS, ZT, VOX, C), 1.0, 6.0, ((0, 8), (1, 4))),
        "cotangent": normal_values(streams_of[1], (COLUMNS, ZT, VOX, C), 1.0, 6.0, ((0, 8), (1, 4))),
        "first_kernel": normal_values(streams_of[2], (27, C, C), (27 * C) ** -0.5, 0.109375),
        "second_kernel": normal_values(streams_of[3], (27, C, C), (27 * C) ** -0.5, 0.109375),
        "slot_tile": draw_slot_tile(jax.random.fold_in(streams_of[6], 71), 0),
        "slot_used": draw_slot_used(jax.random.fold_in(streams_of[6], 71), 0),
    }


SLOPE_COEF = 0.7978845608028654
CUBIC_COEF = 0.044715

def gelu_pair(values):
    inner_arg = SLOPE_COEF * (values + CUBIC_COEF * values * values * values)
    tangent = jnp.tanh(inner_arg)
    output = 0.5 * values * (1.0 + tangent)
    derivative = 0.5 * (1.0 + tangent) + 0.5 * values * (1.0 - tangent * tangent) * SLOPE_COEF * (1.0 + 3.0 * CUBIC_COEF * values * values)
    return (output, derivative)

def columns_to_volume(dense):
    width = dense.shape[-1]
    shaped = dense.reshape(GX, GY, ZT, TE, TE, TE, width)
    return jnp.transpose(shaped, (2, 3, 0, 4, 1, 5, 6)).reshape(ZT * TE, GX * TE, GY * TE, width)

def volume_to_columns(volume):
    width = volume.shape[-1]
    shaped = volume.reshape(ZT, TE, GX, TE, GY, TE, width)
    return jnp.transpose(shaped, (2, 4, 0, 1, 3, 5, 6)).reshape(COLUMNS, ZT, VOX, width)

def convolve(volume, kernel):
    weights = kernel.astype(jnp.float32).reshape(3, 3, 3, kernel.shape[1], kernel.shape[2])
    result = lax.conv_general_dilated(volume.astype(jnp.float32)[None], weights, (1, 1, 1), ((1, 1), (1, 1), (1, 1)), dimension_numbers=('NDHWC', 'DHWIO', 'NDHWC'), precision=lax.Precision.HIGHEST)
    return result[0]

def convolve_back(volume, kernel):
    weights = kernel.astype(jnp.float32).reshape(3, 3, 3, kernel.shape[1], kernel.shape[2])
    flipped = jnp.transpose(weights[::-1, ::-1, ::-1], (0, 1, 2, 4, 3))
    result = lax.conv_general_dilated(volume.astype(jnp.float32)[None], flipped, (1, 1, 1), ((1, 1), (1, 1), (1, 1)), dimension_numbers=('NDHWC', 'DHWIO', 'NDHWC'), precision=lax.Precision.HIGHEST)
    return result[0]

def kernel_grad(source, delta):
    padded = jnp.pad(source.astype(jnp.float32), ((1, 1), (1, 1), (1, 1), (0, 0)))
    delta_f = delta.astype(jnp.float32)

    def per_tap(kernel_tap):
        z_step = (kernel_tap // 9).astype(jnp.int32)
        x_step = (kernel_tap // 3 % 3).astype(jnp.int32)
        y_step = (kernel_tap % 3).astype(jnp.int32)
        zero_idx = jnp.zeros((), jnp.int32)
        window = lax.dynamic_slice(padded, (z_step, x_step, y_step, zero_idx), delta_f.shape[:3] + (padded.shape[3],))
        return jnp.einsum('zxyi,zxyo->io', window, delta_f, precision=lax.Precision.HIGHEST)
    summed = lax.map(per_tap, jnp.arange(27).astype(jnp.int32))
    return (summed * (1.0 / VOX)).reshape(-1)

def reference(features, cotangent, first_kernel, second_kernel, slot_tile, slot_used):
    positions = jnp.arange(ZT).astype(jnp.int32)
    placement = ((slot_tile[:, None, :] == positions[None, :, None]) & (slot_used[:, None, :] == 1)).astype(jnp.float32)
    occupancy = lax.optimization_barrier(jnp.sum(placement, axis=2))
    occupied = columns_to_volume(jnp.broadcast_to(occupancy[:, :, None, None], (COLUMNS, ZT, VOX, 1)))
    source = columns_to_volume(jnp.einsum('ctj,cjvk->ctvk', placement, features.astype(jnp.float32))).astype(jnp.bfloat16)
    upstream = columns_to_volume(jnp.einsum('ctj,cjvk->ctvk', placement, cotangent.astype(jnp.float32))).astype(jnp.bfloat16)
    pre_one = convolve(source, first_kernel)
    act_value, slope_one = gelu_pair(pre_one)
    act_one = (act_value * occupied).astype(jnp.bfloat16)
    pre_two = convolve(act_one, second_kernel)
    slope_two = gelu_pair(pre_two)[1]
    delta_two = (upstream.astype(jnp.float32) * slope_two * occupied).astype(jnp.bfloat16)
    delta_one = (convolve_back(delta_two, second_kernel) * slope_one * occupied).astype(jnp.bfloat16)
    back_zero = volume_to_columns(convolve_back(delta_one, first_kernel))
    input_grad = jnp.einsum('ctj,ctvk->cjvk', placement, back_zero).astype(jnp.bfloat16)
    first_kernel_grad = kernel_grad(source, delta_one)
    second_kernel_grad = kernel_grad(act_one, delta_two)
    return (input_grad, first_kernel_grad, second_kernel_grad)
```

```python
import jax
import jax.numpy as jnp
from jax import lax
from jax.experimental import pallas as pl
from jax.experimental.pallas import tpu as pltpu
from jax.sharding import PartitionSpec as P

TE = 8
GY = 8


SLOPE_COEF = 0.7978845608028654
CUBIC_COEF = 0.044715


def from_behind(block, axis, distance):
    devices = range(lax.axis_size(axis))
    route = [(i - distance, i) for i in devices if i - distance in devices]
    return lax.ppermute(block, axis, route)


def gelu_pair(values):
    inner_arg = SLOPE_COEF * (values + CUBIC_COEF * values * values * values)
    tangent = jnp.tanh(inner_arg)
    output = 0.5 * values * (1.0 + tangent)
    derivative = 0.5 * (1.0 + tangent) + 0.5 * values * (1.0 - tangent * tangent) * SLOPE_COEF * (
        1.0 + 3.0 * CUBIC_COEF * values * values
    )
    return (output, derivative)


def gelu_slope(values):
    inner_arg = SLOPE_COEF * (values + CUBIC_COEF * values * values * values)
    tangent = jnp.tanh(inner_arg)
    return 0.5 * (1.0 + tangent) + 0.5 * values * (1.0 - tangent * tangent) * SLOPE_COEF * (
        1.0 + 3.0 * CUBIC_COEF * values * values
    )


def place_matrix(slot_tile, slot_used, position_count):
    positions = jnp.arange(position_count, dtype=jnp.int32)
    matches = (slot_tile[0][None, :] == positions[:, None]) & (slot_used[0][None, :] == 1)
    return matches.astype(jnp.bfloat16)


def dense_column(tile_rows, placement):
    summed = jnp.einsum(
        "tj,jvc->tvc",
        placement,
        lax.all_gather(tile_rows, "depth", axis=0, tiled=True),
        preferred_element_type=jnp.float32,
    )
    return summed.astype(jnp.bfloat16).reshape(-1, TE, TE, summed.shape[-1])


def extend_sides(own_block, move_face, space_index):
    y_coord = space_index % GY
    below = move_face(own_block[:, :, -1:, :], 1) * (y_coord > 0).astype(own_block.dtype)
    above = move_face(own_block[:, :, :1, :], -1) * (y_coord < GY - 1).astype(own_block.dtype)
    widened = jnp.concatenate([below, own_block, above], axis=2)
    behind = move_face(widened[:, -1:, :, :], GY)
    ahead = move_face(widened[:, :1, :, :], -GY)
    return jnp.concatenate([behind, widened, ahead], axis=1)


def pad_depth(own_block):
    return jnp.pad(own_block, ((1, 1), (0, 0), (0, 0), (0, 0)))


def windows_at(padded, positions):

    def one_window(z_index):
        return lax.dynamic_slice_in_dim(padded, z_index * TE, TE + 2, 0)

    return jax.vmap(one_window)(positions)


def unfold(windows, flipped):
    pieces = []
    for kernel_tap in range(27):
        z_step, x_step, y_step = (kernel_tap // 9, kernel_tap // 3 % 3, kernel_tap % 3)
        if flipped:
            z_step, x_step, y_step = (2 - z_step, 2 - x_step, 2 - y_step)
        pieces.append(
            windows[:, z_step : z_step + TE, x_step : x_step + TE, y_step : y_step + TE, :]
        )
    stacked = jnp.concatenate(pieces, axis=-1)
    return stacked.reshape(-1, stacked.shape[-1])


def tile_sum(columns, delta):
    return lax.dot_general(
        columns, delta, (((0,), (0,)), ((), ())), preferred_element_type=jnp.float32
    )


def on_device_wide(features, cotangent, first_kernel, second_kernel, slot_tile, slot_used):
    depth_index = lax.axis_index("depth")
    space_index = lax.axis_index("space")
    slot_count = features.shape[1]
    voxels = features.shape[2]
    channels = features.shape[3]
    position_count = slot_tile.shape[1]
    placement = place_matrix(slot_tile, slot_used, position_count)
    own_first = depth_index * slot_count
    own_tiles = lax.dynamic_slice_in_dim(slot_tile[0], own_first, slot_count, 0)
    own_used = lax.dynamic_slice_in_dim(slot_used[0], own_first, slot_count, 0).astype(jnp.float32)
    feature_slots = features[0]
    upstream_slots = cotangent[0]

    def column_move(face, offset):
        return from_behind(face, "space", offset)

    def halo_of(tile_rows):
        column = dense_column(tile_rows.reshape(slot_count, voxels, channels), placement)
        return pad_depth(extend_sides(column, column_move, space_index))

    upstream = upstream_slots.reshape(-1, channels)
    source_column = halo_of(feature_slots)
    alive_rows = jnp.repeat(own_used, voxels)[:, None]
    forward_one = first_kernel.reshape(-1, channels)
    forward_two = second_kernel.reshape(-1, channels)
    backward_one = jnp.transpose(first_kernel, (0, 2, 1)).reshape(-1, channels)
    backward_two = jnp.transpose(second_kernel, (0, 2, 1)).reshape(-1, channels)
    source_cols = unfold(windows_at(source_column, own_tiles), False)
    pre_one = jnp.dot(source_cols, forward_one, preferred_element_type=jnp.float32)
    act_value, slope_one = gelu_pair(pre_one)
    act_one = (act_value * alive_rows).astype(jnp.bfloat16)
    act_cols = unfold(windows_at(halo_of(act_one), own_tiles), False)
    pre_two = jnp.dot(act_cols, forward_two, preferred_element_type=jnp.float32)
    slope_two = gelu_slope(pre_two)
    delta_two = (upstream.astype(jnp.float32) * slope_two * alive_rows).astype(jnp.bfloat16)
    second_grad = tile_sum(act_cols, delta_two).reshape(-1) * (1.0 / voxels)
    back_one = jnp.dot(
        unfold(windows_at(halo_of(delta_two), own_tiles), True),
        backward_two,
        preferred_element_type=jnp.float32,
    )
    delta_one = (back_one * slope_one * alive_rows).astype(jnp.bfloat16)
    first_grad = tile_sum(source_cols, delta_one).reshape(-1) * (1.0 / voxels)
    back_zero = jnp.dot(
        unfold(windows_at(halo_of(delta_one), own_tiles), True),
        backward_one,
        preferred_element_type=jnp.float32,
    )
    used_rows = jnp.repeat(own_used, voxels)[:, None]
    input_grad = (back_zero * used_rows).astype(jnp.bfloat16).reshape(features.shape)
    first_share, second_share = (
        lax.psum_scatter(first_grad, ("space", "depth"), scatter_dimension=0, tiled=True),
        lax.psum_scatter(second_grad, ("space", "depth"), scatter_dimension=0, tiled=True),
    )
    return (input_grad, first_share, second_share)


HALO = 4
BF = jnp.bfloat16
F32 = jnp.float32


class Region:
    def __init__(self, even, odd, z_size, y_size):
        self.even, self.odd, self.z_size, self.y_size = even, odd, z_size, y_size

    def planes(self, first):
        return (self.odd, (first - 1) // 2) if first % 2 else (self.even, first // 2)

    def store_row(self, y_pair, y_parity, column):
        z_size, width, channels = column.shape
        place = lax.broadcasted_iota(jnp.int32, column.shape, 1)
        before = jnp.where(place == 0, 0.0, pltpu.roll(column, 1, 1))
        after = jnp.where(place == width - 1, 0.0, pltpu.roll(column, width - 1, 1))
        wide = jnp.concatenate([before, column, after], axis=-1)
        self.even[:, y_pair, y_parity] = wide.reshape(z_size // 2, 2 * width, 3 * channels).astype(BF)
        if self.odd is not None:
            inner = wide[1:-1].reshape(z_size // 2 - 1, 2 * width, 3 * channels)
            self.odd[:, y_pair, y_parity] = inner.astype(BF)

    def tile_rows(self, z_first, y_first, lanes, lane_first, edge):
        ref, q_first = self.planes(z_first)
        parts = []
        for y_at in range(y_first, y_first + edge):
            part = ref[q_first : q_first + edge // 2, y_at // 2, y_at % 2, :, lane_first : lane_first + lanes]
            parts.append(part.reshape(-1, lanes))
        return jnp.concatenate(parts, axis=0)


def region_shapes(z_size, y_size, width, channels, with_odd):
    tail = (y_size // 2, 2, 2 * width, 3 * channels)
    shapes = [pltpu.VMEM((z_size // 2,) + tail, BF)]
    if with_odd:
        shapes.append(pltpu.VMEM((z_size // 2 - 1,) + tail, BF))
    return shapes


def convolve_region(region, weights, transposed, result):
    q_size, r_size = region.z_size // 2 - 1, region.y_size // 2 - 1
    channels = region.even.shape[-1] // 3
    pieces = []
    for z_tap in range(3):
        ref, q_first = region.planes(z_tap)
        for x_tap in range(3):
            for y_at in range(4):
                piece = ref[
                    q_first : q_first + q_size,
                    y_at // 2 : y_at // 2 + r_size,
                    y_at % 2,
                    :,
                    x_tap * channels : (x_tap + 1) * channels,
                ]
                pieces.append(piece.reshape(-1, channels))
    left = jnp.concatenate(pieces, axis=1)
    contract = (((1,), (1 if transposed else 0,)), ((), ()))
    product = lax.dot_general(left, weights[...], contract, preferred_element_type=F32)
    result[0:q_size, 0:r_size] = product.reshape(q_size, r_size, product.shape[0] // (q_size * r_size), -1)


def kernel_copies(kernel, weights, sems, transposed):
    channels = kernel.shape[-1]
    copies = []
    for z_tap in range(3):
        for x_tap in range(3):
            block = (z_tap * 3 + x_tap) * 4 * channels
            for parity in range(2):
                out = pl.ds(parity * channels, channels)
                if transposed:
                    for y_tap in range(3):
                        tap = (2 - z_tap) * 9 + (2 - x_tap) * 3 + 2 - y_tap
                        lanes = pl.ds(block + (parity + y_tap) * channels, channels)
                        copies.append((kernel.at[tap], weights.at[out, lanes]))
                else:
                    tap = z_tap * 9 + x_tap * 3
                    for y_tap in range(3):
                        rows = pl.ds(block + (parity + y_tap) * channels, channels)
                        copies.append((kernel.at[tap + y_tap], weights.at[rows, out]))
    return [pltpu.make_async_copy(a, b, sems.at[n]) for n, (a, b) in enumerate(copies)]


def clear_unused(weights, transposed):
    channels = min(weights.shape) // 2
    blank = jnp.zeros((channels, channels), BF)
    for block in range(9):
        for parity, y_at in ((0, 3), (1, 0)):
            inner = pl.ds((block * 4 + y_at) * channels, channels)
            out = pl.ds(parity * channels, channels)
            if transposed:
                weights[out, inner] = blank
            else:
                weights[inner, out] = blank


def place_slots(slots, codes, sources, volume, mask):
    raw, offset, stride, y_first, y_count, cls, lifted = sources
    for block in range(len(raw)):
        code = codes[cls, slots[block]]

        @pl.when(code > 0)
        def _():
            z_first = HALO + (code - 1) * TE
            rows = TE * TE * stride
            lifted[0:rows] = raw[block][offset : offset + rows].astype(F32)
            for z_at in range(TE):
                for y_at in range(y_count):
                    volume[z_first + z_at, y_first + y_at] = lifted[pl.ds(z_at * TE * stride + y_at, TE, stride=stride)]
            if mask is not None:
                mask[cls, pl.ds(z_first, TE)] = jnp.ones((TE,) + mask.shape[2:], F32)


def backward_kernel(block_count, packs_per, channels, tiles, codes, depth_at, *refs):
    own = refs[:block_count]
    rims = refs[block_count : 2 * block_count]
    first_kernel, second_kernel = refs[2 * block_count : 2 * block_count + 2]
    input_grad, grads = refs[2 * block_count + 2 : 2 * block_count + 4]
    rest = list(refs[2 * block_count + 4 :])

    def take():
        return rest.pop(0)

    volume, upstream, mask, lifted, result, grad_rows = (take() for _ in range(6))
    weights = [take() for _ in range(4)]
    sems = [take() for _ in range(4)]
    regions = []
    for number in range(tiles):
        halo = HALO - number
        group = []
        for layer in range(4):
            size = TE + 2 * (halo - layer)
            even = take()
            odd = take() if size > TE else None
            group.append(Region(even, odd, size, size))
        regions.append(group)
    slopes = [take() for _ in range(tiles)]

    copies = [
        kernel_copies(first_kernel, weights[0], sems[0], False),
        kernel_copies(second_kernel, weights[1], sems[1], False),
        kernel_copies(second_kernel, weights[2], sems[2], True),
        kernel_copies(first_kernel, weights[3], sems[3], True),
    ]
    for group in copies:
        for copy in group:
            copy.start()
    for at in range(4):
        clear_unused(weights[at], at > 1)

    me = depth_at[0]
    slots = [me ^ block for block in range(block_count)]
    voxels = TE * TE * TE
    volume[...] = jnp.zeros_like(volume)
    upstream[...] = jnp.zeros_like(upstream)
    mask[...] = jnp.zeros_like(mask)
    face, thin = voxels // 2, voxels // 4
    rim_size = face + thin + 16
    for cls, raw, offset, y_first in ((0, rims, 0, 0), (2, rims, rim_size, HALO + TE)):
        place_slots(slots, codes, (raw, offset, HALO, y_first, HALO, cls, lifted), volume, mask)
        place_slots(slots, codes, (raw, offset + face, 2, y_first if cls else 2, 2, cls, lifted), upstream, None)
    place_slots(slots, codes, (own, 0, TE, HALO, TE, 1, lifted), volume, mask)
    place_slots(slots, codes, (own, voxels, TE, HALO, TE, 1, lifted), upstream, None)

    starts = []
    alive = []
    for number in range(tiles):
        slot = slots[2 * number]
        starts.append(codes[3, slot] * TE)
        alive.append((codes[1, slot] > 0).astype(F32))

    for number in range(tiles):
        source = regions[number][0]
        z_first = starts[number] + number

        @pl.loop(0, source.y_size // 2)
        def _(pair):
            for parity in range(2):
                source.store_row(pair, parity, volume[pl.ds(z_first, source.z_size), number + 2 * pair + parity])

    def finish_layer(number, layer, kind):
        region = regions[number][layer]
        inset = number + layer
        z_first = starts[number] + inset
        q_size = region.z_size // 2

        @pl.loop(0, region.y_size // 2)
        def _(pair):
            for parity in range(2):
                y_at = inset + 2 * pair + parity
                side = (y_at >= HALO).astype(jnp.int32) + (y_at >= HALO + TE).astype(jnp.int32)
                window = pl.ds(z_first, region.z_size)
                keep = mask[side, window]
                value = result[0:q_size, pair, :, parity * channels : (parity + 1) * channels]
                value = value.reshape(keep.shape)
                if kind == "act":
                    out, slope = gelu_pair(value)
                    slopes[number][:, pair, parity] = slope * keep
                    out = out * keep
                elif kind == "delta_two":
                    out = upstream[window, y_at] * gelu_slope(value) * keep
                else:
                    out = value * slopes[number][2 : 2 + region.z_size, pair + 1, parity]
                region.store_row(pair, parity, out)

    def wait(at):
        for copy in copies[at]:
            copy.wait()

    def kernel_gradient(at, left, delta):
        flipped = []
        for number in range(tiles):
            region = regions[number][delta]
            inset = (region.z_size - TE) // 2
            rows = region.tile_rows(inset, inset, channels, channels, TE).astype(F32) * (alive[number] * (1.0 / voxels))
            flipped.append(rows.T.astype(BF))
        flipped = jnp.concatenate(flipped, axis=1)
        for z_tap in range(3):
            columns = []
            for number in range(tiles):
                region = regions[number][left]
                inset = (region.z_size - TE) // 2 - 1
                shifted = [
                    region.tile_rows(inset + z_tap, inset + y_tap, 3 * channels, 0, TE) for y_tap in range(3)
                ]
                columns.append(jnp.concatenate(shifted, axis=1))
            product = jnp.dot(flipped, jnp.concatenate(columns, axis=0), preferred_element_type=F32)
            for y_tap in range(3):
                for x_tap in range(3):
                    lane = (y_tap * 3 + x_tap) * channels
                    row = (z_tap * 9 + x_tap * 3 + y_tap) * channels
                    grad_rows[row : row + channels] = product[:, lane : lane + channels].T
        share = 27 * channels // grads.shape[1]
        padded = grads.shape[2]
        for part in range(grads.shape[1]):
            grads[at, part] = grad_rows[part * share : part * share + padded].astype(BF)

    grad_rows[27 * channels :] = jnp.zeros_like(grad_rows[27 * channels :])
    wait(0)
    for number in range(tiles):
        convolve_region(regions[number][0], weights[0], False, result)
        finish_layer(number, 1, "act")
    wait(1)
    for number in range(tiles):
        convolve_region(regions[number][1], weights[1], False, result)
        finish_layer(number, 2, "delta_two")
    kernel_gradient(1, 1, 2)
    wait(2)
    for number in range(tiles):
        convolve_region(regions[number][2], weights[2], True, result)
        finish_layer(number, 3, "delta_one")
    kernel_gradient(0, 0, 3)
    wait(3)
    convolve_region(regions[0][3], weights[3], True, result)
    for pair in range(TE // 2):
        for parity in range(2):
            value = result[0 : TE // 2, pair, :, parity * channels : (parity + 1) * channels] * alive[0]
            value = value.reshape(TE, TE, channels)
            for z_at in range(TE):
                lifted[pl.ds(z_at * TE * TE + 2 * pair + parity, TE, stride=TE)] = value[z_at]
    input_grad[...] = lifted[...].astype(BF)


def backward_call(own, rims, first_kernel, second_kernel, codes, depth_at, shares, tiles):
    channels = first_kernel.shape[-1]
    voxels = TE * TE * TE
    positions = codes.shape[1]
    planes = positions * TE + 2 * HALO
    span = TE + 2 * HALO
    inner = span // 2 - 1
    padded = -(-(27 * channels // shares) // 16) * 16
    scratch = [
        pltpu.VMEM((planes, span, TE, channels), F32),
        pltpu.VMEM((planes, span, TE, channels), F32),
        pltpu.VMEM((3, planes, TE, channels), F32),
        pltpu.VMEM((voxels, channels), F32),
        pltpu.VMEM((inner, inner, 2 * TE, 2 * channels), F32),
        pltpu.VMEM((27 * channels + 16, channels), F32),
    ]
    scratch += [pltpu.VMEM((36 * channels, 2 * channels), BF)] * 2
    scratch += [pltpu.VMEM((2 * channels, 36 * channels), BF)] * 2
    scratch += [pltpu.SemaphoreType.DMA((54,))] * 4
    for number in range(tiles):
        for layer in range(4):
            size = span - 2 * (number + layer)
            scratch += region_shapes(size, size, TE, channels, size > TE)
    for number in range(tiles):
        size = span - 2 * (number + 1)
        scratch.append(pltpu.VMEM((size, size // 2, 2, TE, channels), F32))
    vmem = pl.BlockSpec(memory_space=pltpu.VMEM)
    smem = pl.BlockSpec(memory_space=pltpu.SMEM)
    hbm = pl.BlockSpec(memory_space=pl.ANY)

    def body(codes_ref, depth_ref, *refs):
        backward_kernel(len(own), 0, channels, tiles, codes_ref, depth_ref, *refs)

    return pl.pallas_call(
        body,
        out_shape=[
            jax.ShapeDtypeStruct((voxels, channels), BF),
            jax.ShapeDtypeStruct((2, shares, padded, channels), BF),
        ],
        in_specs=[smem, smem] + [vmem] * (2 * len(own)) + [hbm, hbm],
        out_specs=[vmem, vmem],
        scratch_shapes=scratch,
        compiler_params=pltpu.CompilerParams(vmem_limit_bytes=60 * 1024 * 1024),
        name="tile_backward",
    )(codes, depth_at, *own, *rims, first_kernel, second_kernel)


def on_device_line(features, cotangent, first_kernel, second_kernel, slot_tile, slot_used):
    voxels, channels = features.shape[2:]
    depth_size, space_size = lax.axis_size("depth"), lax.axis_size("space")
    depth_at, space_at = lax.axis_index("depth"), lax.axis_index("space")
    feature_rows, upstream_rows = features[0, 0], cotangent[0, 0]
    own_code = jnp.where(slot_used[0] == 1, slot_tile[0] + 1, 0)

    code_rows = jnp.pad(own_code, (0, 16 - own_code.shape[0])).astype(BF)
    code_rows = jnp.broadcast_to(code_rows[:, None], (16, channels))
    feature_box = feature_rows.reshape(TE, TE, TE, channels)
    upstream_box = upstream_rows.reshape(TE, TE, TE, channels)

    def side(feature_part, upstream_part):
        return jnp.concatenate(
            [feature_part.reshape(-1, channels), upstream_part.reshape(-1, channels), code_rows], axis=0
        )

    from_below = from_behind(side(feature_box[:, :, TE - HALO :], upstream_box[:, :, TE - 2 :]), "space", 1)
    from_above = from_behind(side(feature_box[:, :, :HALO], upstream_box[:, :, :2]), "space", -1)
    own = jnp.concatenate([feature_rows, upstream_rows], axis=0)
    rim = jnp.concatenate([from_below, from_above], axis=0)
    rim_size = rim.shape[0] // 2

    def swap(block, bit):
        return lax.ppermute(block, "depth", [(i, i ^ bit) for i in range(depth_size)])

    own_far, rim_far = swap(own, 2), swap(rim, 2)
    own_blocks = [own, swap(own, 1), own_far, swap(own_far, 1)]
    rim_blocks = [rim, swap(rim, 1), rim_far, swap(rim_far, 1)]

    def side_code(first):
        return rim[first : first + own_code.shape[0], 0].astype(jnp.int32)

    codes = jnp.stack([side_code(rim_size - 16), own_code, side_code(2 * rim_size - 16), slot_tile[0]])
    shares = depth_size * space_size
    input_grad, grads = backward_call(
        own_blocks,
        rim_blocks,
        first_kernel,
        second_kernel,
        codes,
        depth_at.reshape(1),
        shares,
        2,
    )
    share = 27 * channels // shares
    by_owner = grads.reshape(2, space_size, depth_size, grads.shape[2], channels)

    def for_depth(owner):
        return lax.dynamic_index_in_dim(by_owner, owner, 2, keepdims=False)

    summed = for_depth(depth_at).astype(F32) + swap(for_depth(depth_at ^ 1), 1).astype(F32)
    parts = lax.all_to_all(summed.astype(BF), "space", 1, 1, tiled=True)
    total = jnp.sum(parts.astype(F32), axis=1)[:, :share]
    first_share, second_share = total[0].reshape(-1), total[1].reshape(-1)
    return (input_grad.reshape(features.shape), first_share, second_share)


def solution(mesh):
    line = mesh.shape["space"] == GY and mesh.shape["depth"] == 4
    run = on_device_line if line else on_device_wide
    return jax.shard_map(
        run,
        mesh=mesh,
        in_specs=(
            P("space", "depth", None, None),
            P("space", "depth", None, None),
            P(),
            P(),
            P("space", None),
            P("space", None),
        ),
        out_specs=(P("space", "depth", None, None), P(("space", "depth")), P(("space", "depth"))),
        check_vma=False,
    )
```

```python
import jax
import jax.numpy as jnp
from jax import lax
from jax.experimental import pallas as pl
from jax.experimental.pallas import tpu as pltpu
from jax.sharding import PartitionSpec as P

TE = 8
GY = 8


SLOPE_COEF = 0.7978845608028654
CUBIC_COEF = 0.044715


def from_behind(block, axis, distance):
    devices = range(lax.axis_size(axis))
    route = [(i - distance, i) for i in devices if i - distance in devices]
    return lax.ppermute(block, axis, route)


def gelu_pair(values):
    inner_arg = SLOPE_COEF * (values + CUBIC_COEF * values * values * values)
    tangent = jnp.tanh(inner_arg)
    output = 0.5 * values * (1.0 + tangent)
    derivative = 0.5 * (1.0 + tangent) + 0.5 * values * (1.0 - tangent * tangent) * SLOPE_COEF * (
        1.0 + 3.0 * CUBIC_COEF * values * values
    )
    return (output, derivative)


def gelu_slope(values):
    inner_arg = SLOPE_COEF * (values + CUBIC_COEF * values * values * values)
    tangent = jnp.tanh(inner_arg)
    return 0.5 * (1.0 + tangent) + 0.5 * values * (1.0 - tangent * tangent) * SLOPE_COEF * (
        1.0 + 3.0 * CUBIC_COEF * values * values
    )


def place_matrix(slot_tile, slot_used, position_count):
    positions = jnp.arange(position_count, dtype=jnp.int32)
    matches = (slot_tile[0][None, :] == positions[:, None]) & (slot_used[0][None, :] == 1)
    return matches.astype(jnp.bfloat16)


def dense_column(tile_rows, placement):
    summed = jnp.einsum(
        "tj,jvc->tvc",
        placement,
        lax.all_gather(tile_rows, "depth", axis=0, tiled=True),
        preferred_element_type=jnp.float32,
    )
    return summed.astype(jnp.bfloat16).reshape(-1, TE, TE, summed.shape[-1])


def extend_sides(own_block, move_face, space_index):
    y_coord = space_index % GY
    below = move_face(own_block[:, :, -1:, :], 1) * (y_coord > 0).astype(own_block.dtype)
    above = move_face(own_block[:, :, :1, :], -1) * (y_coord < GY - 1).astype(own_block.dtype)
    widened = jnp.concatenate([below, own_block, above], axis=2)
    behind = move_face(widened[:, -1:, :, :], GY)
    ahead = move_face(widened[:, :1, :, :], -GY)
    return jnp.concatenate([behind, widened, ahead], axis=1)


def pad_depth(own_block):
    return jnp.pad(own_block, ((1, 1), (0, 0), (0, 0), (0, 0)))


def windows_at(padded, positions):

    def one_window(z_index):
        return lax.dynamic_slice_in_dim(padded, z_index * TE, TE + 2, 0)

    return jax.vmap(one_window)(positions)


def unfold(windows, flipped):
    pieces = []
    for kernel_tap in range(27):
        z_step, x_step, y_step = (kernel_tap // 9, kernel_tap // 3 % 3, kernel_tap % 3)
        if flipped:
            z_step, x_step, y_step = (2 - z_step, 2 - x_step, 2 - y_step)
        pieces.append(
            windows[:, z_step : z_step + TE, x_step : x_step + TE, y_step : y_step + TE, :]
        )
    stacked = jnp.concatenate(pieces, axis=-1)
    return stacked.reshape(-1, stacked.shape[-1])


def tile_sum(columns, delta):
    return lax.dot_general(
        columns, delta, (((0,), (0,)), ((), ())), preferred_element_type=jnp.float32
    )


def on_device_wide(features, cotangent, first_kernel, second_kernel, slot_tile, slot_used):
    depth_index = lax.axis_index("depth")
    space_index = lax.axis_index("space")
    slot_count = features.shape[1]
    voxels = features.shape[2]
    channels = features.shape[3]
    position_count = slot_tile.shape[1]
    placement = place_matrix(slot_tile, slot_used, position_count)
    own_first = depth_index * slot_count
    own_tiles = lax.dynamic_slice_in_dim(slot_tile[0], own_first, slot_count, 0)
    own_used = lax.dynamic_slice_in_dim(slot_used[0], own_first, slot_count, 0).astype(jnp.float32)
    feature_slots = features[0]
    upstream_slots = cotangent[0]

    def column_move(face, offset):
        return from_behind(face, "space", offset)

    def halo_of(tile_rows):
        column = dense_column(tile_rows.reshape(slot_count, voxels, channels), placement)
        return pad_depth(extend_sides(column, column_move, space_index))

    upstream = upstream_slots.reshape(-1, channels)
    source_column = halo_of(feature_slots)
    alive_rows = jnp.repeat(own_used, voxels)[:, None]
    forward_one = first_kernel.reshape(-1, channels)
    forward_two = second_kernel.reshape(-1, channels)
    backward_one = jnp.transpose(first_kernel, (0, 2, 1)).reshape(-1, channels)
    backward_two = jnp.transpose(second_kernel, (0, 2, 1)).reshape(-1, channels)
    source_cols = unfold(windows_at(source_column, own_tiles), False)
    pre_one = jnp.dot(source_cols, forward_one, preferred_element_type=jnp.float32)
    act_value, slope_one = gelu_pair(pre_one)
    act_one = (act_value * alive_rows).astype(jnp.bfloat16)
    act_cols = unfold(windows_at(halo_of(act_one), own_tiles), False)
    pre_two = jnp.dot(act_cols, forward_two, preferred_element_type=jnp.float32)
    slope_two = gelu_slope(pre_two)
    delta_two = (upstream.astype(jnp.float32) * slope_two * alive_rows).astype(jnp.bfloat16)
    second_grad = tile_sum(act_cols, delta_two).reshape(-1) * (1.0 / voxels)
    back_one = jnp.dot(
        unfold(windows_at(halo_of(delta_two), own_tiles), True),
        backward_two,
        preferred_element_type=jnp.float32,
    )
    delta_one = (back_one * slope_one * alive_rows).astype(jnp.bfloat16)
    first_grad = tile_sum(source_cols, delta_one).reshape(-1) * (1.0 / voxels)
    back_zero = jnp.dot(
        unfold(windows_at(halo_of(delta_one), own_tiles), True),
        backward_one,
        preferred_element_type=jnp.float32,
    )
    used_rows = jnp.repeat(own_used, voxels)[:, None]
    input_grad = (back_zero * used_rows).astype(jnp.bfloat16).reshape(features.shape)
    first_share, second_share = (
        lax.psum_scatter(first_grad, ("space", "depth"), scatter_dimension=0, tiled=True),
        lax.psum_scatter(second_grad, ("space", "depth"), scatter_dimension=0, tiled=True),
    )
    return (input_grad, first_share, second_share)


HALO = 4
BF = jnp.bfloat16
F32 = jnp.float32


class Region:
    def __init__(self, even, odd, z_size, y_size):
        self.even, self.odd, self.z_size, self.y_size = even, odd, z_size, y_size

    def planes(self, first):
        return (self.odd, (first - 1) // 2) if first % 2 else (self.even, first // 2)

    def store_row(self, y_pair, y_parity, column):
        z_size, width, channels = column.shape
        place = lax.broadcasted_iota(jnp.int32, column.shape, 1)
        before = jnp.where(place == 0, 0.0, pltpu.roll(column, 1, 1))
        after = jnp.where(place == width - 1, 0.0, pltpu.roll(column, width - 1, 1))
        wide = jnp.concatenate([before, column, after], axis=-1)
        self.even[:, y_pair, y_parity] = wide.reshape(z_size // 2, 2 * width, 3 * channels).astype(BF)
        if self.odd is not None:
            inner = wide[1:-1].reshape(z_size // 2 - 1, 2 * width, 3 * channels)
            self.odd[:, y_pair, y_parity] = inner.astype(BF)

    def tile_rows(self, z_first, y_first, lanes, lane_first, edge):
        ref, q_first = self.planes(z_first)
        parts = []
        for y_at in range(y_first, y_first + edge):
            part = ref[q_first : q_first + edge // 2, y_at // 2, y_at % 2, :, lane_first : lane_first + lanes]
            parts.append(part.reshape(-1, lanes))
        return jnp.concatenate(parts, axis=0)


def region_shapes(z_size, y_size, width, channels, with_odd):
    tail = (y_size // 2, 2, 2 * width, 3 * channels)
    shapes = [pltpu.VMEM((z_size // 2,) + tail, BF)]
    if with_odd:
        shapes.append(pltpu.VMEM((z_size // 2 - 1,) + tail, BF))
    return shapes


def convolve_region(region, weights, transposed, result):
    q_size, r_size = region.z_size // 2 - 1, region.y_size // 2 - 1
    channels = region.even.shape[-1] // 3
    pieces = []
    for block in range(9):
        z_tap, x_tap = block // 3, block % 3
        if transposed:
            z_tap, x_tap = 2 - z_tap, 2 - x_tap
        ref, q_first = region.planes(z_tap)
        for y_at in range(4):
            if transposed:
                y_at = 3 - y_at
            piece = ref[
                q_first : q_first + q_size,
                y_at // 2 : y_at // 2 + r_size,
                y_at % 2,
                :,
                x_tap * channels : (x_tap + 1) * channels,
            ]
            pieces.append(piece.reshape(-1, channels))
    left = jnp.concatenate(pieces, axis=1)
    if transposed:
        right = jnp.concatenate([weights[at // 4, at % 4] for at in range(36)], axis=1)
        contract = (((1,), (1,)), ((), ()))
    else:
        right = weights[...].reshape(36 * channels, 2 * channels)
        contract = (((1,), (0,)), ((), ()))
    product = lax.dot_general(left, right, contract, preferred_element_type=F32)
    result[0:q_size, 0:r_size] = product.reshape(q_size, r_size, product.shape[0] // (q_size * r_size), -1)


def kernel_copies(kernel, weights, sems, transposed):
    channels = kernel.shape[-1]
    copies = []
    for parity in range(2):
        out = pl.ds(parity * channels, channels)
        if transposed:
            place = weights.at[:, pl.ds(1 - parity, 3), out, :]
        else:
            place = weights.at[:, pl.ds(parity, 3), :, out]
        copies.append(pltpu.make_async_copy(kernel, place, sems.at[parity]))
    return copies


def clear_unused(weights, transposed):
    channels = min(weights.shape[2:])
    blank = jnp.zeros((channels, channels), BF)
    for block in range(9):
        if transposed:
            weights[block, 0, 0:channels, :] = blank
            weights[block, 3, channels:, :] = blank
        else:
            weights[block, 3, :, 0:channels] = blank
            weights[block, 0, :, channels:] = blank


def place_slots(slots, codes, sources, volume, mask):
    raw, offset, stride, y_first, y_count, cls, lifted = sources
    for block in range(len(raw)):
        code = codes[cls, slots[block]]

        @pl.when(code > 0)
        def _():
            z_first = HALO + (code - 1) * TE
            rows = TE * TE * stride
            lifted[0:rows] = raw[block][offset : offset + rows].astype(F32)
            for z_at in range(TE):
                for y_at in range(y_count):
                    volume[z_first + z_at, y_first + y_at] = lifted[pl.ds(z_at * TE * stride + y_at, TE, stride=stride)]
            if mask is not None:
                mask[cls, pl.ds(z_first, TE)] = jnp.ones((TE,) + mask.shape[2:], F32)


def backward_kernel(block_count, packs_per, channels, tiles, codes, depth_at, *refs):
    own = refs[:block_count]
    rims = refs[block_count : 2 * block_count]
    first_kernel, second_kernel = refs[2 * block_count : 2 * block_count + 2]
    input_grad, grads = refs[2 * block_count + 2 : 2 * block_count + 4]
    rest = list(refs[2 * block_count + 4 :])

    def take():
        return rest.pop(0)

    volume, upstream, mask, lifted, result, grad_rows = (take() for _ in range(6))
    weights = [take() for _ in range(4)]
    sems = [take() for _ in range(4)]
    regions = []
    for number in range(tiles):
        halo = HALO - number
        group = []
        for layer in range(4):
            size = TE + 2 * (halo - layer)
            even = take()
            odd = take() if size > TE else None
            group.append(Region(even, odd, size, size))
        regions.append(group)
    slopes = [take() for _ in range(tiles)]

    copies = [
        kernel_copies(first_kernel, weights[0], sems[0], False),
        kernel_copies(second_kernel, weights[1], sems[1], False),
        kernel_copies(second_kernel, weights[2], sems[2], True),
        kernel_copies(first_kernel, weights[3], sems[3], True),
    ]
    for group in copies:
        for copy in group:
            copy.start()
    for at in range(4):
        clear_unused(weights[at], at > 1)

    me = depth_at[0]
    slots = [me ^ block for block in range(block_count)]
    voxels = TE * TE * TE
    volume[...] = jnp.zeros_like(volume)
    upstream[...] = jnp.zeros_like(upstream)
    mask[...] = jnp.zeros_like(mask)
    face, thin = voxels // 2, voxels // 4
    rim_size = face + thin + 16
    for cls, raw, offset, y_first in ((0, rims, 0, 0), (2, rims, rim_size, HALO + TE)):
        place_slots(slots, codes, (raw, offset, HALO, y_first, HALO, cls, lifted), volume, mask)
        place_slots(slots, codes, (raw, offset + face, 2, y_first if cls else 2, 2, cls, lifted), upstream, None)
    place_slots(slots, codes, (own, 0, TE, HALO, TE, 1, lifted), volume, mask)
    place_slots(slots, codes, (own, voxels, TE, HALO, TE, 1, lifted), upstream, None)

    starts = []
    alive = []
    for number in range(tiles):
        slot = slots[2 * number]
        starts.append(codes[3, slot] * TE)
        alive.append((codes[1, slot] > 0).astype(F32))

    for number in range(tiles):
        source = regions[number][0]
        z_first = starts[number] + number

        for pair in range(source.y_size // 2):
            for parity in range(2):
                source.store_row(pair, parity, volume[pl.ds(z_first, source.z_size), number + 2 * pair + parity])

    def finish_layer(number, layer, kind):
        region = regions[number][layer]
        inset = number + layer
        z_first = starts[number] + inset
        q_size = region.z_size // 2

        for pair in range(region.y_size // 2):
            for parity in range(2):
                y_at = inset + 2 * pair + parity
                side = (y_at >= HALO) + (y_at >= HALO + TE)
                window = pl.ds(z_first, region.z_size)
                keep = mask[side, window]
                value = result[0:q_size, pair, :, parity * channels : (parity + 1) * channels]
                value = value.reshape(keep.shape)
                if kind == "act":
                    out, slope = gelu_pair(value)
                    slopes[number][:, pair, parity] = slope * keep
                    out = out * keep
                elif kind == "delta_two":
                    out = upstream[window, y_at] * gelu_slope(value) * keep
                else:
                    out = value * slopes[number][2 : 2 + region.z_size, pair + 1, parity]
                region.store_row(pair, parity, out)

    def wait(at):
        for copy in copies[at]:
            copy.wait()

    def kernel_gradient(at, left, delta):
        flipped = []
        for number in range(tiles):
            region = regions[number][delta]
            inset = (region.z_size - TE) // 2
            rows = region.tile_rows(inset, inset, channels, channels, TE).astype(F32) * (alive[number] * (1.0 / voxels))
            flipped.append(rows.T.astype(BF))
        flipped = jnp.concatenate(flipped, axis=1)
        for z_tap in range(3):
            columns = []
            for number in range(tiles):
                region = regions[number][left]
                inset = (region.z_size - TE) // 2 - 1
                shifted = [
                    region.tile_rows(inset + z_tap, inset + y_tap, 3 * channels, 0, TE) for y_tap in range(3)
                ]
                columns.append(jnp.concatenate(shifted, axis=1))
            product = jnp.dot(flipped, jnp.concatenate(columns, axis=0), preferred_element_type=F32)
            for y_tap in range(3):
                for x_tap in range(3):
                    lane = (y_tap * 3 + x_tap) * channels
                    row = (z_tap * 9 + x_tap * 3 + y_tap) * channels
                    grad_rows[row : row + channels] = product[:, lane : lane + channels].T
        share = 27 * channels // grads.shape[1]
        padded = grads.shape[2]
        for part in range(grads.shape[1]):
            grads[at, part] = grad_rows[part * share : part * share + padded].astype(BF)

    grad_rows[27 * channels :] = jnp.zeros_like(grad_rows[27 * channels :])
    wait(0)
    for number in range(tiles):
        convolve_region(regions[number][0], weights[0], False, result)
        finish_layer(number, 1, "act")
    wait(1)
    for number in range(tiles):
        convolve_region(regions[number][1], weights[1], False, result)
        finish_layer(number, 2, "delta_two")
    kernel_gradient(1, 1, 2)
    wait(2)
    for number in range(tiles):
        convolve_region(regions[number][2], weights[2], True, result)
        finish_layer(number, 3, "delta_one")
    kernel_gradient(0, 0, 3)
    wait(3)
    convolve_region(regions[0][3], weights[3], True, result)
    for pair in range(TE // 2):
        for parity in range(2):
            value = result[0 : TE // 2, pair, :, parity * channels : (parity + 1) * channels] * alive[0]
            value = value.reshape(TE, TE, channels)
            for z_at in range(TE):
                lifted[pl.ds(z_at * TE * TE + 2 * pair + parity, TE, stride=TE)] = value[z_at]
    input_grad[...] = lifted[...].astype(BF)


def backward_call(own, rims, first_kernel, second_kernel, codes, depth_at, shares, tiles):
    channels = first_kernel.shape[-1]
    voxels = TE * TE * TE
    positions = codes.shape[1]
    planes = positions * TE + 2 * HALO
    span = TE + 2 * HALO
    inner = span // 2 - 1
    padded = -(-(27 * channels // shares) // 16) * 16
    scratch = [
        pltpu.VMEM((planes, span, TE, channels), F32),
        pltpu.VMEM((planes, span, TE, channels), F32),
        pltpu.VMEM((3, planes, TE, channels), F32),
        pltpu.VMEM((voxels, channels), F32),
        pltpu.VMEM((inner, inner, 2 * TE, 2 * channels), F32),
        pltpu.VMEM((27 * channels + 16, channels), F32),
    ]
    scratch += [pltpu.VMEM((9, 4, channels, 2 * channels), BF)] * 2
    scratch += [pltpu.VMEM((9, 4, 2 * channels, channels), BF)] * 2
    scratch += [pltpu.SemaphoreType.DMA((2,))] * 4
    for number in range(tiles):
        for layer in range(4):
            size = span - 2 * (number + layer)
            scratch += region_shapes(size, size, TE, channels, size > TE)
    for number in range(tiles):
        size = span - 2 * (number + 1)
        scratch.append(pltpu.VMEM((size, size // 2, 2, TE, channels), F32))
    vmem = pl.BlockSpec(memory_space=pltpu.VMEM)
    smem = pl.BlockSpec(memory_space=pltpu.SMEM)
    hbm = pl.BlockSpec(memory_space=pl.ANY)

    def body(codes_ref, depth_ref, *refs):
        backward_kernel(len(own), 0, channels, tiles, codes_ref, depth_ref, *refs)

    return pl.pallas_call(
        body,
        out_shape=[
            jax.ShapeDtypeStruct((voxels, channels), BF),
            jax.ShapeDtypeStruct((2, shares, padded, channels), BF),
        ],
        in_specs=[smem, smem] + [vmem] * (2 * len(own)) + [hbm, hbm],
        out_specs=[vmem, vmem],
        scratch_shapes=scratch,
        compiler_params=pltpu.CompilerParams(vmem_limit_bytes=60 * 1024 * 1024),
        name="tile_backward",
    )(codes, depth_at, *own, *rims, *(kernel.reshape(9, 3, channels, channels) for kernel in (first_kernel, second_kernel)))


def on_device_line(features, cotangent, first_kernel, second_kernel, slot_tile, slot_used):
    voxels, channels = features.shape[2:]
    depth_size, space_size = lax.axis_size("depth"), lax.axis_size("space")
    depth_at, space_at = lax.axis_index("depth"), lax.axis_index("space")
    feature_rows, upstream_rows = features[0, 0], cotangent[0, 0]
    own_code = jnp.where(slot_used[0] == 1, slot_tile[0] + 1, 0)

    code_rows = jnp.pad(own_code, (0, 16 - own_code.shape[0])).astype(BF)
    code_rows = jnp.broadcast_to(code_rows[:, None], (16, channels))
    feature_box = feature_rows.reshape(TE, TE, TE, channels)
    upstream_box = upstream_rows.reshape(TE, TE, TE, channels)

    def side(feature_part, upstream_part):
        return jnp.concatenate(
            [feature_part.reshape(-1, channels), upstream_part.reshape(-1, channels), code_rows], axis=0
        )

    from_below = from_behind(side(feature_box[:, :, TE - HALO :], upstream_box[:, :, TE - 2 :]), "space", 1)
    from_above = from_behind(side(feature_box[:, :, :HALO], upstream_box[:, :, :2]), "space", -1)
    own = jnp.concatenate([feature_rows, upstream_rows], axis=0)
    rim = jnp.concatenate([from_below, from_above], axis=0)
    rim_size = rim.shape[0] // 2

    def swap(block, bit):
        return lax.ppermute(block, "depth", [(i, i ^ bit) for i in range(depth_size)])

    own_far, rim_far = swap(own, 2), swap(rim, 2)
    own_blocks = [own, swap(own, 1), own_far, swap(own_far, 1)]
    rim_blocks = [rim, swap(rim, 1), rim_far, swap(rim_far, 1)]

    def side_code(first):
        return rim[first : first + own_code.shape[0], 0].astype(jnp.int32)

    codes = jnp.stack([side_code(rim_size - 16), own_code, side_code(2 * rim_size - 16), slot_tile[0]])
    shares = depth_size * space_size
    input_grad, grads = backward_call(
        own_blocks,
        rim_blocks,
        first_kernel,
        second_kernel,
        codes,
        depth_at.reshape(1),
        shares,
        2,
    )
    share = 27 * channels // shares
    by_owner = grads.reshape(2, space_size, depth_size, grads.shape[2], channels)

    def for_depth(owner):
        return lax.dynamic_index_in_dim(by_owner, owner, 2, keepdims=False)

    summed = for_depth(depth_at).astype(F32) + swap(for_depth(depth_at ^ 1), 1).astype(F32)
    parts = lax.all_to_all(summed.astype(BF), "space", 1, 1, tiled=True)
    total = jnp.sum(parts.astype(F32), axis=1)[:, :share]
    first_share, second_share = total[0].reshape(-1), total[1].reshape(-1)
    return (input_grad.reshape(features.shape), first_share, second_share)


def solution(mesh):
    line = mesh.shape["space"] == GY and mesh.shape["depth"] == 4
    run = on_device_line if line else on_device_wide
    return jax.shard_map(
        run,
        mesh=mesh,
        in_specs=(
            P("space", "depth", None, None),
            P("space", "depth", None, None),
            P(),
            P(),
            P("space", None),
            P("space", None),
        ),
        out_specs=(P("space", "depth", None, None), P(("space", "depth")), P(("space", "depth"))),
        check_vma=False,
    )
```

```python
import jax
import jax.numpy as jnp
from jax import lax
from jax.experimental import pallas as pl
from jax.experimental.pallas import tpu as pltpu
from jax.sharding import PartitionSpec as P

TE = 8
GY = 8


SLOPE_COEF = 0.7978845608028654
CUBIC_COEF = 0.044715


def from_behind(block, axis, distance):
    devices = range(lax.axis_size(axis))
    route = [(i - distance, i) for i in devices if i - distance in devices]
    return lax.ppermute(block, axis, route)


def gelu_pair(values):
    inner_arg = SLOPE_COEF * (values + CUBIC_COEF * values * values * values)
    tangent = jnp.tanh(inner_arg)
    output = 0.5 * values * (1.0 + tangent)
    derivative = 0.5 * (1.0 + tangent) + 0.5 * values * (1.0 - tangent * tangent) * SLOPE_COEF * (
        1.0 + 3.0 * CUBIC_COEF * values * values
    )
    return (output, derivative)


def gelu_slope(values):
    inner_arg = SLOPE_COEF * (values + CUBIC_COEF * values * values * values)
    tangent = jnp.tanh(inner_arg)
    return 0.5 * (1.0 + tangent) + 0.5 * values * (1.0 - tangent * tangent) * SLOPE_COEF * (
        1.0 + 3.0 * CUBIC_COEF * values * values
    )


def place_matrix(slot_tile, slot_used, position_count):
    positions = jnp.arange(position_count, dtype=jnp.int32)
    matches = (slot_tile[0][None, :] == positions[:, None]) & (slot_used[0][None, :] == 1)
    return matches.astype(jnp.bfloat16)


def dense_column(tile_rows, placement):
    summed = jnp.einsum(
        "tj,jvc->tvc",
        placement,
        lax.all_gather(tile_rows, "depth", axis=0, tiled=True),
        preferred_element_type=jnp.float32,
    )
    return summed.astype(jnp.bfloat16).reshape(-1, TE, TE, summed.shape[-1])


def extend_sides(own_block, move_face, space_index):
    y_coord = space_index % GY
    below = move_face(own_block[:, :, -1:, :], 1) * (y_coord > 0).astype(own_block.dtype)
    above = move_face(own_block[:, :, :1, :], -1) * (y_coord < GY - 1).astype(own_block.dtype)
    widened = jnp.concatenate([below, own_block, above], axis=2)
    behind = move_face(widened[:, -1:, :, :], GY)
    ahead = move_face(widened[:, :1, :, :], -GY)
    return jnp.concatenate([behind, widened, ahead], axis=1)


def pad_depth(own_block):
    return jnp.pad(own_block, ((1, 1), (0, 0), (0, 0), (0, 0)))


def windows_at(padded, positions):

    def one_window(z_index):
        return lax.dynamic_slice_in_dim(padded, z_index * TE, TE + 2, 0)

    return jax.vmap(one_window)(positions)


def unfold(windows, flipped):
    pieces = []
    for kernel_tap in range(27):
        z_step, x_step, y_step = (kernel_tap // 9, kernel_tap // 3 % 3, kernel_tap % 3)
        if flipped:
            z_step, x_step, y_step = (2 - z_step, 2 - x_step, 2 - y_step)
        pieces.append(
            windows[:, z_step : z_step + TE, x_step : x_step + TE, y_step : y_step + TE, :]
        )
    stacked = jnp.concatenate(pieces, axis=-1)
    return stacked.reshape(-1, stacked.shape[-1])


def tile_sum(columns, delta):
    return lax.dot_general(
        columns, delta, (((0,), (0,)), ((), ())), preferred_element_type=jnp.float32
    )


def on_device_wide(features, cotangent, first_kernel, second_kernel, slot_tile, slot_used):
    depth_index = lax.axis_index("depth")
    space_index = lax.axis_index("space")
    slot_count = features.shape[1]
    voxels = features.shape[2]
    channels = features.shape[3]
    position_count = slot_tile.shape[1]
    placement = place_matrix(slot_tile, slot_used, position_count)
    own_first = depth_index * slot_count
    own_tiles = lax.dynamic_slice_in_dim(slot_tile[0], own_first, slot_count, 0)
    own_used = lax.dynamic_slice_in_dim(slot_used[0], own_first, slot_count, 0).astype(jnp.float32)
    feature_slots = features[0]
    upstream_slots = cotangent[0]

    def column_move(face, offset):
        return from_behind(face, "space", offset)

    def halo_of(tile_rows):
        column = dense_column(tile_rows.reshape(slot_count, voxels, channels), placement)
        return pad_depth(extend_sides(column, column_move, space_index))

    upstream = upstream_slots.reshape(-1, channels)
    source_column = halo_of(feature_slots)
    alive_rows = jnp.repeat(own_used, voxels)[:, None]
    forward_one = first_kernel.reshape(-1, channels)
    forward_two = second_kernel.reshape(-1, channels)
    backward_one = jnp.transpose(first_kernel, (0, 2, 1)).reshape(-1, channels)
    backward_two = jnp.transpose(second_kernel, (0, 2, 1)).reshape(-1, channels)
    source_cols = unfold(windows_at(source_column, own_tiles), False)
    pre_one = jnp.dot(source_cols, forward_one, preferred_element_type=jnp.float32)
    act_value, slope_one = gelu_pair(pre_one)
    act_one = (act_value * alive_rows).astype(jnp.bfloat16)
    act_cols = unfold(windows_at(halo_of(act_one), own_tiles), False)
    pre_two = jnp.dot(act_cols, forward_two, preferred_element_type=jnp.float32)
    slope_two = gelu_slope(pre_two)
    delta_two = (upstream.astype(jnp.float32) * slope_two * alive_rows).astype(jnp.bfloat16)
    second_grad = tile_sum(act_cols, delta_two).reshape(-1) * (1.0 / voxels)
    back_one = jnp.dot(
        unfold(windows_at(halo_of(delta_two), own_tiles), True),
        backward_two,
        preferred_element_type=jnp.float32,
    )
    delta_one = (back_one * slope_one * alive_rows).astype(jnp.bfloat16)
    first_grad = tile_sum(source_cols, delta_one).reshape(-1) * (1.0 / voxels)
    back_zero = jnp.dot(
        unfold(windows_at(halo_of(delta_one), own_tiles), True),
        backward_one,
        preferred_element_type=jnp.float32,
    )
    used_rows = jnp.repeat(own_used, voxels)[:, None]
    input_grad = (back_zero * used_rows).astype(jnp.bfloat16).reshape(features.shape)
    first_share, second_share = (
        lax.psum_scatter(first_grad, ("space", "depth"), scatter_dimension=0, tiled=True),
        lax.psum_scatter(second_grad, ("space", "depth"), scatter_dimension=0, tiled=True),
    )
    return (input_grad, first_share, second_share)


HALO = 4
VMEM_LIMIT = 51 * 1024 * 1024
BF = jnp.bfloat16
F32 = jnp.float32


class Region:
    def __init__(self, even, odd, z_size, y_size):
        self.even, self.odd, self.z_size, self.y_size = even, odd, z_size, y_size

    def planes(self, first):
        return (self.odd, (first - 1) // 2) if first % 2 else (self.even, first // 2)

    def store_row(self, y_pair, y_parity, column):
        z_size, width, channels = column.shape
        place = lax.broadcasted_iota(jnp.int32, column.shape, 1)
        before = jnp.where(place == 0, 0.0, pltpu.roll(column, 1, 1))
        after = jnp.where(place == width - 1, 0.0, pltpu.roll(column, width - 1, 1))
        wide = jnp.concatenate([before, column, after], axis=-1)
        self.even[:, y_pair, y_parity] = wide.reshape(z_size // 2, 2 * width, 3 * channels).astype(BF)
        if self.odd is not None:
            inner = wide[1:-1].reshape(z_size // 2 - 1, 2 * width, 3 * channels)
            self.odd[:, y_pair, y_parity] = inner.astype(BF)

    def tile_rows(self, z_first, y_first, lanes, lane_first, edge):
        ref, q_first = self.planes(z_first)
        parts = []
        for y_at in range(y_first, y_first + edge):
            part = ref[q_first : q_first + edge // 2, y_at // 2, y_at % 2, :, lane_first : lane_first + lanes]
            parts.append(part.reshape(-1, lanes))
        return jnp.concatenate(parts, axis=0)


def region_shapes(z_size, y_size, width, channels, with_odd):
    tail = (y_size // 2, 2, 2 * width, 3 * channels)
    shapes = [pltpu.VMEM((z_size // 2,) + tail, BF)]
    if with_odd:
        shapes.append(pltpu.VMEM((z_size // 2 - 1,) + tail, BF))
    return shapes


def convolve_region(region, kernel, transposed, result):
    q_size, r_size = region.z_size // 2 - 1, region.y_size // 2 - 1
    channels = region.even.shape[-1] // 3
    pieces = []
    for block in range(9):
        z_tap, x_tap = block // 3, block % 3
        if transposed:
            z_tap, x_tap = 2 - z_tap, 2 - x_tap
        ref, q_first = region.planes(z_tap)
        for y_at in range(4):
            if transposed:
                y_at = 3 - y_at
            piece = ref[
                q_first : q_first + q_size,
                y_at // 2 : y_at // 2 + r_size,
                y_at % 2,
                :,
                x_tap * channels : (x_tap + 1) * channels,
            ]
            pieces.append(piece.reshape(-1, channels))
    left = jnp.concatenate(pieces, axis=1)
    blank = jnp.zeros((channels, channels), BF)
    blocks = []
    for block in range(9):
        taps = [kernel[block * 3 + y_tap] for y_tap in range(3)]
        for near, far in zip(*((taps + [blank], [blank] + taps) if not transposed else ([blank] + taps, taps + [blank]))):
            blocks.append(jnp.concatenate([near, far], axis=0 if transposed else 1))
    right = jnp.concatenate(blocks, axis=1 if transposed else 0)
    contract = (((1,), (1 if transposed else 0,)), ((), ()))
    product = lax.dot_general(left, right, contract, preferred_element_type=F32)
    result[0:q_size, 0:r_size] = product.reshape(q_size, r_size, product.shape[0] // (q_size * r_size), -1)


def place_slots(codes, blocks, offset, y_first, y_count, lifted, volume, mask, side):
    for code, block in zip(codes, blocks):

        @pl.when(code > 0)
        def _():
            z_first = HALO + (code - 1) * TE
            rows = TE * TE * y_count
            lifted[0:rows] = block[offset : offset + rows].astype(F32)
            for z_at in range(TE):
                for y_at in range(y_count):
                    row = z_at * TE * y_count + y_at
                    volume[z_first + z_at, y_first + y_at] = lifted[pl.ds(row, TE, stride=y_count)]
            if mask is not None:
                mask[side, pl.ds(z_first, TE)] = jnp.ones((TE,) + mask.shape[2:], F32)


def side_sizes():
    face, thin = HALO * TE * TE, 2 * TE * TE
    return face, thin, face + thin + 16


def sides_kernel(tile, used, feature_rows, upstream_rows, to_above, to_below, own, lifted):
    voxels, channels = feature_rows.shape
    face = side_sizes()[0]
    own[0:voxels] = feature_rows[...]
    own[voxels : 2 * voxels] = upstream_rows[...]
    for rows, width, offset in ((feature_rows, HALO, 0), (upstream_rows, 2, face)):
        lifted[...] = rows[...].astype(F32).reshape(lifted.shape)
        count = TE * TE * width
        to_above[offset : offset + count] = lifted[:, TE - width :].reshape(count, channels).astype(BF)
        to_below[offset : offset + count] = lifted[:, :width].reshape(count, channels).astype(BF)
    place = lax.broadcasted_iota(jnp.int32, (16, channels), 0)
    table = jnp.zeros((16, channels), F32)
    for slot in range(tile.shape[1]):
        code = jnp.where(used[0, slot] == 1, tile[0, slot] + 1, 0)
        table = jnp.where(place == slot, code.astype(F32), table)
    for out in (to_above, to_below, own):
        out[out.shape[0] - 16 :] = table.astype(BF)


def sides_call(slot_tile, slot_used, feature_rows, upstream_rows):
    voxels, channels = feature_rows.shape
    smem = pl.BlockSpec(memory_space=pltpu.SMEM)
    vmem = pl.BlockSpec(memory_space=pltpu.VMEM)
    side = jax.ShapeDtypeStruct((side_sizes()[2], channels), BF)
    return pl.pallas_call(
        sides_kernel,
        out_shape=[side, side, jax.ShapeDtypeStruct((2 * voxels + 16, channels), BF)],
        in_specs=[smem, smem, vmem, vmem],
        out_specs=[vmem] * 3,
        scratch_shapes=[pltpu.VMEM((TE * TE, TE, channels), F32)],
        name="pack_sides",
    )(slot_tile, slot_used, feature_rows, upstream_rows)


def backward_kernel(block_count, tiles, depth_ref, *refs):
    own, rims = refs[:block_count], refs[block_count : 2 * block_count]
    far_kernels = refs[2 * block_count : 2 * block_count + 2]
    input_grad, kept, given = refs[2 * block_count + 2 : 2 * block_count + 5]
    rest = list(refs[2 * block_count + 5 :])
    channels = own[0].shape[-1]

    def take():
        return rest.pop(0)

    volume, upstream, mask, lifted, result, grad_rows, first_kernel, second_kernel, near_own, sems = (
        take() for _ in range(10)
    )
    fetches = [
        pltpu.make_async_copy(far, near, sems.at[at])
        for at, (far, near) in enumerate(
            ((own[0], near_own), (far_kernels[0], first_kernel), (far_kernels[1], second_kernel))
        )
    ]
    for fetch in fetches:
        fetch.start()
    own = (near_own,) + own[1:]
    regions = []
    for number in range(tiles):
        halo = HALO - number
        group = []
        for layer in range(4):
            size = TE + 2 * (halo - layer)
            even = take()
            odd = take() if size > TE else None
            group.append(Region(even, odd, size, size))
        regions.append(group)
    slopes = [take() for _ in range(tiles)]

    me = depth_ref[0]
    slots = [me ^ block for block in range(block_count)]
    voxels = TE * TE * TE
    volume[...] = jnp.zeros_like(volume)
    upstream[...] = jnp.zeros_like(upstream)
    mask[...] = jnp.zeros_like(mask)
    face, thin, side_rows = side_sizes()

    def table_at(block, first):
        table = block[first : first + 16].astype(F32)
        place = lax.broadcasted_iota(jnp.int32, table.shape, 0)
        return [jnp.max(jnp.where(place == slot, table, 0.0)).astype(jnp.int32) for slot in slots]

    fetches[0].wait()
    held = table_at(own[0], 2 * voxels)
    place_slots(held, own, 0, HALO, TE, lifted, volume, mask, 1)
    place_slots(held, own, voxels, HALO, TE, lifted, upstream, None, 1)
    codes = table_at(rims[0], face + thin)
    place_slots(codes, rims, 0, 0, HALO, lifted, volume, mask, 0)
    place_slots(codes, rims, face, HALO - 2, 2, lifted, upstream, None, 0)
    codes = table_at(rims[0], side_rows + face + thin)
    place_slots(codes, rims, side_rows, HALO + TE, HALO, lifted, volume, mask, 2)
    place_slots(codes, rims, side_rows + face, HALO + TE, 2, lifted, upstream, None, 2)

    starts = []
    alive = []
    for number in range(tiles):
        starts.append(jnp.maximum(held[2 * number] - 1, 0) * TE)
        alive.append((held[2 * number] > 0).astype(F32))

    for number in range(tiles):
        source = regions[number][0]
        z_first = starts[number] + number

        for pair in range(source.y_size // 2):
            for parity in range(2):
                source.store_row(pair, parity, volume[pl.ds(z_first, source.z_size), number + 2 * pair + parity])

    def finish_layer(number, layer, kind):
        region = regions[number][layer]
        inset = number + layer
        z_first = starts[number] + inset
        q_size = region.z_size // 2

        for pair in range(region.y_size // 2):
            for parity in range(2):
                y_at = inset + 2 * pair + parity
                side = (y_at >= HALO) + (y_at >= HALO + TE)
                window = pl.ds(z_first, region.z_size)
                keep = mask[side, window]
                value = result[0:q_size, pair, :, parity * channels : (parity + 1) * channels]
                value = value.reshape(keep.shape)
                if kind == "act":
                    out, slope = gelu_pair(value)
                    slopes[number][:, pair, parity] = slope * keep
                    out = out * keep
                elif kind == "delta_two":
                    out = upstream[window, y_at] * gelu_slope(value) * keep
                else:
                    out = value * slopes[number][2 : 2 + region.z_size, pair + 1, parity]
                region.store_row(pair, parity, out)

    def kernel_gradient(at, left, delta):
        flipped = []
        for number in range(tiles):
            region = regions[number][delta]
            inset = (region.z_size - TE) // 2
            rows = region.tile_rows(inset, inset, channels, channels, TE).astype(F32) * (alive[number] * (1.0 / voxels))
            flipped.append(rows.T.astype(BF))
        flipped = jnp.concatenate(flipped, axis=1)
        for z_tap in range(3):
            columns = []
            for number in range(tiles):
                region = regions[number][left]
                inset = (region.z_size - TE) // 2 - 1
                shifted = [
                    region.tile_rows(inset + z_tap, inset + y_tap, 3 * channels, 0, TE) for y_tap in range(3)
                ]
                columns.append(jnp.concatenate(shifted, axis=1))
            product = jnp.dot(flipped, jnp.concatenate(columns, axis=0), preferred_element_type=F32)
            for y_tap in range(3):
                for x_tap in range(3):
                    lane = (y_tap * 3 + x_tap) * channels
                    row = (z_tap * 9 + x_tap * 3 + y_tap) * channels
                    grad_rows[row : row + channels] = product[:, lane : lane + channels].T
        y_parts, z_parts, _, padded, _ = kept.shape
        share = 27 * channels // (y_parts * z_parts * block_count)
        for y_at in range(y_parts):
            for z_at in range(z_parts):
                column = (z_at * y_parts + y_at) * block_count
                for out, owner in ((kept, me), (given, me ^ 1)):
                    rows = grad_rows[pl.ds((column + owner) * share, padded)]
                    out[y_at, z_at, at] = rows.astype(BF)

    grad_rows[27 * channels :] = jnp.zeros_like(grad_rows[27 * channels :])
    fetches[1].wait()
    for number in range(tiles):
        convolve_region(regions[number][0], first_kernel, False, result)
        finish_layer(number, 1, "act")
    fetches[2].wait()
    for number in range(tiles):
        convolve_region(regions[number][1], second_kernel, False, result)
        finish_layer(number, 2, "delta_two")
    kernel_gradient(1, 1, 2)
    for number in range(tiles):
        convolve_region(regions[number][2], second_kernel, True, result)
        finish_layer(number, 3, "delta_one")
    kernel_gradient(0, 0, 3)
    convolve_region(regions[0][3], first_kernel, True, result)
    for pair in range(TE // 2):
        for parity in range(2):
            value = result[0 : TE // 2, pair, :, parity * channels : (parity + 1) * channels] * alive[0]
            value = value.reshape(TE, TE, channels)
            for z_at in range(TE):
                lifted[pl.ds(z_at * TE * TE + 2 * pair + parity, TE, stride=TE)] = value[z_at]
    input_grad[...] = lifted[...].astype(BF)


def backward_call(own, rims, kernels, depth_at, columns, positions, tiles):
    channels = own[0].shape[-1]
    voxels = TE * TE * TE
    planes = positions * TE + 2 * HALO
    span = TE + 2 * HALO
    inner = span // 2 - 1
    padded = -(-(27 * channels // (columns * len(own))) // 16) * 16
    scratch = [
        pltpu.VMEM((planes, span, TE, channels), F32),
        pltpu.VMEM((planes, span, TE, channels), F32),
        pltpu.VMEM((3, planes, TE, channels), F32),
        pltpu.VMEM((voxels, channels), F32),
        pltpu.VMEM((inner, inner, 2 * TE, 2 * channels), F32),
        pltpu.VMEM((27 * channels + 16, channels), F32),
        pltpu.VMEM((27, channels, channels), BF),
        pltpu.VMEM((27, channels, channels), BF),
        pltpu.VMEM(own[0].shape, BF),
        pltpu.SemaphoreType.DMA((3,)),
    ]
    for number in range(tiles):
        for layer in range(4):
            size = span - 2 * (number + layer)
            scratch += region_shapes(size, size, TE, channels, size > TE)
    for number in range(tiles):
        size = span - 2 * (number + 1)
        scratch.append(pltpu.VMEM((size, size // 2, 2, TE, channels), F32))
    vmem = pl.BlockSpec(memory_space=pltpu.VMEM)
    smem = pl.BlockSpec(memory_space=pltpu.SMEM)
    hbm = pl.BlockSpec(memory_space=pltpu.HBM)

    def body(*refs):
        backward_kernel(len(own), tiles, *refs)

    share = jax.ShapeDtypeStruct((2, columns // 2, 2, padded, channels), BF)
    return pl.pallas_call(
        body,
        out_shape=[jax.ShapeDtypeStruct((voxels, channels), BF), share, share],
        in_specs=[smem, hbm] + [vmem] * (2 * len(own) - 1) + [hbm, hbm],
        out_specs=[vmem] * 3,
        scratch_shapes=scratch,
        compiler_params=pltpu.CompilerParams(vmem_limit_bytes=VMEM_LIMIT),
        name="tile_backward",
    )(depth_at.reshape(1), *own, *rims, *kernels)


def on_device_line(features, cotangent, first_kernel, second_kernel, slot_tile, slot_used):
    channels = features.shape[3]
    depth_size, space_size = lax.axis_size("depth"), lax.axis_size("space")
    depth_at, space_at = lax.axis_index("depth"), lax.axis_index("space")

    def swap(block, axis, bits):
        return lax.ppermute(block, axis, [(i, i ^ bits) for i in range(lax.axis_size(axis))])

    to_above, to_below, own = sides_call(slot_tile, slot_used, features[0, 0], cotangent[0, 0])
    own_far = swap(own, "depth", 2)
    below, above = from_behind(to_above, "space", 1), from_behind(to_below, "space", -1)
    rim = jnp.concatenate([below, above], axis=0)
    rim_far = swap(rim, "depth", 2)

    def with_sibling(near, far):
        return [near, swap(near, "depth", 1), far, swap(far, "depth", 1)]

    input_grad, kept, given = backward_call(
        with_sibling(own, own_far),
        with_sibling(rim, rim_far),
        (first_kernel, second_kernel),
        depth_at,
        space_size,
        slot_tile.shape[1],
        2,
    )
    share = 27 * channels // (depth_size * space_size)

    def part(block, at):
        return lax.dynamic_index_in_dim(block, at, 0, keepdims=False)

    y_at, z_at = space_at % 2, space_at // 2
    column_sum = kept.astype(F32) + swap(given, "depth", 1).astype(F32)
    line = part(column_sum, y_at) + swap(part(column_sum, 1 - y_at).astype(BF), "space", 1).astype(F32)
    total = part(line, z_at)
    for step in range(1, space_size // 2):
        total = total + swap(part(line, z_at ^ step).astype(BF), "space", 2 * step).astype(F32)
    first_share, second_share = (total[at, :share].reshape(-1) for at in range(2))
    return (input_grad.reshape(features.shape), first_share, second_share)


def solution(mesh):
    line = mesh.shape["space"] == GY and mesh.shape["depth"] == 4
    run = on_device_line if line else on_device_wide
    return jax.shard_map(
        run,
        mesh=mesh,
        in_specs=(
            P("space", "depth", None, None),
            P("space", "depth", None, None),
            P(),
            P(),
            P("space", None),
            P("space", None),
        ),
        out_specs=(P("space", "depth", None, None), P(("space", "depth")), P(("space", "depth"))),
        check_vma=False,
    )
```

```python
import jax
import jax.numpy as jnp
from jax import lax
from jax.experimental import pallas as pl
from jax.experimental.pallas import tpu as pltpu
from jax.sharding import PartitionSpec as P

TE = 8
GY = 8


SLOPE_COEF = 0.7978845608028654
CUBIC_COEF = 0.044715


def from_behind(block, axis, distance):
    devices = range(lax.axis_size(axis))
    route = [(i - distance, i) for i in devices if i - distance in devices]
    return lax.ppermute(block, axis, route)


def gelu_pair(values):
    inner_arg = SLOPE_COEF * (values + CUBIC_COEF * values * values * values)
    tangent = jnp.tanh(inner_arg)
    output = 0.5 * values * (1.0 + tangent)
    derivative = 0.5 * (1.0 + tangent) + 0.5 * values * (1.0 - tangent * tangent) * SLOPE_COEF * (
        1.0 + 3.0 * CUBIC_COEF * values * values
    )
    return (output, derivative)


def gelu_slope(values):
    inner_arg = SLOPE_COEF * (values + CUBIC_COEF * values * values * values)
    tangent = jnp.tanh(inner_arg)
    return 0.5 * (1.0 + tangent) + 0.5 * values * (1.0 - tangent * tangent) * SLOPE_COEF * (
        1.0 + 3.0 * CUBIC_COEF * values * values
    )


def place_matrix(slot_tile, slot_used, position_count):
    positions = jnp.arange(position_count, dtype=jnp.int32)
    matches = (slot_tile[0][None, :] == positions[:, None]) & (slot_used[0][None, :] == 1)
    return matches.astype(jnp.bfloat16)


def dense_column(tile_rows, placement):
    summed = jnp.einsum(
        "tj,jvc->tvc",
        placement,
        lax.all_gather(tile_rows, "depth", axis=0, tiled=True),
        preferred_element_type=jnp.float32,
    )
    return summed.astype(jnp.bfloat16).reshape(-1, TE, TE, summed.shape[-1])


def extend_sides(own_block, move_face, space_index):
    y_coord = space_index % GY
    below = move_face(own_block[:, :, -1:, :], 1) * (y_coord > 0).astype(own_block.dtype)
    above = move_face(own_block[:, :, :1, :], -1) * (y_coord < GY - 1).astype(own_block.dtype)
    widened = jnp.concatenate([below, own_block, above], axis=2)
    behind = move_face(widened[:, -1:, :, :], GY)
    ahead = move_face(widened[:, :1, :, :], -GY)
    return jnp.concatenate([behind, widened, ahead], axis=1)


def pad_depth(own_block):
    return jnp.pad(own_block, ((1, 1), (0, 0), (0, 0), (0, 0)))


def windows_at(padded, positions):

    def one_window(z_index):
        return lax.dynamic_slice_in_dim(padded, z_index * TE, TE + 2, 0)

    return jax.vmap(one_window)(positions)


def unfold(windows, flipped):
    pieces = []
    for kernel_tap in range(27):
        z_step, x_step, y_step = (kernel_tap // 9, kernel_tap // 3 % 3, kernel_tap % 3)
        if flipped:
            z_step, x_step, y_step = (2 - z_step, 2 - x_step, 2 - y_step)
        pieces.append(
            windows[:, z_step : z_step + TE, x_step : x_step + TE, y_step : y_step + TE, :]
        )
    stacked = jnp.concatenate(pieces, axis=-1)
    return stacked.reshape(-1, stacked.shape[-1])


def tile_sum(columns, delta):
    return lax.dot_general(
        columns, delta, (((0,), (0,)), ((), ())), preferred_element_type=jnp.float32
    )


def on_device_wide(features, cotangent, first_kernel, second_kernel, slot_tile, slot_used):
    depth_index = lax.axis_index("depth")
    space_index = lax.axis_index("space")
    slot_count = features.shape[1]
    voxels = features.shape[2]
    channels = features.shape[3]
    position_count = slot_tile.shape[1]
    placement = place_matrix(slot_tile, slot_used, position_count)
    own_first = depth_index * slot_count
    own_tiles = lax.dynamic_slice_in_dim(slot_tile[0], own_first, slot_count, 0)
    own_used = lax.dynamic_slice_in_dim(slot_used[0], own_first, slot_count, 0).astype(jnp.float32)
    feature_slots = features[0]
    upstream_slots = cotangent[0]

    def column_move(face, offset):
        return from_behind(face, "space", offset)

    def halo_of(tile_rows):
        column = dense_column(tile_rows.reshape(slot_count, voxels, channels), placement)
        return pad_depth(extend_sides(column, column_move, space_index))

    upstream = upstream_slots.reshape(-1, channels)
    source_column = halo_of(feature_slots)
    alive_rows = jnp.repeat(own_used, voxels)[:, None]
    forward_one = first_kernel.reshape(-1, channels)
    forward_two = second_kernel.reshape(-1, channels)
    backward_one = jnp.transpose(first_kernel, (0, 2, 1)).reshape(-1, channels)
    backward_two = jnp.transpose(second_kernel, (0, 2, 1)).reshape(-1, channels)
    source_cols = unfold(windows_at(source_column, own_tiles), False)
    pre_one = jnp.dot(source_cols, forward_one, preferred_element_type=jnp.float32)
    act_value, slope_one = gelu_pair(pre_one)
    act_one = (act_value * alive_rows).astype(jnp.bfloat16)
    act_cols = unfold(windows_at(halo_of(act_one), own_tiles), False)
    pre_two = jnp.dot(act_cols, forward_two, preferred_element_type=jnp.float32)
    slope_two = gelu_slope(pre_two)
    delta_two = (upstream.astype(jnp.float32) * slope_two * alive_rows).astype(jnp.bfloat16)
    second_grad = tile_sum(act_cols, delta_two).reshape(-1) * (1.0 / voxels)
    back_one = jnp.dot(
        unfold(windows_at(halo_of(delta_two), own_tiles), True),
        backward_two,
        preferred_element_type=jnp.float32,
    )
    delta_one = (back_one * slope_one * alive_rows).astype(jnp.bfloat16)
    first_grad = tile_sum(source_cols, delta_one).reshape(-1) * (1.0 / voxels)
    back_zero = jnp.dot(
        unfold(windows_at(halo_of(delta_one), own_tiles), True),
        backward_one,
        preferred_element_type=jnp.float32,
    )
    used_rows = jnp.repeat(own_used, voxels)[:, None]
    input_grad = (back_zero * used_rows).astype(jnp.bfloat16).reshape(features.shape)
    first_share, second_share = (
        lax.psum_scatter(first_grad, ("space", "depth"), scatter_dimension=0, tiled=True),
        lax.psum_scatter(second_grad, ("space", "depth"), scatter_dimension=0, tiled=True),
    )
    return (input_grad, first_share, second_share)


HALO = 4
NEAR = 4
VMEM_LIMIT = 51 * 1024 * 1024
BF = jnp.bfloat16
F32 = jnp.float32


class Region:
    def __init__(self, even, odd, z_size, y_size):
        self.even, self.odd, self.z_size, self.y_size = even, odd, z_size, y_size

    def planes(self, first):
        return (self.odd, (first - 1) // 2) if first % 2 else (self.even, first // 2)

    def store_row(self, y_pair, y_parity, column):
        z_size, width, channels = column.shape
        place = lax.broadcasted_iota(jnp.int32, column.shape, 1)
        before = jnp.where(place == 0, 0.0, pltpu.roll(column, 1, 1))
        after = jnp.where(place == width - 1, 0.0, pltpu.roll(column, width - 1, 1))
        wide = jnp.concatenate([before, column, after], axis=-1)
        self.even[:, y_pair, y_parity] = wide.reshape(z_size // 2, 2 * width, 3 * channels).astype(BF)
        if self.odd is not None:
            inner = wide[1:-1].reshape(z_size // 2 - 1, 2 * width, 3 * channels)
            self.odd[:, y_pair, y_parity] = inner.astype(BF)

    def tile_rows(self, z_first, y_first, lanes, lane_first, edge):
        ref, q_first = self.planes(z_first)
        parts = []
        for y_at in range(y_first, y_first + edge):
            part = ref[q_first : q_first + edge // 2, y_at // 2, y_at % 2, :, lane_first : lane_first + lanes]
            parts.append(part.reshape(-1, lanes))
        return jnp.concatenate(parts, axis=0)


def region_shapes(z_size, y_size, width, channels, with_odd):
    tail = (y_size // 2, 2, 2 * width, 3 * channels)
    shapes = [pltpu.VMEM((z_size // 2,) + tail, BF)]
    if with_odd:
        shapes.append(pltpu.VMEM((z_size // 2 - 1,) + tail, BF))
    return shapes


def convolve_region(region, kernel, transposed, result):
    q_size, r_size = region.z_size // 2 - 1, region.y_size // 2 - 1
    channels = region.even.shape[-1] // 3
    pieces = []
    for block in range(9):
        z_tap, x_tap = block // 3, block % 3
        if transposed:
            z_tap, x_tap = 2 - z_tap, 2 - x_tap
        ref, q_first = region.planes(z_tap)
        for y_at in range(4):
            if transposed:
                y_at = 3 - y_at
            piece = ref[
                q_first : q_first + q_size,
                y_at // 2 : y_at // 2 + r_size,
                y_at % 2,
                :,
                x_tap * channels : (x_tap + 1) * channels,
            ]
            pieces.append(piece.reshape(-1, channels))
    left = jnp.concatenate(pieces, axis=1)
    blank = jnp.zeros((channels, channels), BF)
    blocks = []
    for block in range(9):
        taps = [kernel[block * 3 + y_tap] for y_tap in range(3)]
        for near, far in zip(*((taps + [blank], [blank] + taps) if not transposed else ([blank] + taps, taps + [blank]))):
            blocks.append(jnp.concatenate([near, far], axis=0 if transposed else 1))
    right = jnp.concatenate(blocks, axis=1 if transposed else 0)
    contract = (((1,), (1 if transposed else 0,)), ((), ()))
    product = lax.dot_general(left, right, contract, preferred_element_type=F32)
    result[0:q_size, 0:r_size] = product.reshape(q_size, r_size, product.shape[0] // (q_size * r_size), -1)


def place_slots(codes, blocks, offset, y_first, y_count, lifted, volume, mask, side):
    for code, block in zip(codes, blocks):

        @pl.when(code > 0)
        def _():
            z_first = HALO + (code - 1) * TE
            rows = TE * TE * y_count
            lifted[0:rows] = block[offset : offset + rows].astype(F32)
            for z_at in range(TE):
                for y_at in range(y_count):
                    row = z_at * TE * y_count + y_at
                    volume[z_first + z_at, y_first + y_at] = lifted[pl.ds(row, TE, stride=y_count)]
            if mask is not None:
                mask[side, pl.ds(z_first, TE)] = jnp.ones((TE,) + mask.shape[2:], F32)


def side_sizes():
    face, thin = HALO * TE * TE, 2 * TE * TE
    return face, thin, face + thin + 16


def sides_kernel(tile, used, feature_rows, upstream_rows, to_above, to_below, own_table, lifted):
    channels = feature_rows.shape[1]
    face = side_sizes()[0]
    for rows, width, offset in ((feature_rows, HALO, 0), (upstream_rows, 2, face)):
        lifted[...] = rows[...].astype(F32).reshape(lifted.shape)
        count = TE * TE * width
        to_above[offset : offset + count] = lifted[:, TE - width :].reshape(count, channels).astype(BF)
        to_below[offset : offset + count] = lifted[:, :width].reshape(count, channels).astype(BF)
    place = lax.broadcasted_iota(jnp.int32, (16, channels), 0)
    table = jnp.zeros((16, channels), F32)
    for slot in range(tile.shape[1]):
        code = jnp.where(used[0, slot] == 1, tile[0, slot] + 1, 0)
        table = jnp.where(place == slot, code.astype(F32), table)
    for out in (to_above, to_below, own_table):
        out[out.shape[0] - 16 :] = table.astype(BF)


def sides_call(slot_tile, slot_used, feature_rows, upstream_rows):
    voxels, channels = feature_rows.shape
    smem = pl.BlockSpec(memory_space=pltpu.SMEM)
    vmem = pl.BlockSpec(memory_space=pltpu.VMEM)
    side = jax.ShapeDtypeStruct((side_sizes()[2], channels), BF)
    return pl.pallas_call(
        sides_kernel,
        out_shape=[side, side, jax.ShapeDtypeStruct((16, channels), BF)],
        in_specs=[smem, smem, vmem, vmem],
        out_specs=[vmem] * 3,
        scratch_shapes=[pltpu.VMEM((TE * TE, TE, channels), F32)],
        name="pack_sides",
    )(slot_tile, slot_used, feature_rows, upstream_rows)


def backward_kernel(block_count, tiles, depth_ref, *refs):
    own, up, below, above = (list(refs[at * block_count : (at + 1) * block_count]) for at in range(4))
    own_table, far_first, far_second, input_grad, kept, given = refs[4 * block_count : 4 * block_count + 6]
    rest = list(refs[4 * block_count + 6 :])
    channels = own[0].shape[-1]

    def take():
        return rest.pop(0)

    volume, upstream, mask, lifted, result, grad_rows, first_kernel, second_kernel, near_own, near_up, sems = (
        take() for _ in range(11)
    )
    fetches = [
        pltpu.make_async_copy(far, near, sems.at[at])
        for at, (far, near) in enumerate(
            ((own[0], near_own), (up[0], near_up), (far_first, first_kernel), (far_second, second_kernel))
        )
    ]
    for fetch in fetches:
        fetch.start()
    own[0], up[0] = near_own, near_up
    regions = []
    for number in range(tiles):
        halo = HALO - number
        group = []
        for layer in range(4):
            size = TE + 2 * (halo - layer)
            even = take()
            odd = take() if size > TE else None
            group.append(Region(even, odd, size, size))
        regions.append(group)
    slopes = [take() for _ in range(tiles)]

    me = depth_ref[0]
    slots = [me ^ block for block in range(block_count)]
    voxels = TE * TE * TE
    volume[...] = jnp.zeros_like(volume)
    upstream[...] = jnp.zeros_like(upstream)
    mask[...] = jnp.zeros_like(mask)
    face, thin, _ = side_sizes()

    def table_at(block, first):
        table = block[first : first + 16].astype(F32)
        place = lax.broadcasted_iota(jnp.int32, table.shape, 0)
        return [jnp.max(jnp.where(place == slot, table, 0.0)).astype(jnp.int32) for slot in slots]

    held = table_at(own_table, 0)
    codes = table_at(below[0], face + thin)
    place_slots(codes, below, 0, 0, HALO, lifted, volume, mask, 0)
    place_slots(codes, below, face, HALO - 2, 2, lifted, upstream, None, 0)
    codes = table_at(above[0], face + thin)
    place_slots(codes, above, 0, HALO + TE, HALO, lifted, volume, mask, 2)
    place_slots(codes, above, face, HALO + TE, 2, lifted, upstream, None, 2)

    fetches[0].wait()
    place_slots(held, own, 0, HALO, TE, lifted, volume, mask, 1)
    fetches[1].wait()
    place_slots(held, up, 0, HALO, TE, lifted, upstream, None, 1)

    starts = []
    alive = []
    for number in range(tiles):
        starts.append(jnp.maximum(held[2 * number] - 1, 0) * TE)
        alive.append((held[2 * number] > 0).astype(F32))

    for number in range(tiles):
        source = regions[number][0]
        z_first = starts[number] + number

        for pair in range(source.y_size // 2):
            for parity in range(2):
                source.store_row(pair, parity, volume[pl.ds(z_first, source.z_size), number + 2 * pair + parity])

    def finish_layer(number, layer, kind):
        region = regions[number][layer]
        inset = number + layer
        z_first = starts[number] + inset
        q_size = region.z_size // 2

        for pair in range(region.y_size // 2):
            for parity in range(2):
                y_at = inset + 2 * pair + parity
                side = (y_at >= HALO) + (y_at >= HALO + TE)
                window = pl.ds(z_first, region.z_size)
                keep = mask[side, window]
                value = result[0:q_size, pair, :, parity * channels : (parity + 1) * channels]
                value = value.reshape(keep.shape)
                if kind == "act":
                    out, slope = gelu_pair(value)
                    slopes[number][:, pair, parity] = slope * keep
                    out = out * keep
                elif kind == "delta_two":
                    out = upstream[window, y_at] * gelu_slope(value) * keep
                else:
                    out = value * slopes[number][2 : 2 + region.z_size, pair + 1, parity]
                region.store_row(pair, parity, out)

    def kernel_gradient(at, left, delta):
        flipped = []
        for number in range(tiles):
            region = regions[number][delta]
            inset = (region.z_size - TE) // 2
            rows = region.tile_rows(inset, inset, channels, channels, TE).astype(F32) * (alive[number] * (1.0 / voxels))
            flipped.append(rows.T.astype(BF))
        flipped = jnp.concatenate(flipped, axis=1)
        for z_tap in range(3):
            columns = []
            for number in range(tiles):
                region = regions[number][left]
                inset = (region.z_size - TE) // 2 - 1
                shifted = [
                    region.tile_rows(inset + z_tap, inset + y_tap, 3 * channels, 0, TE) for y_tap in range(3)
                ]
                columns.append(jnp.concatenate(shifted, axis=1))
            product = jnp.dot(flipped, jnp.concatenate(columns, axis=0), preferred_element_type=F32)
            for y_tap in range(3):
                for x_tap in range(3):
                    lane = (y_tap * 3 + x_tap) * channels
                    row = (z_tap * 9 + x_tap * 3 + y_tap) * channels
                    grad_rows[row : row + channels] = product[:, lane : lane + channels].T
        near_parts, far_parts, _, padded, _ = kept.shape
        share = 27 * channels // (near_parts * far_parts * block_count)
        for near_at in range(near_parts):
            for far_at in range(far_parts):
                column = (far_at * near_parts + near_at) * block_count
                for out, owner in ((kept, me), (given, me ^ 1)):
                    rows = grad_rows[pl.ds((column + owner) * share, padded)]
                    out[near_at, far_at, at] = rows.astype(BF)

    grad_rows[27 * channels :] = jnp.zeros_like(grad_rows[27 * channels :])
    fetches[2].wait()
    for number in range(tiles):
        convolve_region(regions[number][0], first_kernel, False, result)
        finish_layer(number, 1, "act")
    fetches[3].wait()
    for number in range(tiles):
        convolve_region(regions[number][1], second_kernel, False, result)
        finish_layer(number, 2, "delta_two")
    kernel_gradient(1, 1, 2)
    for number in range(tiles):
        convolve_region(regions[number][2], second_kernel, True, result)
        finish_layer(number, 3, "delta_one")
    kernel_gradient(0, 0, 3)
    convolve_region(regions[0][3], first_kernel, True, result)
    for pair in range(TE // 2):
        for parity in range(2):
            value = result[0 : TE // 2, pair, :, parity * channels : (parity + 1) * channels] * alive[0]
            value = value.reshape(TE, TE, channels)
            for z_at in range(TE):
                lifted[pl.ds(z_at * TE * TE + 2 * pair + parity, TE, stride=TE)] = value[z_at]
    input_grad[...] = lifted[0:voxels].astype(BF)


def backward_call(own, up, below, above, own_table, kernels, depth_at, columns, positions, tiles):
    channels = own[0].shape[-1]
    voxels = TE * TE * TE
    planes = positions * TE + 2 * HALO
    span = TE + 2 * HALO
    inner = span // 2 - 1
    padded = -(-(27 * channels // (columns * len(own))) // 16) * 16
    scratch = [
        pltpu.VMEM((planes, span, TE, channels), F32),
        pltpu.VMEM((planes, span, TE, channels), F32),
        pltpu.VMEM((3, planes, TE, channels), F32),
        pltpu.VMEM((voxels + 16, channels), F32),
        pltpu.VMEM((inner, inner, 2 * TE, 2 * channels), F32),
        pltpu.VMEM((27 * channels + 16, channels), F32),
        pltpu.VMEM((27, channels, channels), BF),
        pltpu.VMEM((27, channels, channels), BF),
        pltpu.VMEM((voxels, channels), BF),
        pltpu.VMEM((voxels, channels), BF),
        pltpu.SemaphoreType.DMA((4,)),
    ]
    for number in range(tiles):
        for layer in range(4):
            size = span - 2 * (number + layer)
            scratch += region_shapes(size, size, TE, channels, size > TE)
    for number in range(tiles):
        size = span - 2 * (number + 1)
        scratch.append(pltpu.VMEM((size, size // 2, 2, TE, channels), F32))
    vmem = pl.BlockSpec(memory_space=pltpu.VMEM)
    smem = pl.BlockSpec(memory_space=pltpu.SMEM)
    hbm = pl.BlockSpec(memory_space=pltpu.HBM)

    def body(*refs):
        backward_kernel(len(own), tiles, *refs)

    share = jax.ShapeDtypeStruct((NEAR, columns // NEAR, 2, padded, channels), BF)
    return pl.pallas_call(
        body,
        out_shape=[jax.ShapeDtypeStruct((voxels, channels), BF), share, share],
        in_specs=[smem] + ([hbm] + [vmem] * (len(own) - 1)) * 2 + [vmem] * (len(below) + len(above) + 1) + [hbm, hbm],
        out_specs=[vmem] * 3,
        scratch_shapes=scratch,
        compiler_params=pltpu.CompilerParams(vmem_limit_bytes=VMEM_LIMIT),
        name="tile_backward",
    )(depth_at.reshape(1), *own, *up, *below, *above, own_table, *kernels)


def on_device_line(features, cotangent, first_kernel, second_kernel, slot_tile, slot_used):
    channels = features.shape[3]
    depth_size, space_size = lax.axis_size("depth"), lax.axis_size("space")
    depth_at, space_at = lax.axis_index("depth"), lax.axis_index("space")

    def swap(block, axis, bits):
        return lax.ppermute(block, axis, [(i, i ^ bits) for i in range(lax.axis_size(axis))])

    own, up = features[0, 0], cotangent[0, 0]
    own_far, up_far = swap(own, "depth", 2), swap(up, "depth", 2)
    to_above, to_below, own_table = sides_call(slot_tile, slot_used, own, up)
    to_below, own_far = lax.optimization_barrier((to_below, own_far))
    below, above = from_behind(to_above, "space", 1), from_behind(to_below, "space", -1)
    below_far, above_far = swap(below, "depth", 2), swap(above, "depth", 2)

    def with_sibling(near, far):
        return [near, swap(near, "depth", 1), far, swap(far, "depth", 1)]

    input_grad, kept, given = backward_call(
        with_sibling(own, own_far),
        with_sibling(up, up_far),
        with_sibling(below, below_far),
        with_sibling(above, above_far),
        own_table,
        (first_kernel, second_kernel),
        depth_at,
        space_size,
        slot_tile.shape[1],
        2,
    )
    share = 27 * channels // (depth_size * space_size)

    def part(block, at):
        return lax.dynamic_index_in_dim(block, at, 0, keepdims=False)

    near_at, far_at = space_at % NEAR, space_at // NEAR
    column_sum = kept.astype(F32) + swap(given, "depth", 1).astype(F32)
    group = part(column_sum, near_at)
    for step in range(1, NEAR):
        group = group + swap(part(column_sum, near_at ^ step).astype(BF), "space", step).astype(F32)
    total = part(group, far_at)
    for step in range(1, space_size // NEAR):
        total = total + swap(part(group, far_at ^ step).astype(BF), "space", NEAR * step).astype(F32)
    first_share, second_share = (total[at, :share].reshape(-1) for at in range(2))
    return (input_grad.reshape(features.shape), first_share, second_share)


def solution(mesh):
    line = mesh.shape["space"] == GY and mesh.shape["depth"] == 4
    run = on_device_line if line else on_device_wide
    return jax.shard_map(
        run,
        mesh=mesh,
        in_specs=(
            P("space", "depth", None, None),
            P("space", "depth", None, None),
            P(),
            P(),
            P("space", None),
            P("space", None),
        ),
        out_specs=(P("space", "depth", None, None), P(("space", "depth")), P(("space", "depth"))),
        check_vma=False,
    )
```

```python
import jax
import jax.numpy as jnp
from jax import lax
from jax.experimental import pallas as pl
from jax.experimental.pallas import tpu as pltpu
from jax.sharding import PartitionSpec as P

TE = 8
GY = 8


SLOPE_COEF = 0.7978845608028654
CUBIC_COEF = 0.044715


def from_behind(block, axis, distance):
    devices = range(lax.axis_size(axis))
    route = [(i - distance, i) for i in devices if i - distance in devices]
    return lax.ppermute(block, axis, route)


def gelu_pair(values):
    inner_arg = SLOPE_COEF * (values + CUBIC_COEF * values * values * values)
    tangent = jnp.tanh(inner_arg)
    output = 0.5 * values * (1.0 + tangent)
    derivative = 0.5 * (1.0 + tangent) + 0.5 * values * (1.0 - tangent * tangent) * SLOPE_COEF * (
        1.0 + 3.0 * CUBIC_COEF * values * values
    )
    return (output, derivative)


def gelu_slope(values):
    inner_arg = SLOPE_COEF * (values + CUBIC_COEF * values * values * values)
    tangent = jnp.tanh(inner_arg)
    return 0.5 * (1.0 + tangent) + 0.5 * values * (1.0 - tangent * tangent) * SLOPE_COEF * (
        1.0 + 3.0 * CUBIC_COEF * values * values
    )


def place_matrix(slot_tile, slot_used, position_count):
    positions = jnp.arange(position_count, dtype=jnp.int32)
    matches = (slot_tile[0][None, :] == positions[:, None]) & (slot_used[0][None, :] == 1)
    return matches.astype(jnp.bfloat16)


def dense_column(tile_rows, placement):
    summed = jnp.einsum(
        "tj,jvc->tvc",
        placement,
        lax.all_gather(tile_rows, "depth", axis=0, tiled=True),
        preferred_element_type=jnp.float32,
    )
    return summed.astype(jnp.bfloat16).reshape(-1, TE, TE, summed.shape[-1])


def extend_sides(own_block, move_face, space_index):
    y_coord = space_index % GY
    below = move_face(own_block[:, :, -1:, :], 1) * (y_coord > 0).astype(own_block.dtype)
    above = move_face(own_block[:, :, :1, :], -1) * (y_coord < GY - 1).astype(own_block.dtype)
    widened = jnp.concatenate([below, own_block, above], axis=2)
    behind = move_face(widened[:, -1:, :, :], GY)
    ahead = move_face(widened[:, :1, :, :], -GY)
    return jnp.concatenate([behind, widened, ahead], axis=1)


def pad_depth(own_block):
    return jnp.pad(own_block, ((1, 1), (0, 0), (0, 0), (0, 0)))


def windows_at(padded, positions):

    def one_window(z_index):
        return lax.dynamic_slice_in_dim(padded, z_index * TE, TE + 2, 0)

    return jax.vmap(one_window)(positions)


def unfold(windows, flipped):
    pieces = []
    for kernel_tap in range(27):
        z_step, x_step, y_step = (kernel_tap // 9, kernel_tap // 3 % 3, kernel_tap % 3)
        if flipped:
            z_step, x_step, y_step = (2 - z_step, 2 - x_step, 2 - y_step)
        pieces.append(
            windows[:, z_step : z_step + TE, x_step : x_step + TE, y_step : y_step + TE, :]
        )
    stacked = jnp.concatenate(pieces, axis=-1)
    return stacked.reshape(-1, stacked.shape[-1])


def tile_sum(columns, delta):
    return lax.dot_general(
        columns, delta, (((0,), (0,)), ((), ())), preferred_element_type=jnp.float32
    )


def on_device_wide(features, cotangent, first_kernel, second_kernel, slot_tile, slot_used):
    depth_index = lax.axis_index("depth")
    space_index = lax.axis_index("space")
    slot_count = features.shape[1]
    voxels = features.shape[2]
    channels = features.shape[3]
    position_count = slot_tile.shape[1]
    placement = place_matrix(slot_tile, slot_used, position_count)
    own_first = depth_index * slot_count
    own_tiles = lax.dynamic_slice_in_dim(slot_tile[0], own_first, slot_count, 0)
    own_used = lax.dynamic_slice_in_dim(slot_used[0], own_first, slot_count, 0).astype(jnp.float32)
    feature_slots = features[0]
    upstream_slots = cotangent[0]

    def column_move(face, offset):
        return from_behind(face, "space", offset)

    def halo_of(tile_rows):
        column = dense_column(tile_rows.reshape(slot_count, voxels, channels), placement)
        return pad_depth(extend_sides(column, column_move, space_index))

    upstream = upstream_slots.reshape(-1, channels)
    source_column = halo_of(feature_slots)
    alive_rows = jnp.repeat(own_used, voxels)[:, None]
    forward_one = first_kernel.reshape(-1, channels)
    forward_two = second_kernel.reshape(-1, channels)
    backward_one = jnp.transpose(first_kernel, (0, 2, 1)).reshape(-1, channels)
    backward_two = jnp.transpose(second_kernel, (0, 2, 1)).reshape(-1, channels)
    source_cols = unfold(windows_at(source_column, own_tiles), False)
    pre_one = jnp.dot(source_cols, forward_one, preferred_element_type=jnp.float32)
    act_value, slope_one = gelu_pair(pre_one)
    act_one = (act_value * alive_rows).astype(jnp.bfloat16)
    act_cols = unfold(windows_at(halo_of(act_one), own_tiles), False)
    pre_two = jnp.dot(act_cols, forward_two, preferred_element_type=jnp.float32)
    slope_two = gelu_slope(pre_two)
    delta_two = (upstream.astype(jnp.float32) * slope_two * alive_rows).astype(jnp.bfloat16)
    second_grad = tile_sum(act_cols, delta_two).reshape(-1) * (1.0 / voxels)
    back_one = jnp.dot(
        unfold(windows_at(halo_of(delta_two), own_tiles), True),
        backward_two,
        preferred_element_type=jnp.float32,
    )
    delta_one = (back_one * slope_one * alive_rows).astype(jnp.bfloat16)
    first_grad = tile_sum(source_cols, delta_one).reshape(-1) * (1.0 / voxels)
    back_zero = jnp.dot(
        unfold(windows_at(halo_of(delta_one), own_tiles), True),
        backward_one,
        preferred_element_type=jnp.float32,
    )
    used_rows = jnp.repeat(own_used, voxels)[:, None]
    input_grad = (back_zero * used_rows).astype(jnp.bfloat16).reshape(features.shape)
    first_share, second_share = (
        lax.psum_scatter(first_grad, ("space", "depth"), scatter_dimension=0, tiled=True),
        lax.psum_scatter(second_grad, ("space", "depth"), scatter_dimension=0, tiled=True),
    )
    return (input_grad, first_share, second_share)


HALO = 4
NEAR = 4
INPUT_VMEM = 16 * 1024 * 1024
VMEM_LIMIT = 51 * 1024 * 1024
BF = jnp.bfloat16
F32 = jnp.float32


class Region:
    def __init__(self, even, odd, z_size, y_size):
        self.even, self.odd, self.z_size, self.y_size = even, odd, z_size, y_size

    def planes(self, first):
        return (self.odd, (first - 1) // 2) if first % 2 else (self.even, first // 2)

    def store_row(self, y_pair, y_parity, column):
        z_size, width, channels = column.shape
        place = lax.broadcasted_iota(jnp.int32, column.shape, 1)
        before = jnp.where(place == 0, 0.0, pltpu.roll(column, 1, 1))
        after = jnp.where(place == width - 1, 0.0, pltpu.roll(column, width - 1, 1))
        wide = jnp.concatenate([before, column, after], axis=-1)
        self.even[:, y_pair, y_parity] = wide.reshape(z_size // 2, 2 * width, 3 * channels).astype(BF)
        if self.odd is not None:
            inner = wide[1:-1].reshape(z_size // 2 - 1, 2 * width, 3 * channels)
            self.odd[:, y_pair, y_parity] = inner.astype(BF)

    def tile_rows(self, z_first, y_first, lanes, lane_first, edge):
        ref, q_first = self.planes(z_first)
        parts = []
        for y_at in range(y_first, y_first + edge):
            part = ref[q_first : q_first + edge // 2, y_at // 2, y_at % 2, :, lane_first : lane_first + lanes]
            parts.append(part.reshape(-1, lanes))
        return jnp.concatenate(parts, axis=0)


def region_shapes(z_size, y_size, width, channels, with_odd):
    tail = (y_size // 2, 2, 2 * width, 3 * channels)
    shapes = [pltpu.VMEM((z_size // 2,) + tail, BF)]
    if with_odd:
        shapes.append(pltpu.VMEM((z_size // 2 - 1,) + tail, BF))
    return shapes


def convolve_region(region, kernel, transposed, result):
    q_size, r_size = region.z_size // 2 - 1, region.y_size // 2 - 1
    channels = region.even.shape[-1] // 3
    pieces = []
    for block in range(9):
        z_tap, x_tap = block // 3, block % 3
        if transposed:
            z_tap, x_tap = 2 - z_tap, 2 - x_tap
        ref, q_first = region.planes(z_tap)
        for y_at in range(4):
            if transposed:
                y_at = 3 - y_at
            piece = ref[
                q_first : q_first + q_size,
                y_at // 2 : y_at // 2 + r_size,
                y_at % 2,
                :,
                x_tap * channels : (x_tap + 1) * channels,
            ]
            pieces.append(piece.reshape(-1, channels))
    left = jnp.concatenate(pieces, axis=1)
    blank = jnp.zeros((channels, channels), BF)
    blocks = []
    for block in range(9):
        taps = [kernel[block * 3 + y_tap] for y_tap in range(3)]
        for near, far in zip(*((taps + [blank], [blank] + taps) if not transposed else ([blank] + taps, taps + [blank]))):
            blocks.append(jnp.concatenate([near, far], axis=0 if transposed else 1))
    right = jnp.concatenate(blocks, axis=1 if transposed else 0)
    contract = (((1,), (1 if transposed else 0,)), ((), ()))
    product = lax.dot_general(left, right, contract, preferred_element_type=F32)
    result[0:q_size, 0:r_size] = product.reshape(q_size, r_size, product.shape[0] // (q_size * r_size), -1)


def place_slots(codes, blocks, offset, y_first, y_count, lifted, volume, mask, side):
    for code, block in zip(codes, blocks):

        @pl.when(code > 0)
        def _():
            z_first = HALO + (code - 1) * TE
            rows = TE * TE * y_count
            lifted[0:rows] = block[offset : offset + rows].astype(F32)
            for z_at in range(TE):
                for y_at in range(y_count):
                    row = z_at * TE * y_count + y_at
                    volume[z_first + z_at, y_first + y_at] = lifted[pl.ds(row, TE, stride=y_count)]
            if mask is not None:
                mask[side, pl.ds(z_first, TE)] = jnp.ones((TE,) + mask.shape[2:], F32)


def side_sizes():
    face, thin = HALO * TE * TE, 2 * TE * TE
    return face, thin, face + thin + 16


def sides_kernel(tile, used, feature_rows, upstream_rows, to_above, to_below, own_table, lifted):
    channels = feature_rows.shape[1]
    face = side_sizes()[0]
    for rows, width, offset in ((feature_rows, HALO, 0), (upstream_rows, 2, face)):
        lifted[...] = rows[...].astype(F32).reshape(lifted.shape)
        count = TE * TE * width
        to_above[offset : offset + count] = lifted[:, TE - width :].reshape(count, channels).astype(BF)
        to_below[offset : offset + count] = lifted[:, :width].reshape(count, channels).astype(BF)
    place = lax.broadcasted_iota(jnp.int32, (16, channels), 0)
    table = jnp.zeros((16, channels), F32)
    for slot in range(tile.shape[1]):
        code = jnp.where(used[0, slot] == 1, tile[0, slot] + 1, 0)
        table = jnp.where(place == slot, code.astype(F32), table)
    for out in (to_above, to_below, own_table):
        out[out.shape[0] - 16 :] = table.astype(BF)


def sides_call(slot_tile, slot_used, feature_rows, upstream_rows):
    voxels, channels = feature_rows.shape
    smem = pl.BlockSpec(memory_space=pltpu.SMEM)
    vmem = pl.BlockSpec(memory_space=pltpu.VMEM)
    side = jax.ShapeDtypeStruct((side_sizes()[2], channels), BF)
    return pl.pallas_call(
        sides_kernel,
        out_shape=[side, side, jax.ShapeDtypeStruct((16, channels), BF)],
        in_specs=[smem, smem, vmem, vmem],
        out_specs=[vmem] * 3,
        scratch_shapes=[pltpu.VMEM((TE * TE, TE, channels), F32)],
        name="pack_sides",
    )(slot_tile, slot_used, feature_rows, upstream_rows)


def table_at(block, first, slots):
    table = block[first : first + 16].astype(F32)
    place = lax.broadcasted_iota(jnp.int32, table.shape, 0)
    return [jnp.max(jnp.where(place == slot, table, 0.0)).astype(jnp.int32) for slot in slots]


def backward_kernel(block_count, tiles, depth_ref, *refs):
    own, up, below, above = (list(refs[at * block_count : (at + 1) * block_count]) for at in range(4))
    own_table, far_first, far_second, last, kept, given = refs[4 * block_count : 4 * block_count + 6]
    rest = list(refs[4 * block_count + 6 :])
    channels = own[0].shape[-1]

    def take():
        return rest.pop(0)

    volume, upstream, mask, lifted, result, grad_rows, first_kernel, second_kernel, near_own, near_up, sems = (
        take() for _ in range(11)
    )
    fetches = [
        pltpu.make_async_copy(far, near, sems.at[at])
        for at, (far, near) in enumerate(
            ((own[0], near_own), (up[0], near_up), (far_first, first_kernel), (far_second, second_kernel))
        )
    ]
    for fetch in fetches:
        fetch.start()
    own[0], up[0] = near_own, near_up
    regions = []
    for number in range(tiles):
        halo = HALO - number
        group = []
        for layer in range(4):
            size = TE + 2 * (halo - layer)
            even = take()
            odd = take() if size > TE else None
            group.append(Region(even, odd, size, size))
        regions.append(group)
    slopes = [take() for _ in range(tiles)]

    me = depth_ref[0]
    slots = [me ^ block for block in range(block_count)]
    voxels = TE * TE * TE
    volume[...] = jnp.zeros_like(volume)
    upstream[...] = jnp.zeros_like(upstream)
    mask[...] = jnp.zeros_like(mask)
    face, thin, _ = side_sizes()

    held = table_at(own_table, 0, slots)
    codes = table_at(below[0], face + thin, slots)
    place_slots(codes, below, 0, 0, HALO, lifted, volume, mask, 0)
    place_slots(codes, below, face, HALO - 2, 2, lifted, upstream, None, 0)
    codes = table_at(above[0], face + thin, slots)
    place_slots(codes, above, 0, HALO + TE, HALO, lifted, volume, mask, 2)
    place_slots(codes, above, face, HALO + TE, 2, lifted, upstream, None, 2)

    fetches[0].wait()
    place_slots(held, own, 0, HALO, TE, lifted, volume, mask, 1)
    fetches[1].wait()
    place_slots(held, up, 0, HALO, TE, lifted, upstream, None, 1)

    starts = []
    alive = []
    for number in range(tiles):
        starts.append(jnp.maximum(held[2 * number] - 1, 0) * TE)
        alive.append((held[2 * number] > 0).astype(F32))

    for number in range(tiles):
        source = regions[number][0]
        z_first = starts[number] + number

        for pair in range(source.y_size // 2):
            for parity in range(2):
                source.store_row(pair, parity, volume[pl.ds(z_first, source.z_size), number + 2 * pair + parity])

    def finish_layer(number, layer, kind):
        region = regions[number][layer]
        inset = number + layer
        z_first = starts[number] + inset
        q_size = region.z_size // 2

        for pair in range(region.y_size // 2):
            for parity in range(2):
                y_at = inset + 2 * pair + parity
                side = (y_at >= HALO) + (y_at >= HALO + TE)
                window = pl.ds(z_first, region.z_size)
                keep = mask[side, window]
                value = result[0:q_size, pair, :, parity * channels : (parity + 1) * channels]
                value = value.reshape(keep.shape)
                if kind == "act":
                    out, slope = gelu_pair(value)
                    slopes[number][:, pair, parity] = slope * keep
                    out = out * keep
                elif kind == "delta_two":
                    out = upstream[window, y_at] * gelu_slope(value) * keep
                else:
                    out = value * slopes[number][2 : 2 + region.z_size, pair + 1, parity]
                region.store_row(pair, parity, out)

    def kernel_gradient(at, left, delta):
        flipped = []
        for number in range(tiles):
            region = regions[number][delta]
            inset = (region.z_size - TE) // 2
            rows = region.tile_rows(inset, inset, channels, channels, TE).astype(F32) * (alive[number] * (1.0 / voxels))
            flipped.append(rows.T.astype(BF))
        flipped = jnp.concatenate(flipped, axis=1)
        for z_tap in range(3):
            columns = []
            for number in range(tiles):
                region = regions[number][left]
                inset = (region.z_size - TE) // 2 - 1
                shifted = [
                    region.tile_rows(inset + z_tap, inset + y_tap, 3 * channels, 0, TE) for y_tap in range(3)
                ]
                columns.append(jnp.concatenate(shifted, axis=1))
            product = jnp.dot(flipped, jnp.concatenate(columns, axis=0), preferred_element_type=F32)
            for y_tap in range(3):
                for x_tap in range(3):
                    lane = (y_tap * 3 + x_tap) * channels
                    row = (z_tap * 9 + x_tap * 3 + y_tap) * channels
                    grad_rows[row : row + channels] = product[:, lane : lane + channels].T
        near_parts, far_parts, _, padded, _ = kept.shape
        share = 27 * channels // (near_parts * far_parts * block_count)
        for near_at in range(near_parts):
            for far_at in range(far_parts):
                column = (far_at * near_parts + near_at) * block_count
                for out, owner in ((kept, me), (given, me ^ 1)):
                    rows = grad_rows[pl.ds((column + owner) * share, padded)]
                    out[near_at, far_at, at] = rows.astype(BF)

    grad_rows[27 * channels :] = jnp.zeros_like(grad_rows[27 * channels :])
    fetches[2].wait()
    for number in range(tiles):
        convolve_region(regions[number][0], first_kernel, False, result)
        finish_layer(number, 1, "act")
    fetches[3].wait()
    for number in range(tiles):
        convolve_region(regions[number][1], second_kernel, False, result)
        finish_layer(number, 2, "delta_two")
    kernel_gradient(1, 1, 2)
    for number in range(tiles):
        convolve_region(regions[number][2], second_kernel, True, result)
        finish_layer(number, 3, "delta_one")
    last[...] = regions[0][3].even[:, :, :, :, channels : 2 * channels]
    kernel_gradient(0, 0, 3)


def input_kernel(depth_ref, own_table, last, far_first, input_grad, even, odd, lifted, result, first_kernel, sem):
    fetch = pltpu.make_async_copy(far_first, first_kernel, sem.at[0])
    fetch.start()
    (held,) = table_at(own_table, 0, [depth_ref[0]])
    alive = (held > 0).astype(F32)
    channels = input_grad.shape[-1]
    region = Region(even, odd, TE + 2, TE + 2)
    for pair in range(region.y_size // 2):
        for parity in range(2):
            column = last[:, pair, parity].astype(F32)
            region.store_row(pair, parity, column.reshape(region.z_size, TE, channels))
    fetch.wait()
    convolve_region(region, first_kernel, True, result)
    for pair in range(TE // 2):
        for parity in range(2):
            value = result[:, pair, :, parity * channels : (parity + 1) * channels] * alive
            value = value.reshape(TE, TE, channels)
            for z_at in range(TE):
                lifted[pl.ds(z_at * TE * TE + 2 * pair + parity, TE, stride=TE)] = value[z_at]
    input_grad[...] = lifted[0 : input_grad.shape[0]].astype(BF)


def input_call(depth_at, own_table, last, first_kernel):
    channels = first_kernel.shape[-1]
    voxels = TE * TE * TE
    vmem = pl.BlockSpec(memory_space=pltpu.VMEM)
    return pl.pallas_call(
        input_kernel,
        out_shape=jax.ShapeDtypeStruct((voxels, channels), BF),
        in_specs=[
            pl.BlockSpec(memory_space=pltpu.SMEM),
            vmem,
            vmem,
            pl.BlockSpec(memory_space=pltpu.HBM),
        ],
        out_specs=vmem,
        scratch_shapes=region_shapes(TE + 2, TE + 2, TE, channels, True)
        + [
            pltpu.VMEM((voxels + 16, channels), F32),
            pltpu.VMEM((TE // 2, TE // 2, 2 * TE, 2 * channels), F32),
            pltpu.VMEM((27, channels, channels), BF),
            pltpu.SemaphoreType.DMA((1,)),
        ],
        compiler_params=pltpu.CompilerParams(vmem_limit_bytes=INPUT_VMEM),
        cost_estimate=pl.CostEstimate(
            flops=2 * 36 * voxels * channels * channels,
            bytes_accessed=2 * 27 * channels * channels + 8 * voxels * channels,
            transcendentals=0,
        ),
        name="input_gradient",
    )(depth_at.reshape(1), own_table, last, first_kernel)


def backward_call(own, up, below, above, own_table, kernels, depth_at, columns, positions, tiles):
    channels = own[0].shape[-1]
    voxels = TE * TE * TE
    planes = positions * TE + 2 * HALO
    span = TE + 2 * HALO
    inner = span // 2 - 1
    padded = -(-(27 * channels // (columns * len(own))) // 16) * 16
    scratch = [
        pltpu.VMEM((planes, span, TE, channels), F32),
        pltpu.VMEM((planes, span, TE, channels), F32),
        pltpu.VMEM((3, planes, TE, channels), F32),
        pltpu.VMEM((voxels + 16, channels), F32),
        pltpu.VMEM((inner, inner, 2 * TE, 2 * channels), F32),
        pltpu.VMEM((27 * channels + 16, channels), F32),
        pltpu.VMEM((27, channels, channels), BF),
        pltpu.VMEM((27, channels, channels), BF),
        pltpu.VMEM((voxels, channels), BF),
        pltpu.VMEM((voxels, channels), BF),
        pltpu.SemaphoreType.DMA((4,)),
    ]
    for number in range(tiles):
        for layer in range(4):
            size = span - 2 * (number + layer)
            scratch += region_shapes(size, size, TE, channels, size > TE)
    for number in range(tiles):
        size = span - 2 * (number + 1)
        scratch.append(pltpu.VMEM((size, size // 2, 2, TE, channels), F32))
    vmem = pl.BlockSpec(memory_space=pltpu.VMEM)
    smem = pl.BlockSpec(memory_space=pltpu.SMEM)
    hbm = pl.BlockSpec(memory_space=pltpu.HBM)

    def body(*refs):
        backward_kernel(len(own), tiles, *refs)

    last = TE + 2
    share = jax.ShapeDtypeStruct((NEAR, columns // NEAR, 2, padded, channels), BF)
    return pl.pallas_call(
        body,
        out_shape=[
            jax.ShapeDtypeStruct((last // 2, last // 2, 2, 2 * TE, channels), BF),
            share,
            share,
        ],
        in_specs=[smem] + ([hbm] + [vmem] * (len(own) - 1)) * 2 + [vmem] * (len(below) + len(above) + 1) + [hbm, hbm],
        out_specs=[vmem] * 3,
        scratch_shapes=scratch,
        compiler_params=pltpu.CompilerParams(vmem_limit_bytes=VMEM_LIMIT),
        cost_estimate=pl.CostEstimate(
            flops=40 * 27 * voxels * channels * channels,
            bytes_accessed=100 * voxels * channels,
            transcendentals=4 * voxels * channels,
        ),
        name="tile_backward",
    )(depth_at.reshape(1), *own, *up, *below, *above, own_table, *kernels)


def on_device_line(features, cotangent, first_kernel, second_kernel, slot_tile, slot_used):
    channels = features.shape[3]
    depth_size, space_size = lax.axis_size("depth"), lax.axis_size("space")
    depth_at, space_at = lax.axis_index("depth"), lax.axis_index("space")

    def swap(block, axis, bits):
        return lax.ppermute(block, axis, [(i, i ^ bits) for i in range(lax.axis_size(axis))])

    own, up = features[0, 0], cotangent[0, 0]
    own_far, up_far = swap(own, "depth", 2), swap(up, "depth", 2)
    to_above, to_below, own_table = sides_call(slot_tile, slot_used, own, up)
    to_below, own_far = lax.optimization_barrier((to_below, own_far))
    below, above = from_behind(to_above, "space", 1), from_behind(to_below, "space", -1)
    below_far, above_far = swap(below, "depth", 2), swap(above, "depth", 2)

    def with_sibling(near, far):
        return [near, swap(near, "depth", 1), far, swap(far, "depth", 1)]

    last, kept, given = backward_call(
        with_sibling(own, own_far),
        with_sibling(up, up_far),
        with_sibling(below, below_far),
        with_sibling(above, above_far),
        own_table,
        (first_kernel, second_kernel),
        depth_at,
        space_size,
        slot_tile.shape[1],
        2,
    )
    input_grad = input_call(depth_at, own_table, last, first_kernel)
    share = 27 * channels // (depth_size * space_size)

    def part(block, at):
        return lax.dynamic_index_in_dim(block, at, 0, keepdims=False)

    near_at, far_at = space_at % NEAR, space_at // NEAR
    column_sum = kept.astype(F32) + swap(given, "depth", 1).astype(F32)
    group = part(column_sum, near_at)
    for step in range(1, NEAR):
        group = group + swap(part(column_sum, near_at ^ step).astype(BF), "space", step).astype(F32)
    total = part(group, far_at)
    for step in range(1, space_size // NEAR):
        total = total + swap(part(group, far_at ^ step).astype(BF), "space", NEAR * step).astype(F32)
    first_share, second_share = (total[at, :share].reshape(-1) for at in range(2))
    return (input_grad.reshape(features.shape), first_share, second_share)


def solution(mesh):
    line = mesh.shape["space"] == GY and mesh.shape["depth"] == 4
    run = on_device_line if line else on_device_wide
    return jax.shard_map(
        run,
        mesh=mesh,
        in_specs=(
            P("space", "depth", None, None),
            P("space", "depth", None, None),
            P(),
            P(),
            P("space", None),
            P("space", None),
        ),
        out_specs=(P("space", "depth", None, None), P(("space", "depth")), P(("space", "depth"))),
        check_vma=False,
    )
```

```python
import jax
import jax.numpy as jnp
from jax import lax
from jax.experimental import pallas as pl
from jax.experimental.pallas import tpu as pltpu
from jax.sharding import PartitionSpec as P

TE = 8
GY = 8


SLOPE_COEF = 0.7978845608028654
CUBIC_COEF = 0.044715


def from_behind(block, axis, distance):
    devices = range(lax.axis_size(axis))
    route = [(i - distance, i) for i in devices if i - distance in devices]
    return lax.ppermute(block, axis, route)


def gelu_pair(values):
    inner_arg = SLOPE_COEF * (values + CUBIC_COEF * values * values * values)
    tangent = jnp.tanh(inner_arg)
    output = 0.5 * values * (1.0 + tangent)
    derivative = 0.5 * (1.0 + tangent) + 0.5 * values * (1.0 - tangent * tangent) * SLOPE_COEF * (
        1.0 + 3.0 * CUBIC_COEF * values * values
    )
    return (output, derivative)


def gelu_slope(values):
    inner_arg = SLOPE_COEF * (values + CUBIC_COEF * values * values * values)
    tangent = jnp.tanh(inner_arg)
    return 0.5 * (1.0 + tangent) + 0.5 * values * (1.0 - tangent * tangent) * SLOPE_COEF * (
        1.0 + 3.0 * CUBIC_COEF * values * values
    )


def place_matrix(slot_tile, slot_used, position_count):
    positions = jnp.arange(position_count, dtype=jnp.int32)
    matches = (slot_tile[0][None, :] == positions[:, None]) & (slot_used[0][None, :] == 1)
    return matches.astype(jnp.bfloat16)


def dense_column(tile_rows, placement):
    summed = jnp.einsum(
        "tj,jvc->tvc",
        placement,
        lax.all_gather(tile_rows, "depth", axis=0, tiled=True),
        preferred_element_type=jnp.float32,
    )
    return summed.astype(jnp.bfloat16).reshape(-1, TE, TE, summed.shape[-1])


def extend_sides(own_block, move_face, space_index):
    y_coord = space_index % GY
    below = move_face(own_block[:, :, -1:, :], 1) * (y_coord > 0).astype(own_block.dtype)
    above = move_face(own_block[:, :, :1, :], -1) * (y_coord < GY - 1).astype(own_block.dtype)
    widened = jnp.concatenate([below, own_block, above], axis=2)
    behind = move_face(widened[:, -1:, :, :], GY)
    ahead = move_face(widened[:, :1, :, :], -GY)
    return jnp.concatenate([behind, widened, ahead], axis=1)


def pad_depth(own_block):
    return jnp.pad(own_block, ((1, 1), (0, 0), (0, 0), (0, 0)))


def windows_at(padded, positions):

    def one_window(z_index):
        return lax.dynamic_slice_in_dim(padded, z_index * TE, TE + 2, 0)

    return jax.vmap(one_window)(positions)


def unfold(windows, flipped):
    pieces = []
    for kernel_tap in range(27):
        z_step, x_step, y_step = (kernel_tap // 9, kernel_tap // 3 % 3, kernel_tap % 3)
        if flipped:
            z_step, x_step, y_step = (2 - z_step, 2 - x_step, 2 - y_step)
        pieces.append(
            windows[:, z_step : z_step + TE, x_step : x_step + TE, y_step : y_step + TE, :]
        )
    stacked = jnp.concatenate(pieces, axis=-1)
    return stacked.reshape(-1, stacked.shape[-1])


def tile_sum(columns, delta):
    return lax.dot_general(
        columns, delta, (((0,), (0,)), ((), ())), preferred_element_type=jnp.float32
    )


def on_device_wide(features, cotangent, first_kernel, second_kernel, slot_tile, slot_used):
    depth_index = lax.axis_index("depth")
    space_index = lax.axis_index("space")
    slot_count = features.shape[1]
    voxels = features.shape[2]
    channels = features.shape[3]
    position_count = slot_tile.shape[1]
    placement = place_matrix(slot_tile, slot_used, position_count)
    own_first = depth_index * slot_count
    own_tiles = lax.dynamic_slice_in_dim(slot_tile[0], own_first, slot_count, 0)
    own_used = lax.dynamic_slice_in_dim(slot_used[0], own_first, slot_count, 0).astype(jnp.float32)
    feature_slots = features[0]
    upstream_slots = cotangent[0]

    def column_move(face, offset):
        return from_behind(face, "space", offset)

    def halo_of(tile_rows):
        column = dense_column(tile_rows.reshape(slot_count, voxels, channels), placement)
        return pad_depth(extend_sides(column, column_move, space_index))

    upstream = upstream_slots.reshape(-1, channels)
    source_column = halo_of(feature_slots)
    alive_rows = jnp.repeat(own_used, voxels)[:, None]
    forward_one = first_kernel.reshape(-1, channels)
    forward_two = second_kernel.reshape(-1, channels)
    backward_one = jnp.transpose(first_kernel, (0, 2, 1)).reshape(-1, channels)
    backward_two = jnp.transpose(second_kernel, (0, 2, 1)).reshape(-1, channels)
    source_cols = unfold(windows_at(source_column, own_tiles), False)
    pre_one = jnp.dot(source_cols, forward_one, preferred_element_type=jnp.float32)
    act_value, slope_one = gelu_pair(pre_one)
    act_one = (act_value * alive_rows).astype(jnp.bfloat16)
    act_cols = unfold(windows_at(halo_of(act_one), own_tiles), False)
    pre_two = jnp.dot(act_cols, forward_two, preferred_element_type=jnp.float32)
    slope_two = gelu_slope(pre_two)
    delta_two = (upstream.astype(jnp.float32) * slope_two * alive_rows).astype(jnp.bfloat16)
    second_grad = tile_sum(act_cols, delta_two).reshape(-1) * (1.0 / voxels)
    back_one = jnp.dot(
        unfold(windows_at(halo_of(delta_two), own_tiles), True),
        backward_two,
        preferred_element_type=jnp.float32,
    )
    delta_one = (back_one * slope_one * alive_rows).astype(jnp.bfloat16)
    first_grad = tile_sum(source_cols, delta_one).reshape(-1) * (1.0 / voxels)
    back_zero = jnp.dot(
        unfold(windows_at(halo_of(delta_one), own_tiles), True),
        backward_one,
        preferred_element_type=jnp.float32,
    )
    used_rows = jnp.repeat(own_used, voxels)[:, None]
    input_grad = (back_zero * used_rows).astype(jnp.bfloat16).reshape(features.shape)
    first_share, second_share = (
        lax.psum_scatter(first_grad, ("space", "depth"), scatter_dimension=0, tiled=True),
        lax.psum_scatter(second_grad, ("space", "depth"), scatter_dimension=0, tiled=True),
    )
    return (input_grad, first_share, second_share)


HALO = 4
NEAR = 4
INPUT_VMEM = 16 * 1024 * 1024
VMEM_LIMIT = 51 * 1024 * 1024
BF = jnp.bfloat16
F32 = jnp.float32


class Region:
    def __init__(self, even, odd, z_size, y_size):
        self.even, self.odd, self.z_size, self.y_size = even, odd, z_size, y_size

    def planes(self, first):
        return (self.odd, (first - 1) // 2) if first % 2 else (self.even, first // 2)

    def store_row(self, y_pair, y_parity, column):
        z_size, width, channels = column.shape
        place = lax.broadcasted_iota(jnp.int32, column.shape, 1)
        before = jnp.where(place == 0, 0.0, pltpu.roll(column, 1, 1))
        after = jnp.where(place == width - 1, 0.0, pltpu.roll(column, width - 1, 1))
        wide = jnp.concatenate([before, column, after], axis=-1)
        self.even[:, y_pair, y_parity] = wide.reshape(z_size // 2, 2 * width, 3 * channels).astype(BF)
        if self.odd is not None:
            inner = wide[1:-1].reshape(z_size // 2 - 1, 2 * width, 3 * channels)
            self.odd[:, y_pair, y_parity] = inner.astype(BF)

    def tile_rows(self, z_first, y_first, lanes, lane_first, edge):
        ref, q_first = self.planes(z_first)
        parts = []
        for y_at in range(y_first, y_first + edge):
            part = ref[q_first : q_first + edge // 2, y_at // 2, y_at % 2, :, lane_first : lane_first + lanes]
            parts.append(part.reshape(-1, lanes))
        return jnp.concatenate(parts, axis=0)


def region_shapes(z_size, y_size, width, channels, with_odd):
    tail = (y_size // 2, 2, 2 * width, 3 * channels)
    shapes = [pltpu.VMEM((z_size // 2,) + tail, BF)]
    if with_odd:
        shapes.append(pltpu.VMEM((z_size // 2 - 1,) + tail, BF))
    return shapes


def convolve_region(region, kernel, transposed, result):
    q_size, r_size = region.z_size // 2 - 1, region.y_size // 2 - 1
    channels = region.even.shape[-1] // 3
    pieces = []
    for block in range(9):
        z_tap, x_tap = block // 3, block % 3
        if transposed:
            z_tap, x_tap = 2 - z_tap, 2 - x_tap
        ref, q_first = region.planes(z_tap)
        for y_at in range(4):
            if transposed:
                y_at = 3 - y_at
            piece = ref[
                q_first : q_first + q_size,
                y_at // 2 : y_at // 2 + r_size,
                y_at % 2,
                :,
                x_tap * channels : (x_tap + 1) * channels,
            ]
            pieces.append(piece.reshape(-1, channels))
    left = jnp.concatenate(pieces, axis=1)
    blank = jnp.zeros((channels, channels), BF)
    blocks = []
    for block in range(9):
        taps = [kernel[block * 3 + y_tap] for y_tap in range(3)]
        for near, far in zip(*((taps + [blank], [blank] + taps) if not transposed else ([blank] + taps, taps + [blank]))):
            blocks.append(jnp.concatenate([near, far], axis=0 if transposed else 1))
    right = jnp.concatenate(blocks, axis=1 if transposed else 0)
    contract = (((1,), (1 if transposed else 0,)), ((), ()))
    product = lax.dot_general(left, right, contract, preferred_element_type=F32)
    result[0:q_size, 0:r_size] = product.reshape(q_size, r_size, product.shape[0] // (q_size * r_size), -1)


def place_slots(codes, blocks, offset, y_first, y_count, lifted, volume, mask, side):
    for code, block in zip(codes, blocks):

        @pl.when(code > 0)
        def _():
            z_first = HALO + (code - 1) * TE
            rows = TE * TE * y_count
            lifted[0:rows] = block[offset : offset + rows].astype(F32)
            for z_at in range(TE):
                for y_at in range(y_count):
                    row = z_at * TE * y_count + y_at
                    volume[z_first + z_at, y_first + y_at] = lifted[pl.ds(row, TE, stride=y_count)]
            if mask is not None:
                mask[side, pl.ds(z_first, TE)] = jnp.ones((TE,) + mask.shape[2:], F32)


def side_sizes():
    face, thin = HALO * TE * TE, 2 * TE * TE
    return face, thin, face + thin + 16


def sides_kernel(tile, used, odd, feature_rows, upstream_rows, to_pair, to_cross, own_table, lifted):
    channels = feature_rows.shape[1]
    face = side_sizes()[0]
    for rows, width, offset in ((feature_rows, HALO, 0), (upstream_rows, 2, face)):
        lifted[...] = rows[...].astype(F32).reshape(lifted.shape)
        count = TE * TE * width
        high = lifted[:, TE - width :].reshape(count, channels)
        low = lifted[:, :width].reshape(count, channels)
        to_pair[offset : offset + count] = jnp.where(odd[0] == 1, low, high).astype(BF)
        to_cross[offset : offset + count] = jnp.where(odd[0] == 1, high, low).astype(BF)
    place = lax.broadcasted_iota(jnp.int32, (16, channels), 0)
    table = jnp.zeros((16, channels), F32)
    for slot in range(tile.shape[1]):
        code = jnp.where(used[0, slot] == 1, tile[0, slot] + 1, 0)
        table = jnp.where(place == slot, code.astype(F32), table)
    for out in (to_pair, to_cross, own_table):
        out[out.shape[0] - 16 :] = table.astype(BF)


def sides_call(slot_tile, slot_used, odd, feature_rows, upstream_rows):
    voxels, channels = feature_rows.shape
    smem = pl.BlockSpec(memory_space=pltpu.SMEM)
    vmem = pl.BlockSpec(memory_space=pltpu.VMEM)
    side = jax.ShapeDtypeStruct((side_sizes()[2], channels), BF)
    return pl.pallas_call(
        sides_kernel,
        out_shape=[side, side, jax.ShapeDtypeStruct((16, channels), BF)],
        in_specs=[smem, smem, smem, vmem, vmem],
        out_specs=[vmem] * 3,
        scratch_shapes=[pltpu.VMEM((TE * TE, TE, channels), F32)],
        name="pack_sides",
    )(slot_tile, slot_used, odd, feature_rows, upstream_rows)


def table_at(block, first, slots):
    table = block[first : first + 16].astype(F32)
    place = lax.broadcasted_iota(jnp.int32, table.shape, 0)
    return [jnp.max(jnp.where(place == slot, table, 0.0)).astype(jnp.int32) for slot in slots]


def backward_kernel(block_count, tiles, depth_ref, odd_ref, *refs):
    own, up, pair, cross = (list(refs[at * block_count : (at + 1) * block_count]) for at in range(4))
    own_table, far_first, far_second, last, kept, given = refs[4 * block_count : 4 * block_count + 6]
    rest = list(refs[4 * block_count + 6 :])
    channels = own[0].shape[-1]

    def take():
        return rest.pop(0)

    volume, upstream, mask, lifted, result, grad_rows, first_kernel, second_kernel, near_own, near_up, sems = (
        take() for _ in range(11)
    )
    fetches = [
        pltpu.make_async_copy(far, near, sems.at[at])
        for at, (far, near) in enumerate(
            ((own[0], near_own), (up[0], near_up), (far_first, first_kernel), (far_second, second_kernel))
        )
    ]
    for fetch in fetches:
        fetch.start()
    own[0], up[0] = near_own, near_up
    regions = []
    for number in range(tiles):
        halo = HALO - number
        group = []
        for layer in range(4):
            size = TE + 2 * (halo - layer)
            even = take()
            odd = take() if size > TE else None
            group.append(Region(even, odd, size, size))
        regions.append(group)
    slopes = [take() for _ in range(tiles)]

    me = depth_ref[0]
    slots = [me ^ block for block in range(block_count)]
    voxels = TE * TE * TE
    volume[...] = jnp.zeros_like(volume)
    upstream[...] = jnp.zeros_like(upstream)
    mask[...] = jnp.zeros_like(mask)
    face, thin, _ = side_sizes()

    held = table_at(own_table, 0, slots)
    odd = odd_ref[0]
    for blocks, low in ((pair, odd), (cross, 1 - odd)):
        codes = table_at(blocks[0], face + thin, slots)
        side = 2 * (1 - low)
        y_feature = (1 - low) * (HALO + TE)
        y_upstream = (1 - low) * (TE + 2) + HALO - 2
        place_slots(codes, blocks, 0, y_feature, HALO, lifted, volume, mask, side)
        place_slots(codes, blocks, face, y_upstream, 2, lifted, upstream, None, side)
    fetches[0].wait()
    place_slots(held, own, 0, HALO, TE, lifted, volume, mask, 1)
    fetches[1].wait()
    place_slots(held, up, 0, HALO, TE, lifted, upstream, None, 1)

    starts = []
    alive = []
    for number in range(tiles):
        starts.append(jnp.maximum(held[2 * number] - 1, 0) * TE)
        alive.append((held[2 * number] > 0).astype(F32))

    for number in range(tiles):
        source = regions[number][0]
        z_first = starts[number] + number

        for pair in range(source.y_size // 2):
            for parity in range(2):
                source.store_row(pair, parity, volume[pl.ds(z_first, source.z_size), number + 2 * pair + parity])

    def finish_layer(number, layer, kind):
        region = regions[number][layer]
        inset = number + layer
        z_first = starts[number] + inset
        q_size = region.z_size // 2

        for pair in range(region.y_size // 2):
            for parity in range(2):
                y_at = inset + 2 * pair + parity
                side = (y_at >= HALO) + (y_at >= HALO + TE)
                window = pl.ds(z_first, region.z_size)
                keep = mask[side, window]
                value = result[0:q_size, pair, :, parity * channels : (parity + 1) * channels]
                value = value.reshape(keep.shape)
                if kind == "act":
                    out, slope = gelu_pair(value)
                    slopes[number][:, pair, parity] = slope * keep
                    out = out * keep
                elif kind == "delta_two":
                    out = upstream[window, y_at] * gelu_slope(value) * keep
                else:
                    out = value * slopes[number][2 : 2 + region.z_size, pair + 1, parity]
                region.store_row(pair, parity, out)

    def kernel_gradient(at, left, delta):
        flipped = []
        for number in range(tiles):
            region = regions[number][delta]
            inset = (region.z_size - TE) // 2
            rows = region.tile_rows(inset, inset, channels, channels, TE).astype(F32) * (alive[number] * (1.0 / voxels))
            flipped.append(rows.T.astype(BF))
        flipped = jnp.concatenate(flipped, axis=1)
        for z_tap in range(3):
            columns = []
            for number in range(tiles):
                region = regions[number][left]
                inset = (region.z_size - TE) // 2 - 1
                shifted = [
                    region.tile_rows(inset + z_tap, inset + y_tap, 3 * channels, 0, TE) for y_tap in range(3)
                ]
                columns.append(jnp.concatenate(shifted, axis=1))
            product = jnp.dot(flipped, jnp.concatenate(columns, axis=0), preferred_element_type=F32)
            for y_tap in range(3):
                for x_tap in range(3):
                    lane = (y_tap * 3 + x_tap) * channels
                    row = (z_tap * 9 + x_tap * 3 + y_tap) * channels
                    grad_rows[row : row + channels] = product[:, lane : lane + channels].T
        near_parts, far_parts, _, padded, _ = kept.shape
        share = 27 * channels // (near_parts * far_parts * block_count)
        for near_at in range(near_parts):
            for far_at in range(far_parts):
                column = (far_at * near_parts + near_at) * block_count
                for out, owner in ((kept, me), (given, me ^ 1)):
                    rows = grad_rows[pl.ds((column + owner) * share, padded)]
                    out[near_at, far_at, at] = rows.astype(BF)

    grad_rows[27 * channels :] = jnp.zeros_like(grad_rows[27 * channels :])
    fetches[2].wait()
    for number in range(tiles):
        convolve_region(regions[number][0], first_kernel, False, result)
        finish_layer(number, 1, "act")
    fetches[3].wait()
    for number in range(tiles):
        convolve_region(regions[number][1], second_kernel, False, result)
        finish_layer(number, 2, "delta_two")
    kernel_gradient(1, 1, 2)
    for number in range(tiles):
        convolve_region(regions[number][2], second_kernel, True, result)
        finish_layer(number, 3, "delta_one")
    last[...] = regions[0][3].even[:, :, :, :, channels : 2 * channels]
    kernel_gradient(0, 0, 3)


def input_kernel(depth_ref, own_table, last, far_first, input_grad, even, odd, lifted, result, first_kernel, sem):
    fetch = pltpu.make_async_copy(far_first, first_kernel, sem.at[0])
    fetch.start()
    (held,) = table_at(own_table, 0, [depth_ref[0]])
    alive = (held > 0).astype(F32)
    channels = input_grad.shape[-1]
    region = Region(even, odd, TE + 2, TE + 2)
    for pair in range(region.y_size // 2):
        for parity in range(2):
            column = last[:, pair, parity].astype(F32)
            region.store_row(pair, parity, column.reshape(region.z_size, TE, channels))
    fetch.wait()
    convolve_region(region, first_kernel, True, result)
    for pair in range(TE // 2):
        for parity in range(2):
            value = result[:, pair, :, parity * channels : (parity + 1) * channels] * alive
            value = value.reshape(TE, TE, channels)
            for z_at in range(TE):
                lifted[pl.ds(z_at * TE * TE + 2 * pair + parity, TE, stride=TE)] = value[z_at]
    input_grad[...] = lifted[0 : input_grad.shape[0]].astype(BF)


def input_call(depth_at, own_table, last, first_kernel):
    channels = first_kernel.shape[-1]
    voxels = TE * TE * TE
    vmem = pl.BlockSpec(memory_space=pltpu.VMEM)
    return pl.pallas_call(
        input_kernel,
        out_shape=jax.ShapeDtypeStruct((voxels, channels), BF),
        in_specs=[
            pl.BlockSpec(memory_space=pltpu.SMEM),
            vmem,
            vmem,
            pl.BlockSpec(memory_space=pltpu.HBM),
        ],
        out_specs=vmem,
        scratch_shapes=region_shapes(TE + 2, TE + 2, TE, channels, True)
        + [
            pltpu.VMEM((voxels + 16, channels), F32),
            pltpu.VMEM((TE // 2, TE // 2, 2 * TE, 2 * channels), F32),
            pltpu.VMEM((27, channels, channels), BF),
            pltpu.SemaphoreType.DMA((1,)),
        ],
        compiler_params=pltpu.CompilerParams(vmem_limit_bytes=INPUT_VMEM),
        cost_estimate=pl.CostEstimate(
            flops=2 * 36 * voxels * channels * channels,
            bytes_accessed=2 * 27 * channels * channels + 8 * voxels * channels,
            transcendentals=0,
        ),
        name="input_gradient",
    )(depth_at.reshape(1), own_table, last, first_kernel)


def backward_call(own, up, pair, cross, own_table, kernels, depth_at, odd, columns, positions, tiles):
    channels = own[0].shape[-1]
    voxels = TE * TE * TE
    planes = positions * TE + 2 * HALO
    span = TE + 2 * HALO
    inner = span // 2 - 1
    padded = -(-(27 * channels // (columns * len(own))) // 16) * 16
    scratch = [
        pltpu.VMEM((planes, span, TE, channels), F32),
        pltpu.VMEM((planes, span, TE, channels), F32),
        pltpu.VMEM((3, planes, TE, channels), F32),
        pltpu.VMEM((voxels + 16, channels), F32),
        pltpu.VMEM((inner, inner, 2 * TE, 2 * channels), F32),
        pltpu.VMEM((27 * channels + 16, channels), F32),
        pltpu.VMEM((27, channels, channels), BF),
        pltpu.VMEM((27, channels, channels), BF),
        pltpu.VMEM((voxels, channels), BF),
        pltpu.VMEM((voxels, channels), BF),
        pltpu.SemaphoreType.DMA((4,)),
    ]
    for number in range(tiles):
        for layer in range(4):
            size = span - 2 * (number + layer)
            scratch += region_shapes(size, size, TE, channels, size > TE)
    for number in range(tiles):
        size = span - 2 * (number + 1)
        scratch.append(pltpu.VMEM((size, size // 2, 2, TE, channels), F32))
    vmem = pl.BlockSpec(memory_space=pltpu.VMEM)
    smem = pl.BlockSpec(memory_space=pltpu.SMEM)
    hbm = pl.BlockSpec(memory_space=pltpu.HBM)

    def body(*refs):
        backward_kernel(len(own), tiles, *refs)

    last = TE + 2
    share = jax.ShapeDtypeStruct((NEAR, columns // NEAR, 2, padded, channels), BF)
    return pl.pallas_call(
        body,
        out_shape=[
            jax.ShapeDtypeStruct((last // 2, last // 2, 2, 2 * TE, channels), BF),
            share,
            share,
        ],
        in_specs=[smem, smem] + ([hbm] + [vmem] * (len(own) - 1)) * 2 + [vmem] * (len(pair) + len(cross) + 1) + [hbm, hbm],
        out_specs=[vmem] * 3,
        scratch_shapes=scratch,
        compiler_params=pltpu.CompilerParams(vmem_limit_bytes=VMEM_LIMIT),
        cost_estimate=pl.CostEstimate(
            flops=40 * 27 * voxels * channels * channels,
            bytes_accessed=100 * voxels * channels,
            transcendentals=4 * voxels * channels,
        ),
        name="tile_backward",
    )(depth_at.reshape(1), odd, *own, *up, *pair, *cross, own_table, *kernels)


def on_device_line(features, cotangent, first_kernel, second_kernel, slot_tile, slot_used):
    channels = features.shape[3]
    depth_size, space_size = lax.axis_size("depth"), lax.axis_size("space")
    depth_at, space_at = lax.axis_index("depth"), lax.axis_index("space")

    def swap(block, axis, bits):
        return lax.ppermute(block, axis, [(i, i ^ bits) for i in range(lax.axis_size(axis))])

    own, up = features[0, 0], cotangent[0, 0]
    own_far, up_far = swap(own, "depth", 2), swap(up, "depth", 2)
    odd = (space_at % 2).reshape(1)
    to_pair, to_cross, own_table = sides_call(slot_tile, slot_used, odd, own, up)
    to_pair, own_far = lax.optimization_barrier((to_pair, own_far))
    crossing = [(i, i + 1 if i % 2 else i - 1) for i in range(1, space_size - 1)]
    cross, pair = lax.ppermute(to_cross, "space", crossing), swap(to_pair, "space", 1)
    cross_far, pair_far = swap(cross, "depth", 2), swap(pair, "depth", 2)

    def with_sibling(near, far):
        return [near, swap(near, "depth", 1), far, swap(far, "depth", 1)]

    last, kept, given = backward_call(
        with_sibling(own, own_far),
        with_sibling(up, up_far),
        with_sibling(pair, pair_far),
        with_sibling(cross, cross_far),
        own_table,
        (first_kernel, second_kernel),
        depth_at,
        odd,
        space_size,
        slot_tile.shape[1],
        2,
    )
    input_grad = input_call(depth_at, own_table, last, first_kernel)
    share = 27 * channels // (depth_size * space_size)

    def part(block, at):
        return lax.dynamic_index_in_dim(block, at, 0, keepdims=False)

    near_at, far_at = space_at % NEAR, space_at // NEAR
    column_sum = kept.astype(F32) + swap(given, "depth", 1).astype(F32)
    group = part(column_sum, near_at)
    for step in range(1, NEAR):
        group = group + swap(part(column_sum, near_at ^ step).astype(BF), "space", step).astype(F32)
    total = part(group, far_at)
    for step in range(1, space_size // NEAR):
        total = total + swap(part(group, far_at ^ step).astype(BF), "space", NEAR * step).astype(F32)
    first_share, second_share = (total[at, :share].reshape(-1) for at in range(2))
    return (input_grad.reshape(features.shape), first_share, second_share)


def solution(mesh):
    line = mesh.shape["space"] == GY and mesh.shape["depth"] == 4
    run = on_device_line if line else on_device_wide
    return jax.shard_map(
        run,
        mesh=mesh,
        in_specs=(
            P("space", "depth", None, None),
            P("space", "depth", None, None),
            P(),
            P(),
            P("space", None),
            P("space", None),
        ),
        out_specs=(P("space", "depth", None, None), P(("space", "depth")), P(("space", "depth"))),
        check_vma=False,
    )
```

```python
import jax
import jax.numpy as jnp
from jax import lax
from jax.experimental import pallas as pl
from jax.experimental.pallas import tpu as pltpu
from jax.sharding import PartitionSpec as P

TE = 8
GY = 8


SLOPE_COEF = 0.7978845608028654
CUBIC_COEF = 0.044715


def from_behind(block, axis, distance):
    devices = range(lax.axis_size(axis))
    route = [(i - distance, i) for i in devices if i - distance in devices]
    return lax.ppermute(block, axis, route)


def gelu_pair(values):
    inner_arg = SLOPE_COEF * (values + CUBIC_COEF * values * values * values)
    tangent = jnp.tanh(inner_arg)
    output = 0.5 * values * (1.0 + tangent)
    derivative = 0.5 * (1.0 + tangent) + 0.5 * values * (1.0 - tangent * tangent) * SLOPE_COEF * (
        1.0 + 3.0 * CUBIC_COEF * values * values
    )
    return (output, derivative)


def gelu_slope(values):
    inner_arg = SLOPE_COEF * (values + CUBIC_COEF * values * values * values)
    tangent = jnp.tanh(inner_arg)
    return 0.5 * (1.0 + tangent) + 0.5 * values * (1.0 - tangent * tangent) * SLOPE_COEF * (
        1.0 + 3.0 * CUBIC_COEF * values * values
    )


def place_matrix(slot_tile, slot_used, position_count):
    positions = jnp.arange(position_count, dtype=jnp.int32)
    matches = (slot_tile[0][None, :] == positions[:, None]) & (slot_used[0][None, :] == 1)
    return matches.astype(jnp.bfloat16)


def dense_column(tile_rows, placement):
    summed = jnp.einsum(
        "tj,jvc->tvc",
        placement,
        lax.all_gather(tile_rows, "depth", axis=0, tiled=True),
        preferred_element_type=jnp.float32,
    )
    return summed.astype(jnp.bfloat16).reshape(-1, TE, TE, summed.shape[-1])


def extend_sides(own_block, move_face, space_index):
    y_coord = space_index % GY
    below = move_face(own_block[:, :, -1:, :], 1) * (y_coord > 0).astype(own_block.dtype)
    above = move_face(own_block[:, :, :1, :], -1) * (y_coord < GY - 1).astype(own_block.dtype)
    widened = jnp.concatenate([below, own_block, above], axis=2)
    behind = move_face(widened[:, -1:, :, :], GY)
    ahead = move_face(widened[:, :1, :, :], -GY)
    return jnp.concatenate([behind, widened, ahead], axis=1)


def pad_depth(own_block):
    return jnp.pad(own_block, ((1, 1), (0, 0), (0, 0), (0, 0)))


def windows_at(padded, positions):

    def one_window(z_index):
        return lax.dynamic_slice_in_dim(padded, z_index * TE, TE + 2, 0)

    return jax.vmap(one_window)(positions)


def unfold(windows, flipped):
    pieces = []
    for kernel_tap in range(27):
        z_step, x_step, y_step = (kernel_tap // 9, kernel_tap // 3 % 3, kernel_tap % 3)
        if flipped:
            z_step, x_step, y_step = (2 - z_step, 2 - x_step, 2 - y_step)
        pieces.append(
            windows[:, z_step : z_step + TE, x_step : x_step + TE, y_step : y_step + TE, :]
        )
    stacked = jnp.concatenate(pieces, axis=-1)
    return stacked.reshape(-1, stacked.shape[-1])


def tile_sum(columns, delta):
    return lax.dot_general(
        columns, delta, (((0,), (0,)), ((), ())), preferred_element_type=jnp.float32
    )


def on_device_wide(features, cotangent, first_kernel, second_kernel, slot_tile, slot_used):
    depth_index = lax.axis_index("depth")
    space_index = lax.axis_index("space")
    slot_count = features.shape[1]
    voxels = features.shape[2]
    channels = features.shape[3]
    position_count = slot_tile.shape[1]
    placement = place_matrix(slot_tile, slot_used, position_count)
    own_first = depth_index * slot_count
    own_tiles = lax.dynamic_slice_in_dim(slot_tile[0], own_first, slot_count, 0)
    own_used = lax.dynamic_slice_in_dim(slot_used[0], own_first, slot_count, 0).astype(jnp.float32)
    feature_slots = features[0]
    upstream_slots = cotangent[0]

    def column_move(face, offset):
        return from_behind(face, "space", offset)

    def halo_of(tile_rows):
        column = dense_column(tile_rows.reshape(slot_count, voxels, channels), placement)
        return pad_depth(extend_sides(column, column_move, space_index))

    upstream = upstream_slots.reshape(-1, channels)
    source_column = halo_of(feature_slots)
    alive_rows = jnp.repeat(own_used, voxels)[:, None]
    forward_one = first_kernel.reshape(-1, channels)
    forward_two = second_kernel.reshape(-1, channels)
    backward_one = jnp.transpose(first_kernel, (0, 2, 1)).reshape(-1, channels)
    backward_two = jnp.transpose(second_kernel, (0, 2, 1)).reshape(-1, channels)
    source_cols = unfold(windows_at(source_column, own_tiles), False)
    pre_one = jnp.dot(source_cols, forward_one, preferred_element_type=jnp.float32)
    act_value, slope_one = gelu_pair(pre_one)
    act_one = (act_value * alive_rows).astype(jnp.bfloat16)
    act_cols = unfold(windows_at(halo_of(act_one), own_tiles), False)
    pre_two = jnp.dot(act_cols, forward_two, preferred_element_type=jnp.float32)
    slope_two = gelu_slope(pre_two)
    delta_two = (upstream.astype(jnp.float32) * slope_two * alive_rows).astype(jnp.bfloat16)
    second_grad = tile_sum(act_cols, delta_two).reshape(-1) * (1.0 / voxels)
    back_one = jnp.dot(
        unfold(windows_at(halo_of(delta_two), own_tiles), True),
        backward_two,
        preferred_element_type=jnp.float32,
    )
    delta_one = (back_one * slope_one * alive_rows).astype(jnp.bfloat16)
    first_grad = tile_sum(source_cols, delta_one).reshape(-1) * (1.0 / voxels)
    back_zero = jnp.dot(
        unfold(windows_at(halo_of(delta_one), own_tiles), True),
        backward_one,
        preferred_element_type=jnp.float32,
    )
    used_rows = jnp.repeat(own_used, voxels)[:, None]
    input_grad = (back_zero * used_rows).astype(jnp.bfloat16).reshape(features.shape)
    first_share, second_share = (
        lax.psum_scatter(first_grad, ("space", "depth"), scatter_dimension=0, tiled=True),
        lax.psum_scatter(second_grad, ("space", "depth"), scatter_dimension=0, tiled=True),
    )
    return (input_grad, first_share, second_share)


HALO = 4
NEAR = 4
INPUT_VMEM = 16 * 1024 * 1024
VMEM_LIMIT = 51 * 1024 * 1024
BF = jnp.bfloat16
F32 = jnp.float32


class Region:
    def __init__(self, even, odd, z_size, y_size):
        self.even, self.odd, self.z_size, self.y_size = even, odd, z_size, y_size

    def planes(self, first):
        return (self.odd, (first - 1) // 2) if first % 2 else (self.even, first // 2)

    def store_row(self, y_pair, y_parity, column):
        z_size, width, channels = column.shape
        place = lax.broadcasted_iota(jnp.int32, column.shape, 1)
        before = jnp.where(place == 0, 0.0, pltpu.roll(column, 1, 1))
        after = jnp.where(place == width - 1, 0.0, pltpu.roll(column, width - 1, 1))
        wide = jnp.concatenate([before, column, after], axis=-1)
        self.even[:, y_pair, y_parity] = wide.reshape(z_size // 2, 2 * width, 3 * channels).astype(BF)
        if self.odd is not None:
            inner = wide[1:-1].reshape(z_size // 2 - 1, 2 * width, 3 * channels)
            self.odd[:, y_pair, y_parity] = inner.astype(BF)

    def tile_rows(self, z_first, y_first, lanes, lane_first, edge):
        ref, q_first = self.planes(z_first)
        parts = []
        for y_at in range(y_first, y_first + edge):
            part = ref[q_first : q_first + edge // 2, y_at // 2, y_at % 2, :, lane_first : lane_first + lanes]
            parts.append(part.reshape(-1, lanes))
        return jnp.concatenate(parts, axis=0)


def region_shapes(z_size, y_size, width, channels, with_odd):
    tail = (y_size // 2, 2, 2 * width, 3 * channels)
    shapes = [pltpu.VMEM((z_size // 2,) + tail, BF)]
    if with_odd:
        shapes.append(pltpu.VMEM((z_size // 2 - 1,) + tail, BF))
    return shapes


def convolve_region(region, kernel, transposed, result):
    q_size, r_size = region.z_size // 2 - 1, region.y_size // 2 - 1
    channels = region.even.shape[-1] // 3
    pieces = []
    for block in range(9):
        z_tap, x_tap = block // 3, block % 3
        if transposed:
            z_tap, x_tap = 2 - z_tap, 2 - x_tap
        ref, q_first = region.planes(z_tap)
        for y_at in range(4):
            if transposed:
                y_at = 3 - y_at
            piece = ref[
                q_first : q_first + q_size,
                y_at // 2 : y_at // 2 + r_size,
                y_at % 2,
                :,
                x_tap * channels : (x_tap + 1) * channels,
            ]
            pieces.append(piece.reshape(-1, channels))
    left = jnp.concatenate(pieces, axis=1)
    blank = jnp.zeros((channels, channels), BF)
    blocks = []
    for block in range(9):
        taps = [kernel[block * 3 + y_tap] for y_tap in range(3)]
        for near, far in zip(*((taps + [blank], [blank] + taps) if not transposed else ([blank] + taps, taps + [blank]))):
            blocks.append(jnp.concatenate([near, far], axis=0 if transposed else 1))
    right = jnp.concatenate(blocks, axis=1 if transposed else 0)
    contract = (((1,), (1 if transposed else 0,)), ((), ()))
    product = lax.dot_general(left, right, contract, preferred_element_type=F32)
    result[0:q_size, 0:r_size] = product.reshape(q_size, r_size, product.shape[0] // (q_size * r_size), -1)


def place_slots(codes, blocks, offset, y_first, y_count, lifted, volume, mask, side):
    spare = volume.shape[0] - TE
    for at, (code, block) in enumerate(zip(codes, blocks)):
        z_first = jnp.where(code > 0, HALO + (code - 1) * TE, spare)
        rows = TE * TE * y_count
        lifted[at, 0:rows] = block[offset : offset + rows].astype(F32)
        for z_at in range(TE):
            for y_at in range(y_count):
                row = z_at * TE * y_count + y_at
                volume[z_first + z_at, y_first + y_at] = lifted[at, pl.ds(row, TE, stride=y_count)]
        if mask is not None:
            mask[side, pl.ds(z_first, TE)] = jnp.ones((TE,) + mask.shape[2:], F32)


def side_sizes():
    face, thin = HALO * TE * TE, 2 * TE * TE
    return face, thin, face + thin + 16


def sides_kernel(tile, used, odd, feature_rows, upstream_rows, to_pair, to_cross, own_table, lifted):
    channels = feature_rows.shape[1]
    face = side_sizes()[0]
    for rows, width, offset in ((feature_rows, HALO, 0), (upstream_rows, 2, face)):
        lifted[...] = rows[...].astype(F32).reshape(lifted.shape)
        count = TE * TE * width
        up_first = odd[0] * (TE - width)
        low_first = (1 - odd[0]) * (TE - width)
        to_cross[offset : offset + count] = lifted[:, pl.ds(up_first, width)].reshape(count, channels).astype(BF)
        to_pair[offset : offset + count] = lifted[:, pl.ds(low_first, width)].reshape(count, channels).astype(BF)
    place = lax.broadcasted_iota(jnp.int32, (16, channels), 0)
    table = jnp.zeros((16, channels), F32)
    for slot in range(tile.shape[1]):
        code = jnp.where(used[0, slot] == 1, tile[0, slot] + 1, 0)
        table = jnp.where(place == slot, code.astype(F32), table)
    for out in (to_pair, to_cross, own_table):
        out[out.shape[0] - 16 :] = table.astype(BF)


def sides_call(slot_tile, slot_used, odd, feature_rows, upstream_rows):
    voxels, channels = feature_rows.shape
    smem = pl.BlockSpec(memory_space=pltpu.SMEM)
    vmem = pl.BlockSpec(memory_space=pltpu.VMEM)
    side = jax.ShapeDtypeStruct((side_sizes()[2], channels), BF)
    return pl.pallas_call(
        sides_kernel,
        out_shape=[side, side, jax.ShapeDtypeStruct((16, channels), BF)],
        in_specs=[smem, smem, smem, vmem, vmem],
        out_specs=[vmem] * 3,
        scratch_shapes=[pltpu.VMEM((TE * TE, TE, channels), F32)],
        name="pack_sides",
    )(slot_tile, slot_used, odd, feature_rows, upstream_rows)


def table_at(block, first, slots):
    table = block[first : first + 16].astype(F32)
    place = lax.broadcasted_iota(jnp.int32, table.shape, 0)
    return [jnp.max(jnp.where(place == slot, table, 0.0)).astype(jnp.int32) for slot in slots]


def backward_kernel(block_count, tiles, depth_ref, odd_ref, *refs):
    own, up, pair, cross = (list(refs[at * block_count : (at + 1) * block_count]) for at in range(4))
    own_table, far_first, far_second, last, kept, given = refs[4 * block_count : 4 * block_count + 6]
    rest = list(refs[4 * block_count + 6 :])
    channels = own[0].shape[-1]

    def take():
        return rest.pop(0)

    volume, upstream, mask, lifted, result, grad_rows, first_kernel, second_kernel, near_own, near_up, sems = (
        take() for _ in range(11)
    )
    fetches = [
        pltpu.make_async_copy(far, near, sems.at[at])
        for at, (far, near) in enumerate(
            ((own[0], near_own), (up[0], near_up), (far_first, first_kernel), (far_second, second_kernel))
        )
    ]
    for fetch in fetches:
        fetch.start()
    own[0], up[0] = near_own, near_up
    regions = []
    for number in range(tiles):
        halo = HALO - number
        group = []
        for layer in range(4):
            size = TE + 2 * (halo - layer)
            even = take()
            odd = take() if size > TE else None
            group.append(Region(even, odd, size, size))
        regions.append(group)
    slopes = [take() for _ in range(tiles)]

    me = depth_ref[0]
    slots = [me ^ block for block in range(block_count)]
    voxels = TE * TE * TE
    volume[...] = jnp.zeros_like(volume)
    upstream[...] = jnp.zeros_like(upstream)
    mask[...] = jnp.zeros_like(mask)
    face, thin, _ = side_sizes()

    held = table_at(own_table, 0, slots)
    odd = odd_ref[0]
    for blocks, low in ((pair, odd), (cross, 1 - odd)):
        codes = table_at(blocks[0], face + thin, slots)
        side = 2 * (1 - low)
        y_feature = (1 - low) * (HALO + TE)
        y_upstream = (1 - low) * (TE + 2) + HALO - 2
        place_slots(codes, blocks, 0, y_feature, HALO, lifted, volume, mask, side)
        place_slots(codes, blocks, face, y_upstream, 2, lifted, upstream, None, side)
    fetches[0].wait()
    place_slots(held, own, 0, HALO, TE, lifted, volume, mask, 1)
    fetches[1].wait()
    place_slots(held, up, 0, HALO, TE, lifted, upstream, None, 1)

    starts = []
    alive = []
    for number in range(tiles):
        starts.append(jnp.maximum(held[2 * number] - 1, 0) * TE)
        alive.append((held[2 * number] > 0).astype(F32))

    for number in range(tiles):
        source = regions[number][0]
        z_first = starts[number] + number

        for pair in range(source.y_size // 2):
            for parity in range(2):
                source.store_row(pair, parity, volume[pl.ds(z_first, source.z_size), number + 2 * pair + parity])

    def finish_layer(number, layer, kind):
        region = regions[number][layer]
        inset = number + layer
        z_first = starts[number] + inset
        q_size = region.z_size // 2

        for pair in range(region.y_size // 2):
            for parity in range(2):
                y_at = inset + 2 * pair + parity
                side = (y_at >= HALO) + (y_at >= HALO + TE)
                window = pl.ds(z_first, region.z_size)
                keep = mask[side, window]
                value = result[0:q_size, pair, :, parity * channels : (parity + 1) * channels]
                value = value.reshape(keep.shape)
                if kind == "act":
                    out, slope = gelu_pair(value)
                    slopes[number][:, pair, parity] = slope * keep
                    out = out * keep
                elif kind == "delta_two":
                    out = upstream[window, y_at] * gelu_slope(value) * keep
                else:
                    out = value * slopes[number][2 : 2 + region.z_size, pair + 1, parity]
                region.store_row(pair, parity, out)

    def kernel_gradient(at, left, delta):
        flipped = []
        for number in range(tiles):
            region = regions[number][delta]
            inset = (region.z_size - TE) // 2
            rows = region.tile_rows(inset, inset, channels, channels, TE).astype(F32) * (alive[number] * (1.0 / voxels))
            flipped.append(rows.T.astype(BF))
        flipped = jnp.concatenate(flipped, axis=1)
        for z_tap in range(3):
            columns = []
            for number in range(tiles):
                region = regions[number][left]
                inset = (region.z_size - TE) // 2 - 1
                shifted = [
                    region.tile_rows(inset + z_tap, inset + y_tap, 3 * channels, 0, TE) for y_tap in range(3)
                ]
                columns.append(jnp.concatenate(shifted, axis=1))
            product = jnp.dot(flipped, jnp.concatenate(columns, axis=0), preferred_element_type=F32)
            for y_tap in range(3):
                for x_tap in range(3):
                    lane = (y_tap * 3 + x_tap) * channels
                    row = (z_tap * 9 + x_tap * 3 + y_tap) * channels
                    grad_rows[row : row + channels] = product[:, lane : lane + channels].T
        near_parts, far_parts, _, padded, _ = kept.shape
        share = 27 * channels // (near_parts * far_parts * block_count)
        for near_at in range(near_parts):
            for far_at in range(far_parts):
                column = (far_at * near_parts + near_at) * block_count
                for out, owner in ((kept, me), (given, me ^ 1)):
                    rows = grad_rows[pl.ds((column + owner) * share, padded)]
                    out[near_at, far_at, at] = rows.astype(BF)

    grad_rows[27 * channels :] = jnp.zeros_like(grad_rows[27 * channels :])
    fetches[2].wait()
    for number in range(tiles):
        convolve_region(regions[number][0], first_kernel, False, result)
        finish_layer(number, 1, "act")
    fetches[3].wait()
    for number in range(tiles):
        convolve_region(regions[number][1], second_kernel, False, result)
        finish_layer(number, 2, "delta_two")
    kernel_gradient(1, 1, 2)
    for number in range(tiles):
        convolve_region(regions[number][2], second_kernel, True, result)
        finish_layer(number, 3, "delta_one")
    last[...] = regions[0][3].even[:, :, :, :, channels : 2 * channels]
    kernel_gradient(0, 0, 3)


def input_kernel(depth_ref, own_table, last, far_first, input_grad, even, odd, lifted, result, first_kernel, sem):
    fetch = pltpu.make_async_copy(far_first, first_kernel, sem.at[0])
    fetch.start()
    (held,) = table_at(own_table, 0, [depth_ref[0]])
    alive = (held > 0).astype(F32)
    channels = input_grad.shape[-1]
    region = Region(even, odd, TE + 2, TE + 2)
    for pair in range(region.y_size // 2):
        for parity in range(2):
            column = last[:, pair, parity].astype(F32)
            region.store_row(pair, parity, column.reshape(region.z_size, TE, channels))
    fetch.wait()
    convolve_region(region, first_kernel, True, result)
    for pair in range(TE // 2):
        for parity in range(2):
            value = result[:, pair, :, parity * channels : (parity + 1) * channels] * alive
            value = value.reshape(TE, TE, channels)
            for z_at in range(TE):
                lifted[pl.ds(z_at * TE * TE + 2 * pair + parity, TE, stride=TE)] = value[z_at]
    input_grad[...] = lifted[0 : input_grad.shape[0]].astype(BF)


def input_call(depth_at, own_table, last, first_kernel):
    channels = first_kernel.shape[-1]
    voxels = TE * TE * TE
    vmem = pl.BlockSpec(memory_space=pltpu.VMEM)
    return pl.pallas_call(
        input_kernel,
        out_shape=jax.ShapeDtypeStruct((voxels, channels), BF),
        in_specs=[
            pl.BlockSpec(memory_space=pltpu.SMEM),
            vmem,
            vmem,
            pl.BlockSpec(memory_space=pltpu.HBM),
        ],
        out_specs=vmem,
        scratch_shapes=region_shapes(TE + 2, TE + 2, TE, channels, True)
        + [
            pltpu.VMEM((voxels + 16, channels), F32),
            pltpu.VMEM((TE // 2, TE // 2, 2 * TE, 2 * channels), F32),
            pltpu.VMEM((27, channels, channels), BF),
            pltpu.SemaphoreType.DMA((1,)),
        ],
        compiler_params=pltpu.CompilerParams(vmem_limit_bytes=INPUT_VMEM),
        cost_estimate=pl.CostEstimate(
            flops=2 * 36 * voxels * channels * channels,
            bytes_accessed=2 * 27 * channels * channels + 8 * voxels * channels,
            transcendentals=0,
        ),
        name="input_gradient",
    )(depth_at.reshape(1), own_table, last, first_kernel)


def backward_call(own, up, pair, cross, own_table, kernels, depth_at, odd, columns, positions, tiles):
    channels = own[0].shape[-1]
    voxels = TE * TE * TE
    planes = positions * TE + 2 * HALO + TE
    span = TE + 2 * HALO
    inner = span // 2 - 1
    padded = -(-(27 * channels // (columns * len(own))) // 16) * 16
    scratch = [
        pltpu.VMEM((planes, span, TE, channels), F32),
        pltpu.VMEM((planes, span, TE, channels), F32),
        pltpu.VMEM((3, planes, TE, channels), F32),
        pltpu.VMEM((len(own), voxels + 16, channels), F32),
        pltpu.VMEM((inner, inner, 2 * TE, 2 * channels), F32),
        pltpu.VMEM((27 * channels + 16, channels), F32),
        pltpu.VMEM((27, channels, channels), BF),
        pltpu.VMEM((27, channels, channels), BF),
        pltpu.VMEM((voxels, channels), BF),
        pltpu.VMEM((voxels, channels), BF),
        pltpu.SemaphoreType.DMA((4,)),
    ]
    for number in range(tiles):
        for layer in range(4):
            size = span - 2 * (number + layer)
            scratch += region_shapes(size, size, TE, channels, size > TE)
    for number in range(tiles):
        size = span - 2 * (number + 1)
        scratch.append(pltpu.VMEM((size, size // 2, 2, TE, channels), F32))
    vmem = pl.BlockSpec(memory_space=pltpu.VMEM)
    smem = pl.BlockSpec(memory_space=pltpu.SMEM)
    hbm = pl.BlockSpec(memory_space=pltpu.HBM)

    def body(*refs):
        backward_kernel(len(own), tiles, *refs)

    last = TE + 2
    share = jax.ShapeDtypeStruct((NEAR, columns // NEAR, 2, padded, channels), BF)
    return pl.pallas_call(
        body,
        out_shape=[
            jax.ShapeDtypeStruct((last // 2, last // 2, 2, 2 * TE, channels), BF),
            share,
            share,
        ],
        in_specs=[smem, smem] + ([hbm] + [vmem] * (len(own) - 1)) * 2 + [vmem] * (len(pair) + len(cross) + 1) + [hbm, hbm],
        out_specs=[vmem] * 3,
        scratch_shapes=scratch,
        compiler_params=pltpu.CompilerParams(vmem_limit_bytes=VMEM_LIMIT),
        cost_estimate=pl.CostEstimate(
            flops=40 * 27 * voxels * channels * channels,
            bytes_accessed=100 * voxels * channels,
            transcendentals=4 * voxels * channels,
        ),
        name="tile_backward",
    )(depth_at.reshape(1), odd, *own, *up, *pair, *cross, own_table, *kernels)


def on_device_line(features, cotangent, first_kernel, second_kernel, slot_tile, slot_used):
    channels = features.shape[3]
    depth_size, space_size = lax.axis_size("depth"), lax.axis_size("space")
    depth_at, space_at = lax.axis_index("depth"), lax.axis_index("space")

    def swap(block, axis, bits):
        return lax.ppermute(block, axis, [(i, i ^ bits) for i in range(lax.axis_size(axis))])

    own, up = features[0, 0], cotangent[0, 0]
    own_far, up_far = swap(own, "depth", 2), swap(up, "depth", 2)
    odd = (space_at % 2).reshape(1)
    to_pair, to_cross, own_table = sides_call(slot_tile, slot_used, odd, own, up)
    to_pair, own_far = lax.optimization_barrier((to_pair, own_far))
    crossing = [(i, i + 1 if i % 2 else i - 1) for i in range(1, space_size - 1)]
    cross, pair = lax.ppermute(to_cross, "space", crossing), swap(to_pair, "space", 1)
    cross_far, pair_far = swap(cross, "depth", 2), swap(pair, "depth", 2)

    def with_sibling(near, far):
        return [near, swap(near, "depth", 1), far, swap(far, "depth", 1)]

    last, kept, given = backward_call(
        with_sibling(own, own_far),
        with_sibling(up, up_far),
        with_sibling(pair, pair_far),
        with_sibling(cross, cross_far),
        own_table,
        (first_kernel, second_kernel),
        depth_at,
        odd,
        space_size,
        slot_tile.shape[1],
        2,
    )
    input_grad = input_call(depth_at, own_table, last, first_kernel)
    share = 27 * channels // (depth_size * space_size)

    def part(block, at):
        return lax.dynamic_index_in_dim(block, at, 0, keepdims=False)

    near_at, far_at = space_at % NEAR, space_at // NEAR
    column_sum = kept.astype(F32) + swap(given, "depth", 1).astype(F32)
    group = part(column_sum, near_at)
    for step in range(1, NEAR):
        group = group + swap(part(column_sum, near_at ^ step).astype(BF), "space", step).astype(F32)
    total = part(group, far_at)
    for step in range(1, space_size // NEAR):
        total = total + swap(part(group, far_at ^ step).astype(BF), "space", NEAR * step).astype(F32)
    first_share, second_share = (total[at, :share].reshape(-1) for at in range(2))
    return (input_grad.reshape(features.shape), first_share, second_share)


def solution(mesh):
    line = mesh.shape["space"] == GY and mesh.shape["depth"] == 4
    run = on_device_line if line else on_device_wide
    return jax.shard_map(
        run,
        mesh=mesh,
        in_specs=(
            P("space", "depth", None, None),
            P("space", "depth", None, None),
            P(),
            P(),
            P("space", None),
            P("space", None),
        ),
        out_specs=(P("space", "depth", None, None), P(("space", "depth")), P(("space", "depth"))),
        check_vma=False,
    )
```

```python
import jax
import jax.numpy as jnp
from jax import lax
from jax.experimental import pallas as pl
from jax.experimental.pallas import tpu as pltpu
from jax.sharding import PartitionSpec as P

TE = 8
GY = 8


SLOPE_COEF = 0.7978845608028654
CUBIC_COEF = 0.044715


def from_behind(block, axis, distance):
    devices = range(lax.axis_size(axis))
    route = [(i - distance, i) for i in devices if i - distance in devices]
    return lax.ppermute(block, axis, route)


def gelu_pair(values):
    inner_arg = SLOPE_COEF * (values + CUBIC_COEF * values * values * values)
    tangent = jnp.tanh(inner_arg)
    output = 0.5 * values * (1.0 + tangent)
    derivative = 0.5 * (1.0 + tangent) + 0.5 * values * (1.0 - tangent * tangent) * SLOPE_COEF * (
        1.0 + 3.0 * CUBIC_COEF * values * values
    )
    return (output, derivative)


def gelu_slope(values):
    inner_arg = SLOPE_COEF * (values + CUBIC_COEF * values * values * values)
    tangent = jnp.tanh(inner_arg)
    return 0.5 * (1.0 + tangent) + 0.5 * values * (1.0 - tangent * tangent) * SLOPE_COEF * (
        1.0 + 3.0 * CUBIC_COEF * values * values
    )


def place_matrix(slot_tile, slot_used, position_count):
    positions = jnp.arange(position_count, dtype=jnp.int32)
    matches = (slot_tile[0][None, :] == positions[:, None]) & (slot_used[0][None, :] == 1)
    return matches.astype(jnp.bfloat16)


def dense_column(tile_rows, placement):
    summed = jnp.einsum(
        "tj,jvc->tvc",
        placement,
        lax.all_gather(tile_rows, "depth", axis=0, tiled=True),
        preferred_element_type=jnp.float32,
    )
    return summed.astype(jnp.bfloat16).reshape(-1, TE, TE, summed.shape[-1])


def extend_sides(own_block, move_face, space_index):
    y_coord = space_index % GY
    below = move_face(own_block[:, :, -1:, :], 1) * (y_coord > 0).astype(own_block.dtype)
    above = move_face(own_block[:, :, :1, :], -1) * (y_coord < GY - 1).astype(own_block.dtype)
    widened = jnp.concatenate([below, own_block, above], axis=2)
    behind = move_face(widened[:, -1:, :, :], GY)
    ahead = move_face(widened[:, :1, :, :], -GY)
    return jnp.concatenate([behind, widened, ahead], axis=1)


def pad_depth(own_block):
    return jnp.pad(own_block, ((1, 1), (0, 0), (0, 0), (0, 0)))


def windows_at(padded, positions):

    def one_window(z_index):
        return lax.dynamic_slice_in_dim(padded, z_index * TE, TE + 2, 0)

    return jax.vmap(one_window)(positions)


def unfold(windows, flipped):
    pieces = []
    for kernel_tap in range(27):
        z_step, x_step, y_step = (kernel_tap // 9, kernel_tap // 3 % 3, kernel_tap % 3)
        if flipped:
            z_step, x_step, y_step = (2 - z_step, 2 - x_step, 2 - y_step)
        pieces.append(
            windows[:, z_step : z_step + TE, x_step : x_step + TE, y_step : y_step + TE, :]
        )
    stacked = jnp.concatenate(pieces, axis=-1)
    return stacked.reshape(-1, stacked.shape[-1])


def tile_sum(columns, delta):
    return lax.dot_general(
        columns, delta, (((0,), (0,)), ((), ())), preferred_element_type=jnp.float32
    )


def on_device_wide(features, cotangent, first_kernel, second_kernel, slot_tile, slot_used):
    depth_index = lax.axis_index("depth")
    space_index = lax.axis_index("space")
    slot_count = features.shape[1]
    voxels = features.shape[2]
    channels = features.shape[3]
    position_count = slot_tile.shape[1]
    placement = place_matrix(slot_tile, slot_used, position_count)
    own_first = depth_index * slot_count
    own_tiles = lax.dynamic_slice_in_dim(slot_tile[0], own_first, slot_count, 0)
    own_used = lax.dynamic_slice_in_dim(slot_used[0], own_first, slot_count, 0).astype(jnp.float32)
    feature_slots = features[0]
    upstream_slots = cotangent[0]

    def column_move(face, offset):
        return from_behind(face, "space", offset)

    def halo_of(tile_rows):
        column = dense_column(tile_rows.reshape(slot_count, voxels, channels), placement)
        return pad_depth(extend_sides(column, column_move, space_index))

    upstream = upstream_slots.reshape(-1, channels)
    source_column = halo_of(feature_slots)
    alive_rows = jnp.repeat(own_used, voxels)[:, None]
    forward_one = first_kernel.reshape(-1, channels)
    forward_two = second_kernel.reshape(-1, channels)
    backward_one = jnp.transpose(first_kernel, (0, 2, 1)).reshape(-1, channels)
    backward_two = jnp.transpose(second_kernel, (0, 2, 1)).reshape(-1, channels)
    source_cols = unfold(windows_at(source_column, own_tiles), False)
    pre_one = jnp.dot(source_cols, forward_one, preferred_element_type=jnp.float32)
    act_value, slope_one = gelu_pair(pre_one)
    act_one = (act_value * alive_rows).astype(jnp.bfloat16)
    act_cols = unfold(windows_at(halo_of(act_one), own_tiles), False)
    pre_two = jnp.dot(act_cols, forward_two, preferred_element_type=jnp.float32)
    slope_two = gelu_slope(pre_two)
    delta_two = (upstream.astype(jnp.float32) * slope_two * alive_rows).astype(jnp.bfloat16)
    second_grad = tile_sum(act_cols, delta_two).reshape(-1) * (1.0 / voxels)
    back_one = jnp.dot(
        unfold(windows_at(halo_of(delta_two), own_tiles), True),
        backward_two,
        preferred_element_type=jnp.float32,
    )
    delta_one = (back_one * slope_one * alive_rows).astype(jnp.bfloat16)
    first_grad = tile_sum(source_cols, delta_one).reshape(-1) * (1.0 / voxels)
    back_zero = jnp.dot(
        unfold(windows_at(halo_of(delta_one), own_tiles), True),
        backward_one,
        preferred_element_type=jnp.float32,
    )
    used_rows = jnp.repeat(own_used, voxels)[:, None]
    input_grad = (back_zero * used_rows).astype(jnp.bfloat16).reshape(features.shape)
    first_share, second_share = (
        lax.psum_scatter(first_grad, ("space", "depth"), scatter_dimension=0, tiled=True),
        lax.psum_scatter(second_grad, ("space", "depth"), scatter_dimension=0, tiled=True),
    )
    return (input_grad, first_share, second_share)


HALO = 4
NEAR = 4
INPUT_VMEM = 16 * 1024 * 1024
VMEM_LIMIT = 51 * 1024 * 1024
BF = jnp.bfloat16
F32 = jnp.float32


class Region:
    def __init__(self, even, odd, z_size, y_size):
        self.even, self.odd, self.z_size, self.y_size = even, odd, z_size, y_size

    def planes(self, first):
        return (self.odd, (first - 1) // 2) if first % 2 else (self.even, first // 2)

    def store_row(self, y_pair, y_parity, column):
        z_size, width, channels = column.shape
        place = lax.broadcasted_iota(jnp.int32, column.shape, 1)
        before = jnp.where(place == 0, 0.0, pltpu.roll(column, 1, 1))
        after = jnp.where(place == width - 1, 0.0, pltpu.roll(column, width - 1, 1))
        wide = jnp.concatenate([before, column, after], axis=-1)
        self.even[:, y_pair, y_parity] = wide.reshape(z_size // 2, 2 * width, 3 * channels).astype(BF)
        if self.odd is not None:
            inner = wide[1:-1].reshape(z_size // 2 - 1, 2 * width, 3 * channels)
            self.odd[:, y_pair, y_parity] = inner.astype(BF)

    def tile_rows(self, z_first, y_first, lanes, lane_first, edge):
        ref, q_first = self.planes(z_first)
        parts = []
        for y_at in range(y_first, y_first + edge):
            part = ref[q_first : q_first + edge // 2, y_at // 2, y_at % 2, :, lane_first : lane_first + lanes]
            parts.append(part.reshape(-1, lanes))
        return jnp.concatenate(parts, axis=0)


def region_shapes(z_size, y_size, width, channels, with_odd):
    tail = (y_size // 2, 2, 2 * width, 3 * channels)
    shapes = [pltpu.VMEM((z_size // 2,) + tail, BF)]
    if with_odd:
        shapes.append(pltpu.VMEM((z_size // 2 - 1,) + tail, BF))
    return shapes


def convolve_region(region, kernel, transposed, result):
    q_size, r_size = region.z_size // 2 - 1, region.y_size // 2 - 1
    channels = region.even.shape[-1] // 3
    pieces = []
    for block in range(9):
        z_tap, x_tap = block // 3, block % 3
        if transposed:
            z_tap, x_tap = 2 - z_tap, 2 - x_tap
        ref, q_first = region.planes(z_tap)
        for y_at in range(4):
            if transposed:
                y_at = 3 - y_at
            piece = ref[
                q_first : q_first + q_size,
                y_at // 2 : y_at // 2 + r_size,
                y_at % 2,
                :,
                x_tap * channels : (x_tap + 1) * channels,
            ]
            pieces.append(piece.reshape(-1, channels))
    left = jnp.concatenate(pieces, axis=1)
    blank = jnp.zeros((channels, channels), BF)
    blocks = []
    for block in range(9):
        taps = [kernel[block * 3 + y_tap] for y_tap in range(3)]
        for near, far in zip(*((taps + [blank], [blank] + taps) if not transposed else ([blank] + taps, taps + [blank]))):
            blocks.append(jnp.concatenate([near, far], axis=0 if transposed else 1))
    right = jnp.concatenate(blocks, axis=1 if transposed else 0)
    contract = (((1,), (1 if transposed else 0,)), ((), ()))
    product = lax.dot_general(left, right, contract, preferred_element_type=F32)
    result[0:q_size, 0:r_size] = product.reshape(q_size, r_size, product.shape[0] // (q_size * r_size), -1)


def place_slots(codes, blocks, offset, y_first, y_count, lifted, volume, mask, side):
    spare = volume.shape[0] - TE
    for at, (code, block) in enumerate(zip(codes, blocks)):
        z_first = jnp.where(code > 0, HALO + (code - 1) * TE, spare)
        rows = TE * TE * y_count
        lifted[at, 0:rows] = block[offset : offset + rows].astype(F32)
        for z_at in range(TE):
            for y_at in range(y_count):
                row = z_at * TE * y_count + y_at
                volume[z_first + z_at, y_first + y_at] = lifted[at, pl.ds(row, TE, stride=y_count)]
        if mask is not None:
            mask[side, pl.ds(z_first, TE)] = jnp.ones((TE,) + mask.shape[2:], F32)


def side_sizes():
    face, thin = HALO * TE * TE, 2 * TE * TE
    return face, thin, face + thin + 16


def sides_kernel(tile, used, odd, feature_rows, upstream_rows, to_pair, to_cross, own_table, lifted):
    channels = feature_rows.shape[1]
    face = side_sizes()[0]
    for rows, width, offset in ((feature_rows, HALO, 0), (upstream_rows, 2, face)):
        lifted[...] = rows[...].astype(F32).reshape(lifted.shape)
        count = TE * TE * width
        up_first = odd[0] * (TE - width)
        low_first = (1 - odd[0]) * (TE - width)
        to_cross[offset : offset + count] = lifted[:, pl.ds(up_first, width)].reshape(count, channels).astype(BF)
        to_pair[offset : offset + count] = lifted[:, pl.ds(low_first, width)].reshape(count, channels).astype(BF)
    place = lax.broadcasted_iota(jnp.int32, (16, channels), 0)
    table = jnp.zeros((16, channels), F32)
    for slot in range(tile.shape[1]):
        code = jnp.where(used[0, slot] == 1, tile[0, slot] + 1, 0)
        table = jnp.where(place == slot, code.astype(F32), table)
    for out in (to_pair, to_cross, own_table):
        out[out.shape[0] - 16 :] = table.astype(BF)


def sides_call(slot_tile, slot_used, odd, feature_rows, upstream_rows):
    voxels, channels = feature_rows.shape
    smem = pl.BlockSpec(memory_space=pltpu.SMEM)
    vmem = pl.BlockSpec(memory_space=pltpu.VMEM)
    side = jax.ShapeDtypeStruct((side_sizes()[2], channels), BF)
    return pl.pallas_call(
        sides_kernel,
        out_shape=[side, side, jax.ShapeDtypeStruct((16, channels), BF)],
        in_specs=[smem, smem, smem, vmem, vmem],
        out_specs=[vmem] * 3,
        scratch_shapes=[pltpu.VMEM((TE * TE, TE, channels), F32)],
        name="pack_sides",
    )(slot_tile, slot_used, odd, feature_rows, upstream_rows)


def table_at(block, first, slots):
    table = block[first : first + 16].astype(F32)
    place = lax.broadcasted_iota(jnp.int32, table.shape, 0)
    return [jnp.max(jnp.where(place == slot, table, 0.0)).astype(jnp.int32) for slot in slots]


def backward_kernel(block_count, tiles, depth_ref, odd_ref, *refs):
    own, up, pair, cross = (list(refs[at * block_count : (at + 1) * block_count]) for at in range(4))
    own_table, far_first, far_second, last, kept, given = refs[4 * block_count : 4 * block_count + 6]
    rest = list(refs[4 * block_count + 6 :])
    channels = own[0].shape[-1]

    def take():
        return rest.pop(0)

    volume, upstream, mask, lifted, result, grad_rows, first_kernel, second_kernel, sems = (
        take() for _ in range(9)
    )
    fetches = [
        pltpu.make_async_copy(far, near, sems.at[at])
        for at, (far, near) in enumerate(
            ((far_first, first_kernel), (far_second, second_kernel))
        )
    ]
    for fetch in fetches:
        fetch.start()
    regions = []
    for number in range(tiles):
        halo = HALO - number
        group = []
        for layer in range(4):
            size = TE + 2 * (halo - layer)
            even = take()
            odd = take() if size > TE else None
            group.append(Region(even, odd, size, size))
        regions.append(group)
    slopes = [take() for _ in range(tiles)]

    me = depth_ref[0]
    slots = [me ^ block for block in range(block_count)]
    voxels = TE * TE * TE
    volume[...] = jnp.zeros_like(volume)
    upstream[...] = jnp.zeros_like(upstream)
    mask[...] = jnp.zeros_like(mask)
    face, thin, _ = side_sizes()

    held = table_at(own_table, 0, slots)
    odd = odd_ref[0]
    for blocks, low in ((pair, odd), (cross, 1 - odd)):
        codes = table_at(blocks[0], face + thin, slots)
        side = 2 * (1 - low)
        y_feature = (1 - low) * (HALO + TE)
        y_upstream = (1 - low) * (TE + 2) + HALO - 2
        place_slots(codes, blocks, 0, y_feature, HALO, lifted, volume, mask, side)
        place_slots(codes, blocks, face, y_upstream, 2, lifted, upstream, None, side)
    place_slots(held, own, 0, HALO, TE, lifted, volume, mask, 1)
    place_slots(held, up, 0, HALO, TE, lifted, upstream, None, 1)

    starts = []
    alive = []
    for number in range(tiles):
        starts.append(jnp.maximum(held[2 * number] - 1, 0) * TE)
        alive.append((held[2 * number] > 0).astype(F32))

    for number in range(tiles):
        source = regions[number][0]
        z_first = starts[number] + number

        for pair in range(source.y_size // 2):
            for parity in range(2):
                source.store_row(pair, parity, volume[pl.ds(z_first, source.z_size), number + 2 * pair + parity])

    def finish_layer(number, layer, kind):
        region = regions[number][layer]
        inset = number + layer
        z_first = starts[number] + inset
        q_size = region.z_size // 2

        for pair in range(region.y_size // 2):
            for parity in range(2):
                y_at = inset + 2 * pair + parity
                side = (y_at >= HALO) + (y_at >= HALO + TE)
                window = pl.ds(z_first, region.z_size)
                keep = mask[side, window]
                value = result[0:q_size, pair, :, parity * channels : (parity + 1) * channels]
                value = value.reshape(keep.shape)
                if kind == "act":
                    out, slope = gelu_pair(value)
                    slopes[number][:, pair, parity] = slope * keep
                    out = out * keep
                elif kind == "delta_two":
                    out = upstream[window, y_at] * gelu_slope(value) * keep
                else:
                    out = value * slopes[number][2 : 2 + region.z_size, pair + 1, parity]
                region.store_row(pair, parity, out)

    def kernel_gradient(at, left, delta):
        flipped = []
        for number in range(tiles):
            region = regions[number][delta]
            inset = (region.z_size - TE) // 2
            rows = region.tile_rows(inset, inset, channels, channels, TE).astype(F32) * (alive[number] * (1.0 / voxels))
            flipped.append(rows.T.astype(BF))
        flipped = jnp.concatenate(flipped, axis=1)
        for z_tap in range(3):
            columns = []
            for number in range(tiles):
                region = regions[number][left]
                inset = (region.z_size - TE) // 2 - 1
                shifted = [
                    region.tile_rows(inset + z_tap, inset + y_tap, 3 * channels, 0, TE) for y_tap in range(3)
                ]
                columns.append(jnp.concatenate(shifted, axis=1))
            product = jnp.dot(flipped, jnp.concatenate(columns, axis=0), preferred_element_type=F32)
            for y_tap in range(3):
                for x_tap in range(3):
                    lane = (y_tap * 3 + x_tap) * channels
                    row = (z_tap * 9 + x_tap * 3 + y_tap) * channels
                    grad_rows[row : row + channels] = product[:, lane : lane + channels].T
        near_parts, far_parts, _, padded, _ = kept.shape
        share = 27 * channels // (near_parts * far_parts * block_count)
        for near_at in range(near_parts):
            for far_at in range(far_parts):
                column = (far_at * near_parts + near_at) * block_count
                for out, owner in ((kept, me), (given, me ^ 1)):
                    rows = grad_rows[pl.ds((column + owner) * share, padded)]
                    out[near_at, far_at, at] = rows.astype(BF)

    grad_rows[27 * channels :] = jnp.zeros_like(grad_rows[27 * channels :])
    fetches[0].wait()
    for number in range(tiles):
        convolve_region(regions[number][0], first_kernel, False, result)
        finish_layer(number, 1, "act")
    fetches[1].wait()
    for number in range(tiles):
        convolve_region(regions[number][1], second_kernel, False, result)
        finish_layer(number, 2, "delta_two")
    kernel_gradient(1, 1, 2)
    for number in range(tiles):
        convolve_region(regions[number][2], second_kernel, True, result)
        finish_layer(number, 3, "delta_one")
    last[...] = regions[0][3].even[:, :, :, :, channels : 2 * channels]
    kernel_gradient(0, 0, 3)


def input_kernel(depth_ref, own_table, last, far_first, input_grad, even, odd, lifted, result, first_kernel, sem):
    fetch = pltpu.make_async_copy(far_first, first_kernel, sem.at[0])
    fetch.start()
    (held,) = table_at(own_table, 0, [depth_ref[0]])
    alive = (held > 0).astype(F32)
    channels = input_grad.shape[-1]
    region = Region(even, odd, TE + 2, TE + 2)
    for pair in range(region.y_size // 2):
        for parity in range(2):
            column = last[:, pair, parity].astype(F32)
            region.store_row(pair, parity, column.reshape(region.z_size, TE, channels))
    fetch.wait()
    convolve_region(region, first_kernel, True, result)
    for pair in range(TE // 2):
        for parity in range(2):
            value = result[:, pair, :, parity * channels : (parity + 1) * channels] * alive
            value = value.reshape(TE, TE, channels)
            for z_at in range(TE):
                lifted[pl.ds(z_at * TE * TE + 2 * pair + parity, TE, stride=TE)] = value[z_at]
    input_grad[...] = lifted[0 : input_grad.shape[0]].astype(BF)


def input_call(depth_at, own_table, last, first_kernel):
    channels = first_kernel.shape[-1]
    voxels = TE * TE * TE
    vmem = pl.BlockSpec(memory_space=pltpu.VMEM)
    return pl.pallas_call(
        input_kernel,
        out_shape=jax.ShapeDtypeStruct((voxels, channels), BF),
        in_specs=[
            pl.BlockSpec(memory_space=pltpu.SMEM),
            vmem,
            vmem,
            pl.BlockSpec(memory_space=pltpu.HBM),
        ],
        out_specs=vmem,
        scratch_shapes=region_shapes(TE + 2, TE + 2, TE, channels, True)
        + [
            pltpu.VMEM((voxels + 16, channels), F32),
            pltpu.VMEM((TE // 2, TE // 2, 2 * TE, 2 * channels), F32),
            pltpu.VMEM((27, channels, channels), BF),
            pltpu.SemaphoreType.DMA((1,)),
        ],
        compiler_params=pltpu.CompilerParams(vmem_limit_bytes=INPUT_VMEM),
        cost_estimate=pl.CostEstimate(
            flops=2 * 36 * voxels * channels * channels,
            bytes_accessed=2 * 27 * channels * channels + 8 * voxels * channels,
            transcendentals=0,
        ),
        name="input_gradient",
    )(depth_at.reshape(1), own_table, last, first_kernel)


def backward_call(own, up, pair, cross, own_table, kernels, depth_at, odd, columns, positions, tiles):
    channels = own[0].shape[-1]
    voxels = TE * TE * TE
    planes = positions * TE + 2 * HALO + TE
    span = TE + 2 * HALO
    inner = span // 2 - 1
    padded = -(-(27 * channels // (columns * len(own))) // 16) * 16
    scratch = [
        pltpu.VMEM((planes, span, TE, channels), F32),
        pltpu.VMEM((planes, span, TE, channels), F32),
        pltpu.VMEM((3, planes, TE, channels), F32),
        pltpu.VMEM((len(own), voxels + 16, channels), F32),
        pltpu.VMEM((inner, inner, 2 * TE, 2 * channels), F32),
        pltpu.VMEM((27 * channels + 16, channels), F32),
        pltpu.VMEM((27, channels, channels), BF),
        pltpu.VMEM((27, channels, channels), BF),
        pltpu.SemaphoreType.DMA((2,)),
    ]
    for number in range(tiles):
        for layer in range(4):
            size = span - 2 * (number + layer)
            scratch += region_shapes(size, size, TE, channels, size > TE)
    for number in range(tiles):
        size = span - 2 * (number + 1)
        scratch.append(pltpu.VMEM((size, size // 2, 2, TE, channels), F32))
    vmem = pl.BlockSpec(memory_space=pltpu.VMEM)
    smem = pl.BlockSpec(memory_space=pltpu.SMEM)
    hbm = pl.BlockSpec(memory_space=pltpu.HBM)

    def body(*refs):
        backward_kernel(len(own), tiles, *refs)

    last = TE + 2
    share = jax.ShapeDtypeStruct((NEAR, columns // NEAR, 2, padded, channels), BF)
    return pl.pallas_call(
        body,
        out_shape=[
            jax.ShapeDtypeStruct((last // 2, last // 2, 2, 2 * TE, channels), BF),
            share,
            share,
        ],
        in_specs=[smem, smem] + [vmem] * (len(own) + len(up) + len(pair) + len(cross) + 1) + [hbm, hbm],
        out_specs=[vmem] * 3,
        scratch_shapes=scratch,
        compiler_params=pltpu.CompilerParams(vmem_limit_bytes=VMEM_LIMIT),
        cost_estimate=pl.CostEstimate(
            flops=40 * 27 * voxels * channels * channels,
            bytes_accessed=100 * voxels * channels,
            transcendentals=4 * voxels * channels,
        ),
        name="tile_backward",
    )(depth_at.reshape(1), odd, *own, *up, *pair, *cross, own_table, *kernels)


def on_device_line(features, cotangent, first_kernel, second_kernel, slot_tile, slot_used):
    channels = features.shape[3]
    depth_size, space_size = lax.axis_size("depth"), lax.axis_size("space")
    depth_at, space_at = lax.axis_index("depth"), lax.axis_index("space")

    def swap(block, axis, bits):
        return lax.ppermute(block, axis, [(i, i ^ bits) for i in range(lax.axis_size(axis))])

    own, up = features[0, 0], cotangent[0, 0]
    own_far, up_far = swap(own, "depth", 2), swap(up, "depth", 2)
    odd = (space_at % 2).reshape(1)
    to_pair, to_cross, own_table = sides_call(slot_tile, slot_used, odd, own, up)
    to_pair, own_far = lax.optimization_barrier((to_pair, own_far))
    crossing = [(i, i + 1 if i % 2 else i - 1) for i in range(1, space_size - 1)]
    cross, pair = lax.ppermute(to_cross, "space", crossing), swap(to_pair, "space", 1)
    cross_far, pair_far = swap(cross, "depth", 2), swap(pair, "depth", 2)

    def with_sibling(near, far):
        return [near, swap(near, "depth", 1), far, swap(far, "depth", 1)]

    last, kept, given = backward_call(
        with_sibling(own, own_far),
        with_sibling(up, up_far),
        with_sibling(pair, pair_far),
        with_sibling(cross, cross_far),
        own_table,
        (first_kernel, second_kernel),
        depth_at,
        odd,
        space_size,
        slot_tile.shape[1],
        2,
    )
    input_grad = input_call(depth_at, own_table, last, first_kernel)
    share = 27 * channels // (depth_size * space_size)

    def part(block, at):
        return lax.dynamic_index_in_dim(block, at, 0, keepdims=False)

    near_at, far_at = space_at % NEAR, space_at // NEAR
    column_sum = kept.astype(F32) + swap(given, "depth", 1).astype(F32)
    group = part(column_sum, near_at)
    for step in range(1, NEAR):
        group = group + swap(part(column_sum, near_at ^ step).astype(BF), "space", step).astype(F32)
    total = part(group, far_at)
    for step in range(1, space_size // NEAR):
        total = total + swap(part(group, far_at ^ step).astype(BF), "space", NEAR * step).astype(F32)
    first_share, second_share = (total[at, :share].reshape(-1) for at in range(2))
    return (input_grad.reshape(features.shape), first_share, second_share)


def solution(mesh):
    line = mesh.shape["space"] == GY and mesh.shape["depth"] == 4
    run = on_device_line if line else on_device_wide
    return jax.shard_map(
        run,
        mesh=mesh,
        in_specs=(
            P("space", "depth", None, None),
            P("space", "depth", None, None),
            P(),
            P(),
            P("space", None),
            P("space", None),
        ),
        out_specs=(P("space", "depth", None, None), P(("space", "depth")), P(("space", "depth"))),
        check_vma=False,
    )
```
